128 devices in a mesh: dp: 2 (over core), blk: 8 (over y_hi, x), head: 8 (over z, y_lo).
Axes of the slice: x: 4, y: 4 (y_hi: 2, y_lo: 2; y = y_hi * 2 + y_lo), z: 4, core: 2. Of those that a mesh axis runs over, the one named last changes fastest.
Arguments:
- query_input: bfloat16 [2, 12288, 3072], P('dp', ('blk', 'head')), may hold values from -6 to 6
- key_input: bfloat16 [2, 12288, 3072], P('dp', ('blk', 'head')), may hold values from -6 to 6
- value_input: bfloat16 [2, 12288, 3072], P('dp', ('blk', 'head')), may hold values from -6 to 6
- output_grad: bfloat16 [2, 12288, 3072], P('dp', ('blk', 'head')), may hold values from -16 to 16
- query_gain: float32 [3072], replicated, may hold values from 0.5 to 1.5
- key_gain: float32 [3072], replicated, may hold values from 0.5 to 1.5
- tile_lists: int32 [2, 64, 12], P('dp'), may hold values from 0 to 63, as said below
- tile_counts: int32 [2, 64], P('dp'), may hold values from 2 to 12, as said below
Outputs:
- attention: bfloat16 [2, 12288, 3072], P('dp', ('blk', 'head'))
- query_grad: bfloat16 [2, 12288, 3072], P('dp', ('blk', 'head'))
- key_grad: bfloat16 [2, 12288, 3072], P('dp', ('blk', 'head'))
- value_grad: bfloat16 [2, 12288, 3072], P('dp', ('blk', 'head'))
- query_gain_grad: float32 [3072], P(('dp', 'blk', 'head'))
- key_gain_grad: float32 [3072], P(('dp', 'blk', 'head'))
The draws below stay inside these ranges and needn't reach their ends.
Inputs may be any that keep to these rules, and one draw needn't show every extreme that they name: `tile_lists`: tile t lies in slab t // 8, tile row (t // 4) % 2, tile column t % 4. The first tile_counts[t] entries of row t are distinct tiles, the first being t itself, each at most one slab, one tile row and one tile column away from t; the remaining entries equal t. `tile_counts`: 12 is reached in every sequence.
All inputs are finite; a program needn't handle non-finite values.
Results may differ from the reference program's by a relative error of at most 0.038.
Values may be sent and summed in bfloat16 or wider, within the bound.
A program may use at most 192 MiB of HBM per device.

```python
import jax
import jax.numpy as jnp
from jax import lax

HEADS = 24
HS = 128
TILE = 192
TH = 2
TW = 4
KMAX = 12
NT_SLAB = 8
SEQ = 12288
NTILES = 64
F = 3072
N_DP = 2


def draw_query_input(key, part):
    key = jax.random.fold_in(key, 1)
    base_draw = jax.random.normal(key, (N_DP, SEQ, HEADS * HS), jnp.float32)
    mixed = base_draw
    return jnp.clip(mixed, -6.0, 6.0).astype(jnp.bfloat16)


def draw_key_input(key, part):
    key = jax.random.fold_in(key, 4)
    base_draw = jax.random.normal(key, (N_DP, SEQ, HEADS * HS), jnp.float32)
    mixed = base_draw
    return jnp.clip(mixed, -6.0, 6.0).astype(jnp.bfloat16)


def tile_plan(key):
    tile_index = jnp.arange(NTILES)
    slab_of = tile_index // NT_SLAB
    tile_row = tile_index % NT_SLAB // TW
    column = tile_index % TW
    offset = jnp.arange(27)
    step_slab = offset // 9 - 1
    step_row = offset // 3 % 3 - 1
    step_col = offset % 3 - 1
    near_slab = slab_of[:, None] + step_slab[None, :]
    near_row = tile_row[:, None] + step_row[None, :]
    near_col = column[:, None] + step_col[None, :]
    inside_grid = (near_slab >= 0) & (near_slab < NTILES // NT_SLAB) & (near_row >= 0) & (near_row < TH) & (near_col >= 0) & (near_col < TW)
    target = near_slab * NT_SLAB + near_row * TW + near_col
    noise_bits = jax.random.randint(jax.random.fold_in(key, 11), (N_DP, NTILES, 27), 0, 1 << 20)
    scores = jnp.where(offset[None, None, :] == 13, 1 << 26, noise_bits * 32 + offset[None, None, :])
    scores = jnp.where(inside_grid[None], scores, -1)
    ranked = lax.top_k(scores, KMAX)[1]
    named_tiles = jnp.take_along_axis(jnp.broadcast_to(target[None], (N_DP, NTILES, 27)), ranked, axis=2)
    available = jnp.sum(inside_grid.astype(jnp.int32), axis=1)
    counts = jax.random.randint(jax.random.fold_in(key, 12), (N_DP, NTILES), 2, KMAX + 1)
    counts = jnp.minimum(counts, available[None, :])
    forced = jax.random.randint(jax.random.fold_in(key, 13), (N_DP, NTILES // NT_SLAB), 0, NT_SLAB)
    chosen = (tile_index % NT_SLAB)[None, :] == forced[:, slab_of]
    counts = jnp.where(chosen, jnp.minimum(available, KMAX)[None, :], counts)
    tile_list = jnp.where(jnp.arange(KMAX)[None, None, :] < counts[:, :, None], named_tiles, tile_index[None, :, None])
    return (tile_list.astype(jnp.int32), counts.astype(jnp.int32))


def draw_tile_lists(key, part):
    plan_out = tile_plan(key)
    return plan_out[0]


def draw_tile_counts(key, part):
    plan_out = tile_plan(key)
    return plan_out[1]


def strengthened(drawn, key, source, target, blocks, factor):
    def block_of(axis_at):
        return (jnp.arange(drawn.shape[axis_at]) // (drawn.shape[axis_at] // blocks)).reshape((-1,) + (1,) * (drawn.ndim - 1 - axis_at))

    one_side = jax.random.permutation(key, blocks)[block_of(target)]
    other_side = (block_of(target) + blocks // 2) % blocks
    return jnp.where((block_of(source) == one_side) | (block_of(source) == other_side), factor * drawn, drawn)


def steps_of(key, extent, shards, low, top_value):
    factor_of, own = 1.0, jax.random.fold_in(key, 6)
    for dim, parts in shards:
        heights = jnp.exp(jax.random.uniform(jax.random.fold_in(own, dim), (parts,), jnp.float32, low / len(shards), top_value / len(shards)))
        factor_of = factor_of * jnp.repeat(heights, extent[dim] // parts).reshape([-1 if axis == dim else 1 for axis in range(len(extent))])
    return factor_of


def scatter_about(key, shape, scale, bound, pieces=(), held_as=jnp.bfloat16):
    entries = jax.random.normal(key, shape, jnp.float32) * scale
    if len(pieces) > 0:
        entries = steps_of(key, shape, pieces, -0.22, 0.18) * entries
    return jnp.clip(entries, min=-bound, max=bound).astype(held_as)


def gaussian_with(own_key, extent, scale, reach, shards, heavy, kind=jnp.bfloat16):
    values = scale * jax.random.normal(own_key, extent, jnp.float32)
    if shards:
        values = values * steps_of(own_key, extent, shards, -0.22, 0.18)
    return jnp.clip(strengthened(values, jax.random.fold_in(own_key, 3), *heavy), -reach, reach).astype(kind)


def setup_inputs(seed: int = 0) -> dict:
    splits = jax.random.split(jax.random.key(seed), 9)
    query_input = draw_query_input(jax.random.fold_in(splits[8], 71), 0)
    key_input = draw_key_input(jax.random.fold_in(splits[8], 71), 0)
    value_input = scatter_about(splits[2], (N_DP, SEQ, F), 1.0, 6.0, ((0, 2), (1, 64)))
    output_grad = gaussian_with(splits[3], (N_DP, SEQ, F), 1.0, 16.0, ((0, 2), (1, 64)), (1, 2, 64, 4.0))
    query_gain = jnp.clip(1.0 + 0.1 * jax.random.normal(splits[4], (F,), jnp.float32), 0.5, 1.5)
    key_gain = jnp.clip(1.0 + 0.1 * jax.random.normal(splits[5], (F,), jnp.float32), 0.5, 1.5)
    tile_lists = draw_tile_lists(jax.random.fold_in(splits[8], 71), 0)
    tile_counts = draw_tile_counts(jax.random.fold_in(splits[8], 71), 0)
    return {"query_input": query_input, "key_input": key_input, "value_input": value_input, "output_grad": output_grad, "query_gain": query_gain, "key_gain": key_gain, "tile_lists": tile_lists, "tile_counts": tile_counts}


EPSILON = 1e-06

def normalize(raw_input, gain_vec):
    widened = raw_input.astype(jnp.float32)
    factor = lax.rsqrt(lax.optimization_barrier(jnp.mean(widened * widened, axis=-1, keepdims=True)) + EPSILON)
    normed = widened * factor
    return (normed, factor, (normed * gain_vec).astype(jnp.bfloat16))

def norm_back(grad_input, normed, factor, gain_vec):
    grad_wide = grad_input.astype(jnp.float32)
    scaled = grad_wide * gain_vec
    inner = lax.optimization_barrier(jnp.mean(scaled * normed, axis=-1, keepdims=True))
    return ((factor * (scaled - normed * inner)).astype(jnp.bfloat16), lax.optimization_barrier(jnp.sum(grad_wide * normed, axis=0)))

def tile_step(query_tile, grad_tile, key_tile, value_tile, live_count):
    score_scale = HS ** (-0.5)
    query_wide = query_tile.astype(jnp.float32)
    key_wide = key_tile.astype(jnp.float32)
    value_wide = value_tile.astype(jnp.float32)
    grad_wide = grad_tile.astype(jnp.float32)
    scores = jnp.einsum('qhd,jkhd->hqjk', query_wide, key_wide) * score_scale
    live_slots = (jnp.arange(KMAX, dtype=jnp.int32) < live_count)[None, None, :, None]
    scores = jnp.where(live_slots, scores, -jnp.inf)
    row_max = lax.optimization_barrier(jnp.max(scores, axis=(2, 3), keepdims=True))
    exponent = jnp.exp(scores - row_max)
    weights = (exponent / lax.optimization_barrier(jnp.sum(exponent, axis=(2, 3), keepdims=True))).astype(jnp.bfloat16)
    weights_wide = lax.optimization_barrier(weights).astype(jnp.float32)
    output = jnp.einsum('hqjk,jkhd->qhd', weights_wide, value_wide).astype(jnp.bfloat16)
    grad_probs = jnp.einsum('qhd,jkhd->hqjk', grad_wide, value_wide)
    row_delta = lax.optimization_barrier(jnp.sum(weights_wide * grad_probs, axis=(2, 3), keepdims=True))
    grad_scores = (weights_wide * (grad_probs - row_delta)).astype(jnp.bfloat16)
    grad_scores = lax.optimization_barrier(grad_scores).astype(jnp.float32)
    query_att = (score_scale * jnp.einsum('hqjk,jkhd->qhd', grad_scores, key_wide)).astype(jnp.bfloat16)
    key_part = score_scale * jnp.einsum('hqjk,qhd->jkhd', grad_scores, query_wide)
    value_part = jnp.einsum('hqjk,qhd->jkhd', weights_wide, grad_wide)
    return (output, query_att, key_part, value_part)

def reference(query_input, key_input, value_input, output_grad, query_gain, key_gain, tile_lists, tile_counts):
    attention_all = []
    query_all = []
    key_all = []
    value_all = []
    query_gain_grad = jnp.zeros((F,), jnp.float32)
    key_gain_grad = jnp.zeros((F,), jnp.float32)
    for member in range(N_DP):
        q_hat, q_factor, queries = normalize(query_input[member], query_gain)
        k_hat, k_factor, keys = normalize(key_input[member], key_gain)
        query_grid = queries.reshape(NTILES, TILE, HEADS, HS)
        key_grid = keys.reshape(NTILES, TILE, HEADS, HS)
        value_grid = value_input[member].reshape(NTILES, TILE, HEADS, HS)
        grad_grid = output_grad[member].reshape(NTILES, TILE, HEADS, HS)

        def visit(totals, tile_index):
            chosen = tile_lists[member, tile_index]
            tile_out, tile_qgrad, key_part, value_part = tile_step(query_grid[tile_index], grad_grid[tile_index], key_grid[chosen], value_grid[chosen], tile_counts[member, tile_index])
            totals = (totals[0].at[chosen].add(key_part), totals[1].at[chosen].add(value_part))
            return (totals, (tile_out, tile_qgrad))
        zero_grid = jnp.zeros((NTILES, TILE, HEADS, HS), jnp.float32)
        sums_out, tile_outs = lax.scan(visit, (zero_grid, zero_grid), jnp.arange(NTILES, dtype=jnp.int32))
        attention_all.append(tile_outs[0].reshape(SEQ, F))
        query_att = tile_outs[1].reshape(SEQ, F)
        key_att = sums_out[0].reshape(SEQ, F).astype(jnp.bfloat16)
        value_all.append(sums_out[1].reshape(SEQ, F).astype(jnp.bfloat16))
        query_back, query_gain_part = norm_back(query_att, q_hat, q_factor, query_gain)
        key_back, key_gain_part = norm_back(key_att, k_hat, k_factor, key_gain)
        query_all.append(query_back)
        key_all.append(key_back)
        query_gain_grad = query_gain_grad + query_gain_part
        key_gain_grad = key_gain_grad + key_gain_part
    return (jnp.stack(attention_all), jnp.stack(query_all), jnp.stack(key_all), jnp.stack(value_all), query_gain_grad, key_gain_grad)
```

```python
import functools

import jax
import jax.numpy as jnp
from jax import lax
from jax.experimental import pallas as pl
from jax.experimental.pallas import tpu as pltpu
from jax.sharding import PartitionSpec as P

HS = 128
TILE = 192
KMAX = 12
HEADS = 24
HPD = 3
COLS = 4
NB = 8
NH = 8
F = HEADS * HS
CH = 2 * TILE
ROWS = 16
EPSILON = 1e-06
SCALE = HS**-0.5
SCALE2 = SCALE * 1.4426950408889634
FAR = -1e30
f32 = jnp.float32
bf16 = jnp.bfloat16


def nn(a, b):
    return lax.dot_general(a, b, (((1,), (0,)), ((), ())), preferred_element_type=f32)


def nt(a, b):
    return lax.dot_general(a, b, (((1,), (1,)), ((), ())), preferred_element_type=f32)


def wait_for(ref, sem):
    pltpu.make_async_copy(ref, ref, sem).wait()


def kernel(
    q_in,
    k_in,
    v_in,
    g_in,
    q_gain,
    k_gain,
    bias,
    att_out,
    qgrad_out,
    kgrad_out,
    vgrad_out,
    gain_out,
    q_stage,
    k_stage,
    q_fac,
    k_fac,
    qbuf,
    gbuf,
    kbuf,
    vbuf,
    kt_buf,
    vt_buf,
    s_buf,
    p_buf,
    acc_k,
    acc_v,
    own_acc,
    edge_send,
    edge_recv,
    own_send,
    o_send,
    dq_send,
    dq_recv,
    dk_recv,
    gain_acc,
    in_send,
    in_recv,
    halo_send,
    halo_recv,
    edge_ssem,
    edge_rsem,
    back_send,
    back_recv,
):
    b = lax.axis_index("blk")
    g = lax.axis_index("head")
    has_low = b > 0
    has_high = b < NB - 1
    my_row = g // COLS
    my_col = g % COLS
    my_rows = pl.ds(pl.multiple_of(my_row * TILE, TILE), TILE)

    barrier = pltpu.get_barrier_semaphore()

    def greet(i, carry):
        pl.semaphore_signal(barrier, inc=1, device_id={"head": (g + i) % NH})
        return carry

    lax.fori_loop(1, NH, greet, 0)

    @pl.when(has_low)
    def _():
        pl.semaphore_signal(barrier, inc=1, device_id={"blk": b - 1})

    @pl.when(has_high)
    def _():
        pl.semaphore_signal(barrier, inc=1, device_id={"blk": b + 1})

    def clear_side(slab, side):
        zeros = jnp.zeros((CH, HS), bf16)

        def one(e, carry):
            h, c = e // COLS, e % COLS
            kbuf[h, c, slab] = zeros
            vbuf[h, c, slab] = zeros
            edge_recv[e, side, 0] = zeros
            edge_recv[e, side, 1] = zeros
            return carry

        lax.fori_loop(0, HPD * COLS, one, 0)

    @pl.when(jnp.logical_not(has_low))
    def _():
        clear_side(0, 0)

    @pl.when(jnp.logical_not(has_high))
    def _():
        clear_side(2, 1)

    def normalize(x_in, gain, stage, fac):
        def block(i, carry):
            rows = pl.ds(pl.multiple_of(i * ROWS, ROWS), ROWS)
            total = jnp.zeros((ROWS, HS), f32)
            for h in range(HEADS):
                x = x_in[rows, h * HS : (h + 1) * HS].astype(f32)
                total = total + x * x
            mean = jnp.sum(total, axis=1, keepdims=True) * (1.0 / F)
            factor = jnp.broadcast_to(lax.rsqrt(mean + EPSILON), (ROWS, HS))
            fac[rows, :] = factor
            for h in range(HEADS):
                x = x_in[rows, h * HS : (h + 1) * HS].astype(f32)
                stage[h, rows, :] = (x * factor * gain[:, h * HS : (h + 1) * HS]).astype(bf16)
            return carry

        lax.fori_loop(0, TILE // ROWS, block, 0)

    def send_in(h, which, src_of, dst):
        here = pltpu.make_async_copy(src_of(g * HPD + h), dst, in_recv.at[which, h])
        here.start()

        def one(i, carry):
            to = (g + i) % NH
            pltpu.make_async_remote_copy(
                src_ref=src_of(to * HPD + h),
                dst_ref=dst,
                send_sem=in_send.at[which],
                recv_sem=in_recv.at[which, h],
                device_id={"head": to},
            ).start()
            return carry

        lax.fori_loop(1, NH, one, 0)

    def columns(h):
        return pl.ds(pl.multiple_of(h * HS, HS), HS)

    def send_k(h):
        send_in(h, 0, lambda n: k_stage.at[n], kbuf.at[h, my_col, 1, my_rows])

    def send_v(h):
        send_in(h, 1, lambda n: v_in.at[:, columns(n)], vbuf.at[h, my_col, 1, my_rows])

    def send_q(h):
        send_in(h, 2, lambda n: q_stage.at[n], qbuf.at[h, my_col, my_rows])

    def send_g(h):
        send_in(h, 3, lambda n: g_in.at[:, columns(n)], gbuf.at[h, my_col, my_rows])

    normalize(k_in, k_gain, k_stage, k_fac)
    pl.semaphore_wait(
        barrier, NH - 1 + has_low.astype(jnp.int32) + has_high.astype(jnp.int32)
    )
    send_v(0)
    send_k(0)
    normalize(q_in, q_gain, q_stage, q_fac)
    send_q(0)
    send_g(0)

    def rest(h, carry):
        send_k(h)
        send_v(h)
        send_q(h)
        send_g(h)
        return carry

    lax.fori_loop(1, HPD, rest, 0)

    def halo_copy(h, which, up):
        buf = (kbuf, vbuf)[which]
        side = 1 - up
        side = 0 if up else 1
        return pltpu.make_async_remote_copy(
            src_ref=buf.at[h, :, 1],
            dst_ref=buf.at[h, :, 0 if up else 2],
            send_sem=halo_send.at[h, which, side],
            recv_sem=halo_recv.at[h, which, side],
            device_id={"blk": b + 1 if up else b - 1},
        )

    def forward(h):
        wait_for(kbuf.at[h, :, 1], in_recv.at[0, h])
        wait_for(vbuf.at[h, :, 1], in_recv.at[1, h])
        for which in range(2):

            @pl.when(has_high)
            def _():
                halo_copy(h, which, True).start()

            @pl.when(has_low)
            def _():
                halo_copy(h, which, False).start()

    def await_halo(h):
        for which in range(2):

            @pl.when(has_low)
            def _():
                halo_copy(h, which, True).wait_recv()

            @pl.when(has_high)
            def _():
                halo_copy(h, which, False).wait_recv()

    def send_back(which, src, dst, t):
        @pl.when(t == g)
        def _():
            pltpu.make_async_copy(src, dst, back_recv.at[which]).start()

        @pl.when(t != g)
        def _():
            pltpu.make_async_remote_copy(
                src_ref=src,
                dst_ref=dst,
                send_sem=back_send.at[which],
                recv_sem=back_recv.at[which],
                device_id={"head": t},
            ).start()

    def attend(h, c):
        low = jnp.maximum(c - 1, 0) * 3
        high = jnp.minimum(c + 2, COLS) * 3
        q = qbuf[h, c]

        def first(j, top):
            s = nt(kbuf[h, j // 3, j % 3], q)
            s_buf[j - low] = s
            away = bias[c * 12 + j]
            top = jnp.maximum(top, jnp.max(s[:TILE], axis=0, keepdims=True) + away[0:1])
            return jnp.maximum(top, jnp.max(s[TILE:], axis=0, keepdims=True) + away[1:2])

        top = lax.fori_loop(low, high, first, jnp.full((1, CH), 2 * FAR, f32)) * SCALE2

        def second(j, carry):
            total, out = carry
            away = bias[c * 12 + j]
            s = s_buf[j - low]
            e0 = jnp.exp2(s[:TILE] * SCALE2 - (top - away[0:1]))
            e1 = jnp.exp2(s[TILE:] * SCALE2 - (top - away[1:2]))
            total = total + jnp.sum(e0, axis=0, keepdims=True) + jnp.sum(e1, axis=0, keepdims=True)
            e = jnp.concatenate([e0.astype(bf16), e1.astype(bf16)], axis=0)
            p_buf[j - low] = e
            return total, out + nn(vt_buf[j], e)

        total, out = lax.fori_loop(
            low, high, second, (jnp.zeros((1, CH), f32), jnp.zeros((HS, CH), f32))
        )
        inverse = 1.0 / total
        out = out * inverse
        o_send[h, c] = out.T.astype(bf16)
        grad = gbuf[h, c].astype(f32).T
        delta = jnp.sum(out * grad, axis=0, keepdims=True) * inverse
        grad = grad * inverse
        grad_t = grad.astype(bf16)
        grad_s = grad.T.astype(bf16)

        def third(j, dq):
            e = p_buf[j - low]
            dp = nn(vbuf[h, j // 3, j % 3], grad_t)
            ds = (e.astype(f32) * (dp - delta)).astype(bf16)
            acc_v[j] += nn(e, grad_s)
            acc_k[j] += nn(ds, q)
            return dq + nn(kt_buf[j], ds)

        dq = lax.fori_loop(low, high, third, jnp.zeros((HS, CH), f32))
        dq_send[h, c] = (dq * SCALE).T.astype(bf16)
        for r in range(2):
            rows = pl.ds(r * TILE, TILE)
            t = r * COLS + c
            send_back(0, o_send.at[h, c, rows], att_out.at[:, columns(g * HPD + h)], t)
            send_back(1, dq_send.at[h, c, rows], dq_recv.at[g * HPD + h], t)

    def edge_copy(e, up):
        return pltpu.make_async_remote_copy(
            src_ref=edge_send.at[e, 1 if up else 0],
            dst_ref=edge_recv.at[e, 0 if up else 1],
            send_sem=edge_ssem.at[e, 1 if up else 0],
            recv_sem=edge_rsem.at[e, 0 if up else 1],
            device_id={"blk": b + 1 if up else b - 1},
        )

    def finish(h, c):
        e = h * COLS + c
        for side, slab in ((0, 0), (1, 2)):
            edge_send[e, side, 0] = (acc_k[c * 3 + slab] * SCALE).astype(bf16)
            edge_send[e, side, 1] = acc_v[c * 3 + slab].astype(bf16)
        own_acc[e, 0] = acc_k[c * 3 + 1] * SCALE
        own_acc[e, 1] = acc_v[c * 3 + 1]

        @pl.when(has_high)
        def _():
            edge_copy(e, True).start()

        @pl.when(has_low)
        def _():
            edge_copy(e, False).start()

    def settle(h, c):
        e = h * COLS + c

        @pl.when(has_low)
        def _():
            edge_copy(e, True).wait_recv()

        @pl.when(has_high)
        def _():
            edge_copy(e, False).wait_recv()

        for a in range(2):
            own_send[e, a] = (
                own_acc[e, a] + edge_recv[e, 0, a].astype(f32) + edge_recv[e, 1, a].astype(f32)
            ).astype(bf16)
        for r in range(2):
            rows = pl.ds(r * TILE, TILE)
            t = r * COLS + c
            send_back(2, own_send.at[e, 0, rows], dk_recv.at[g * HPD + h], t)
            send_back(3, own_send.at[e, 1, rows], vgrad_out.at[:, columns(g * HPD + h)], t)

    def start_head(h):
        await_halo(h)
        wait_for(qbuf.at[h], in_recv.at[2, h])
        wait_for(gbuf.at[h], in_recv.at[3, h])

        def turn(j, carry):
            kt_buf[j] = kbuf[h, j // 3, j % 3].T
            vt_buf[j] = vbuf[h, j // 3, j % 3].T
            acc_k[j] = jnp.zeros((CH, HS), f32)
            acc_v[j] = jnp.zeros((CH, HS), f32)
            return carry

        lax.fori_loop(0, 3 * COLS, turn, 0)

    forward(0)

    def step(s, carry):
        h, c = s // COLS, s % COLS

        @pl.when(c == 0)
        def _():
            start_head(h)

        @pl.when((c == 1) & (h < HPD - 1))
        def _():
            forward(h + 1)

        attend(h, c)

        @pl.when(c > 0)
        def _():
            finish(h, c - 1)

        @pl.when(c == COLS - 1)
        def _():
            finish(h, COLS - 1)

        @pl.when(h > 0)
        def _():
            settle(h - 1, c)

        return carry

    lax.fori_loop(0, HPD * COLS, step, 0)

    def last(c, carry):
        settle(HPD - 1, c)
        return carry

    lax.fori_loop(0, COLS, last, 0)

    def norm_back(index, x_in, gain, fac, d_recv, grad_out):
        gain_acc[...] = jnp.zeros((8, F), f32)

        def block(i, carry):
            rows = pl.ds(pl.multiple_of(i * ROWS, ROWS), ROWS)
            factor = fac[rows, :]
            total = jnp.zeros((ROWS, HS), f32)
            for h in range(HEADS):
                lanes = slice(h * HS, (h + 1) * HS)
                hat = x_in[rows, lanes].astype(f32) * factor
                product = d_recv[h, rows, :].astype(f32) * hat
                total = total + product * gain[:, lanes]
                gain_acc[:, lanes] += product[:8] + product[8:]
            inner = jnp.sum(total, axis=1, keepdims=True) * (1.0 / F)
            for h in range(HEADS):
                lanes = slice(h * HS, (h + 1) * HS)
                hat = x_in[rows, lanes].astype(f32) * factor
                scaled = d_recv[h, rows, :].astype(f32) * gain[:, lanes]
                grad_out[rows, lanes] = (factor * (scaled - hat * inner)).astype(bf16)
            return carry

        lax.fori_loop(0, TILE // ROWS, block, 0)
        gain_out[index : index + 1, :] = jnp.sum(gain_acc[...], axis=0, keepdims=True)

    wait_for(dq_recv, back_recv.at[1])
    norm_back(0, q_in, q_gain, q_fac, dq_recv, qgrad_out)
    wait_for(dk_recv, back_recv.at[2])
    norm_back(1, k_in, k_gain, k_fac, dk_recv, kgrad_out)
    wait_for(att_out, back_recv.at[0])
    wait_for(vgrad_out, back_recv.at[3])

    sent = dq_recv.at[0 : HEADS - HPD]
    for which in range(4):
        wait_for(sent, in_send.at[which])
        wait_for(sent, back_send.at[which])

    def drain(h, carry):
        for which in range(2):

            @pl.when(has_high)
            def _():
                halo_copy(h, which, True).wait_send()

            @pl.when(has_low)
            def _():
                halo_copy(h, which, False).wait_send()

        return carry

    lax.fori_loop(0, HPD, drain, 0)

    def drain_edges(e, carry):
        @pl.when(has_high)
        def _():
            edge_copy(e, True).wait_send()

        @pl.when(has_low)
        def _():
            edge_copy(e, False).wait_send()

        return carry

    lax.fori_loop(0, HPD * COLS, drain_edges, 0)


def bias_table(tile_lists, tile_counts):
    per_slab = 2 * COLS
    slab = lax.axis_index("blk")
    lists = lax.dynamic_slice_in_dim(tile_lists, slab * per_slab, per_slab, 0)
    counts = lax.dynamic_slice_in_dim(tile_counts, slab * per_slab, per_slab, 0)
    relative = lists - (slab - 1) * per_slab
    live = jnp.arange(KMAX)[None, :] < counts[:, None]
    named = (relative[:, :, None] == jnp.arange(3 * per_slab)[None, None, :]) & live[:, :, None]
    table = jnp.where(jnp.any(named, axis=1), 0.0, FAR).astype(f32)
    table = table.reshape(2, COLS, 3, 2, COLS).transpose(1, 4, 2, 3, 0)
    return jnp.repeat(table.reshape(COLS * 12, 2, 2), TILE, axis=2)


def shards(
    query_input, key_input, value_input, output_grad, query_gain, key_gain, tile_lists, tile_counts
):
    table = bias_table(tile_lists[0], tile_counts[0])
    vmem = pl.BlockSpec(memory_space=pltpu.VMEM)
    anywhere = pl.BlockSpec(memory_space=pl.ANY)
    token = jax.ShapeDtypeStruct((TILE, F), bf16)
    n = HPD * COLS
    attention, query_grad, key_grad, value_grad, gains = pl.pallas_call(
        kernel,
        name="tiles",
        out_shape=(token, token, token, token, jax.ShapeDtypeStruct((2, F), f32)),
        in_specs=[vmem] * 7,
        out_specs=(anywhere, vmem, vmem, anywhere, vmem),
        scratch_shapes=[
            pltpu.VMEM((HEADS, TILE, HS), bf16),
            pltpu.VMEM((HEADS, TILE, HS), bf16),
            pltpu.VMEM((TILE, HS), f32),
            pltpu.VMEM((TILE, HS), f32),
            pltpu.VMEM((HPD, COLS, CH, HS), bf16),
            pltpu.VMEM((HPD, COLS, CH, HS), bf16),
            pltpu.VMEM((HPD, COLS, 3, CH, HS), bf16),
            pltpu.VMEM((HPD, COLS, 3, CH, HS), bf16),
            pltpu.VMEM((12, HS, CH), bf16),
            pltpu.VMEM((12, HS, CH), bf16),
            pltpu.VMEM((9, CH, CH), f32),
            pltpu.VMEM((9, CH, CH), bf16),
            pltpu.VMEM((12, CH, HS), f32),
            pltpu.VMEM((12, CH, HS), f32),
            pltpu.VMEM((n, 2, CH, HS), f32),
            pltpu.VMEM((n, 2, 2, CH, HS), bf16),
            pltpu.VMEM((n, 2, 2, CH, HS), bf16),
            pltpu.VMEM((n, 2, CH, HS), bf16),
            pltpu.VMEM((HPD, COLS, CH, HS), bf16),
            pltpu.VMEM((HPD, COLS, CH, HS), bf16),
            pltpu.VMEM((HEADS, TILE, HS), bf16),
            pltpu.VMEM((HEADS, TILE, HS), bf16),
            pltpu.VMEM((8, F), f32),
            pltpu.SemaphoreType.DMA((4,)),
            pltpu.SemaphoreType.DMA((4, HPD)),
            pltpu.SemaphoreType.DMA((HPD, 2, 2)),
            pltpu.SemaphoreType.DMA((HPD, 2, 2)),
            pltpu.SemaphoreType.DMA((n, 2)),
            pltpu.SemaphoreType.DMA((n, 2)),
            pltpu.SemaphoreType.DMA((4,)),
            pltpu.SemaphoreType.DMA((4,)),
        ],
        compiler_params=pltpu.CompilerParams(
            collective_id=0, has_side_effects=True, vmem_limit_bytes=62 * 1024 * 1024
        ),
    )(
        query_input[0],
        key_input[0],
        value_input[0],
        output_grad[0],
        query_gain[None],
        key_gain[None],
        table,
    )
    gain_grads = lax.psum_scatter(gains, ("dp", "blk", "head"), scatter_dimension=1, tiled=True)
    return (
        attention[None],
        query_grad[None],
        key_grad[None],
        value_grad[None],
        gain_grads[0],
        gain_grads[1],
    )


def solution(mesh):
    tokens = P("dp", ("blk", "head"), None)
    features = P(("dp", "blk", "head"))
    return jax.shard_map(
        shards,
        mesh=mesh,
        in_specs=(tokens, tokens, tokens, tokens, P(), P(), P("dp", None, None), P("dp", None)),
        out_specs=(tokens, tokens, tokens, tokens, features, features),
        check_vma=False,
    )
```

```python
import functools

import jax
import jax.numpy as jnp
from jax import lax
from jax.experimental import pallas as pl
from jax.experimental.pallas import tpu as pltpu
from jax.sharding import PartitionSpec as P

HS = 128
TILE = 192
KMAX = 12
HEADS = 24
HPD = 3
COLS = 4
NB = 8
NH = 8
F = HEADS * HS
CH = 2 * TILE
ROWS = 16
EPSILON = 1e-06
SCALE = HS**-0.5
SCALE2 = SCALE * 1.4426950408889634
FAR = -1e30
f32 = jnp.float32
bf16 = jnp.bfloat16


def nn(a, b):
    return lax.dot_general(a, b, (((1,), (0,)), ((), ())), preferred_element_type=f32)


def nt(a, b):
    return lax.dot_general(a, b, (((1,), (1,)), ((), ())), preferred_element_type=f32)


def group_of(slab, device):
    low = device % 2
    return device - low + (low + slab // 4) % 2


def wait_for(ref, sem):
    pltpu.make_async_copy(ref, ref, sem).wait()


def kernel(
    q_in,
    k_in,
    v_in,
    g_in,
    q_gain,
    k_gain,
    bias,
    att_out,
    qgrad_out,
    kgrad_out,
    vgrad_out,
    gain_out,
    q_stage,
    k_stage,
    q_fac,
    k_fac,
    qbuf,
    gbuf,
    kbuf,
    vbuf,
    kt_buf,
    vt_buf,
    s_buf,
    p_buf,
    acc_k,
    acc_v,
    own_acc,
    edge_send,
    edge_recv,
    own_send,
    o_send,
    dq_send,
    dq_recv,
    dk_recv,
    gain_tab,
    gain_recv,
    gain_sem,
    in_send,
    in_recv,
    halo_send,
    halo_recv,
    edge_ssem,
    edge_rsem,
    back_send,
    back_recv,
):
    d = lax.axis_index("dp")
    b = lax.axis_index("blk")
    tile = lax.axis_index("head")
    g = group_of(b, tile)
    has_low = b > 0
    has_high = b < NB - 1
    below = {"blk": b - 1, "head": group_of(b - 1, g)}
    above = {"blk": b + 1, "head": group_of(b + 1, g)}
    my_row = tile // COLS
    my_col = tile % COLS
    gain_group = d * 4 + b // 2
    gain_self = gain_group == g
    my_rows = pl.ds(pl.multiple_of(my_row * TILE, TILE), TILE)

    barrier = pltpu.get_barrier_semaphore()

    def greet(i, carry):
        pl.semaphore_signal(barrier, inc=1, device_id={"head": (tile + i) % NH})
        return carry

    lax.fori_loop(1, NH, greet, 0)

    def gain_target(j):
        return {"dp": g // 4, "blk": 2 * (g % 4) + j // NH, "head": j % NH}

    def gain_target_is_me(j):
        return (g // 4 == d) & (2 * (g % 4) + j // NH == b) & (j % NH == tile)

    def greet_gain(j, carry):
        @pl.when(jnp.logical_not(gain_target_is_me(j)))
        def _():
            pl.semaphore_signal(barrier, inc=1, device_id=gain_target(j))

        @pl.when(jnp.logical_not((j // NB == d) & (j % NB == b) & gain_self))
        def _():
            pl.semaphore_signal(
                barrier,
                inc=1,
                device_id={"dp": j // NB, "blk": j % NB, "head": group_of(j % NB, gain_group)},
            )

        return carry

    lax.fori_loop(0, 2 * NB, greet_gain, 0)

    @pl.when(has_low)
    def _():
        pl.semaphore_signal(barrier, inc=1, device_id=below)

    @pl.when(has_high)
    def _():
        pl.semaphore_signal(barrier, inc=1, device_id=above)

    def clear_side(slab, side):
        zeros = jnp.zeros((CH, HS), bf16)

        def one(e, carry):
            h, c = e // COLS, e % COLS
            kbuf[h, c, slab] = zeros
            vbuf[h, c, slab] = zeros
            edge_recv[e, side, 0] = zeros
            edge_recv[e, side, 1] = zeros
            return carry

        lax.fori_loop(0, HPD * COLS, one, 0)

    @pl.when(jnp.logical_not(has_low))
    def _():
        clear_side(0, 0)

    @pl.when(jnp.logical_not(has_high))
    def _():
        clear_side(2, 1)

    def normalize(x_in, gain, stage, fac):
        def block(i, carry):
            rows = pl.ds(pl.multiple_of(i * ROWS, ROWS), ROWS)
            total = jnp.zeros((ROWS, HS), f32)
            for h in range(HEADS):
                x = x_in[rows, h * HS : (h + 1) * HS].astype(f32)
                total = total + x * x
            mean = jnp.sum(total, axis=1, keepdims=True) * (1.0 / F)
            factor = jnp.broadcast_to(lax.rsqrt(mean + EPSILON), (ROWS, HS))
            fac[rows, :] = factor
            for h in range(HEADS):
                x = x_in[rows, h * HS : (h + 1) * HS].astype(f32)
                stage[h, rows, :] = (x * factor * gain[:, h * HS : (h + 1) * HS]).astype(bf16)
            return carry

        lax.fori_loop(0, TILE // ROWS, block, 0)

    def send_in(h, which, src_of, dst):
        here = pltpu.make_async_copy(src_of(g * HPD + h), dst, in_recv.at[which, h])
        here.start()

        def one(i, carry):
            to = (tile + i) % NH
            pltpu.make_async_remote_copy(
                src_ref=src_of(group_of(b, to) * HPD + h),
                dst_ref=dst,
                send_sem=in_send.at[which],
                recv_sem=in_recv.at[which, h],
                device_id={"head": to},
            ).start()
            return carry

        lax.fori_loop(1, NH, one, 0)

    def columns(h):
        return pl.ds(pl.multiple_of(h * HS, HS), HS)

    def send_k(h):
        send_in(h, 0, lambda n: k_stage.at[n], kbuf.at[h, my_col, 1, my_rows])

    def send_v(h):
        send_in(h, 1, lambda n: v_in.at[:, columns(n)], vbuf.at[h, my_col, 1, my_rows])

    def send_q(h):
        send_in(h, 2, lambda n: q_stage.at[n], qbuf.at[h, my_col, my_rows])

    def send_g(h):
        send_in(h, 3, lambda n: g_in.at[:, columns(n)], gbuf.at[h, my_col, my_rows])

    normalize(k_in, k_gain, k_stage, k_fac)
    pl.semaphore_wait(
        barrier,
        NH
        - 1
        + 4 * NB
        - 2 * gain_self.astype(jnp.int32)
        + has_low.astype(jnp.int32)
        + has_high.astype(jnp.int32),
    )
    send_v(0)
    send_k(0)
    normalize(q_in, q_gain, q_stage, q_fac)
    send_q(0)
    send_g(0)

    def rest(h, carry):
        send_k(h)
        send_v(h)
        send_q(h)
        send_g(h)
        return carry

    lax.fori_loop(1, HPD, rest, 0)

    def halo_copy(h, which, up):
        buf = (kbuf, vbuf)[which]
        side = 0 if up else 1
        return pltpu.make_async_remote_copy(
            src_ref=buf.at[h, :, 1],
            dst_ref=buf.at[h, :, 0 if up else 2],
            send_sem=halo_send.at[h, which, side],
            recv_sem=halo_recv.at[h, which, side],
            device_id=above if up else below,
        )

    def forward(h):
        wait_for(kbuf.at[h, :, 1], in_recv.at[0, h])
        wait_for(vbuf.at[h, :, 1], in_recv.at[1, h])
        for which in range(2):

            @pl.when(has_high)
            def _():
                halo_copy(h, which, True).start()

            @pl.when(has_low)
            def _():
                halo_copy(h, which, False).start()

    def await_halo(h):
        for which in range(2):

            @pl.when(has_low)
            def _():
                halo_copy(h, which, True).wait_recv()

            @pl.when(has_high)
            def _():
                halo_copy(h, which, False).wait_recv()

    def send_back(which, src, dst, t):
        @pl.when(t == tile)
        def _():
            pltpu.make_async_copy(src, dst, back_recv.at[which]).start()

        @pl.when(t != tile)
        def _():
            pltpu.make_async_remote_copy(
                src_ref=src,
                dst_ref=dst,
                send_sem=back_send.at[which],
                recv_sem=back_recv.at[which],
                device_id={"head": t},
            ).start()

    def attend(h, c):
        low = jnp.maximum(c - 1, 0) * 3
        high = jnp.minimum(c + 2, COLS) * 3
        q = qbuf[h, c]

        def first(j, top):
            s = nt(kbuf[h, j // 3, j % 3], q)
            s_buf[j - low] = s
            away = bias[c * 12 + j]
            top = jnp.maximum(top, jnp.max(s[:TILE], axis=0, keepdims=True) + away[0:1])
            return jnp.maximum(top, jnp.max(s[TILE:], axis=0, keepdims=True) + away[1:2])

        top = lax.fori_loop(low, high, first, jnp.full((1, CH), 2 * FAR, f32)) * SCALE2

        def second(j, carry):
            total, out = carry
            away = bias[c * 12 + j]
            s = s_buf[j - low]
            e0 = jnp.exp2(s[:TILE] * SCALE2 - (top - away[0:1]))
            e1 = jnp.exp2(s[TILE:] * SCALE2 - (top - away[1:2]))
            total = total + jnp.sum(e0, axis=0, keepdims=True) + jnp.sum(e1, axis=0, keepdims=True)
            e = jnp.concatenate([e0.astype(bf16), e1.astype(bf16)], axis=0)
            p_buf[j - low] = e
            return total, out + nn(vt_buf[j], e)

        total, out = lax.fori_loop(
            low, high, second, (jnp.zeros((1, CH), f32), jnp.zeros((HS, CH), f32))
        )
        inverse = 1.0 / total
        out = out * inverse
        o_send[h, c] = out.T.astype(bf16)
        grad = gbuf[h, c].astype(f32).T
        delta = jnp.sum(out * grad, axis=0, keepdims=True) * inverse
        grad = grad * inverse
        grad_t = grad.astype(bf16)
        grad_s = grad.T.astype(bf16)

        def third(j, dq):
            e = p_buf[j - low]
            dp = nn(vbuf[h, j // 3, j % 3], grad_t)
            ds = (e.astype(f32) * (dp - delta)).astype(bf16)
            acc_v[j] += nn(e, grad_s)
            acc_k[j] += nn(ds, q)
            return dq + nn(kt_buf[j], ds)

        dq = lax.fori_loop(low, high, third, jnp.zeros((HS, CH), f32))
        dq = (dq * SCALE).T.astype(bf16)
        dq_send[h, c] = dq
        gain_tab[h, 0:1, :] += jnp.sum(dq.astype(f32) * q.astype(f32), axis=0, keepdims=True)
        for r in range(2):
            rows = pl.ds(r * TILE, TILE)
            t = r * COLS + c
            send_back(0, o_send.at[h, c, rows], att_out.at[:, columns(g * HPD + h)], t)
            send_back(1, dq_send.at[h, c, rows], dq_recv.at[g * HPD + h], t)

    def edge_copy(e, up):
        return pltpu.make_async_remote_copy(
            src_ref=edge_send.at[e, 1 if up else 0],
            dst_ref=edge_recv.at[e, 0 if up else 1],
            send_sem=edge_ssem.at[e, 1 if up else 0],
            recv_sem=edge_rsem.at[e, 0 if up else 1],
            device_id=above if up else below,
        )

    def finish(h, c):
        e = h * COLS + c
        for side, slab in ((0, 0), (1, 2)):
            edge_send[e, side, 0] = (acc_k[c * 3 + slab] * SCALE).astype(bf16)
            edge_send[e, side, 1] = acc_v[c * 3 + slab].astype(bf16)
        own_acc[e, 0] = acc_k[c * 3 + 1] * SCALE
        own_acc[e, 1] = acc_v[c * 3 + 1]

        @pl.when(has_high)
        def _():
            edge_copy(e, True).start()

        @pl.when(has_low)
        def _():
            edge_copy(e, False).start()

    def settle(h, c):
        e = h * COLS + c

        @pl.when(has_low)
        def _():
            edge_copy(e, True).wait_recv()

        @pl.when(has_high)
        def _():
            edge_copy(e, False).wait_recv()

        for a in range(2):
            own_send[e, a] = (
                own_acc[e, a] + edge_recv[e, 0, a].astype(f32) + edge_recv[e, 1, a].astype(f32)
            ).astype(bf16)
        product = own_send[e, 0].astype(f32) * kbuf[h, c, 1].astype(f32)
        gain_tab[h, 1:2, :] += jnp.sum(product, axis=0, keepdims=True)
        for r in range(2):
            rows = pl.ds(r * TILE, TILE)
            t = r * COLS + c
            send_back(2, own_send.at[e, 0, rows], dk_recv.at[g * HPD + h], t)
            send_back(3, own_send.at[e, 1, rows], vgrad_out.at[:, columns(g * HPD + h)], t)

    def start_head(h):
        await_halo(h)
        wait_for(qbuf.at[h], in_recv.at[2, h])
        wait_for(gbuf.at[h], in_recv.at[3, h])

        def turn(j, carry):
            kt_buf[j] = kbuf[h, j // 3, j % 3].T
            vt_buf[j] = vbuf[h, j // 3, j % 3].T
            acc_k[j] = jnp.zeros((CH, HS), f32)
            acc_v[j] = jnp.zeros((CH, HS), f32)
            return carry

        lax.fori_loop(0, 3 * COLS, turn, 0)

    gain_tab[...] = jnp.zeros_like(gain_tab)
    forward(0)

    def step(s, carry):
        h, c = s // COLS, s % COLS

        @pl.when(c == 0)
        def _():
            start_head(h)

        @pl.when((c == 1) & (h < HPD - 1))
        def _():
            forward(h + 1)

        attend(h, c)

        @pl.when(c > 0)
        def _():
            finish(h, c - 1)

        @pl.when(c == COLS - 1)
        def _():
            finish(h, COLS - 1)

        @pl.when(h > 0)
        def _():
            settle(h - 1, c)

        return carry

    lax.fori_loop(0, HPD * COLS, step, 0)

    def last(c, carry):
        settle(HPD - 1, c)
        return carry

    lax.fori_loop(0, COLS, last, 0)

    for h in range(HPD):
        for row, gain in ((0, q_gain), (1, k_gain)):
            gain_tab[h, row : row + 1, :] = gain_tab[h, row : row + 1, :] / gain[:, columns(g * HPD + h)]

    def give(j, carry):
        dst = gain_recv.at[d * NB + b]
        me = gain_target_is_me(j)

        @pl.when(me)
        def _():
            pltpu.make_async_copy(gain_tab, dst, gain_sem.at[1]).start()

        @pl.when(jnp.logical_not(me))
        def _():
            pltpu.make_async_remote_copy(
                src_ref=gain_tab,
                dst_ref=dst,
                send_sem=gain_sem.at[0],
                recv_sem=gain_sem.at[1],
                device_id=gain_target(j),
            ).start()

        return carry

    lax.fori_loop(0, 2 * NB, give, 0)

    def norm_back(x_in, gain, fac, d_recv, grad_out):
        def block(i, carry):
            rows = pl.ds(pl.multiple_of(i * ROWS, ROWS), ROWS)
            factor = fac[rows, :]
            total = jnp.zeros((ROWS, HS), f32)
            for h in range(HEADS):
                lanes = slice(h * HS, (h + 1) * HS)
                hat = x_in[rows, lanes].astype(f32) * factor
                product = d_recv[h, rows, :].astype(f32) * hat
                total = total + product * gain[:, lanes]
            inner = jnp.sum(total, axis=1, keepdims=True) * (1.0 / F)
            for h in range(HEADS):
                lanes = slice(h * HS, (h + 1) * HS)
                hat = x_in[rows, lanes].astype(f32) * factor
                scaled = d_recv[h, rows, :].astype(f32) * gain[:, lanes]
                grad_out[rows, lanes] = (factor * (scaled - hat * inner)).astype(bf16)
            return carry

        lax.fori_loop(0, TILE // ROWS, block, 0)

    wait_for(dq_recv, back_recv.at[1])
    norm_back(q_in, q_gain, q_fac, dq_recv, qgrad_out)
    wait_for(dk_recv, back_recv.at[2])
    norm_back(k_in, k_gain, k_fac, dk_recv, kgrad_out)
    wait_for(gain_recv, gain_sem.at[1])
    start = 24 * ((b % 2) * NH + tile)
    lane = lax.broadcasted_iota(jnp.int32, (HS, HS), 1)
    source = lax.broadcasted_iota(jnp.int32, (HS, HS), 0)
    sums = jnp.zeros((8, HS), f32)
    for h in range(HPD):
        pick = ((source + h * HS == lane + start) & (lane < 24)).astype(f32)
        part = gain_recv[0, h]
        for i in range(1, 2 * NB):
            part = part + gain_recv[i, h]
        sums = sums + jnp.dot(
            part, pick, precision=lax.Precision.HIGHEST, preferred_element_type=f32
        )
    gain_out[...] = sums
    wait_for(att_out, back_recv.at[0])
    wait_for(vgrad_out, back_recv.at[3])

    wait_for(gain_recv.at[0 : 2 * NB - 1], gain_sem.at[0])

    @pl.when(jnp.logical_not(gain_self))
    def _():
        wait_for(gain_recv.at[0], gain_sem.at[0])

    sent = dq_recv.at[0 : HEADS - HPD]
    for which in range(4):
        wait_for(sent, in_send.at[which])
        wait_for(sent, back_send.at[which])

    def drain(h, carry):
        for which in range(2):

            @pl.when(has_high)
            def _():
                halo_copy(h, which, True).wait_send()

            @pl.when(has_low)
            def _():
                halo_copy(h, which, False).wait_send()

        return carry

    lax.fori_loop(0, HPD, drain, 0)

    def drain_edges(e, carry):
        @pl.when(has_high)
        def _():
            edge_copy(e, True).wait_send()

        @pl.when(has_low)
        def _():
            edge_copy(e, False).wait_send()

        return carry

    lax.fori_loop(0, HPD * COLS, drain_edges, 0)


def bias_table(tile_lists, tile_counts):
    per_slab = 2 * COLS
    slab = lax.axis_index("blk")
    lists = lax.dynamic_slice_in_dim(tile_lists, slab * per_slab, per_slab, 0)
    counts = lax.dynamic_slice_in_dim(tile_counts, slab * per_slab, per_slab, 0)
    relative = lists - (slab - 1) * per_slab
    live = jnp.arange(KMAX)[None, :] < counts[:, None]
    named = (relative[:, :, None] == jnp.arange(3 * per_slab)[None, None, :]) & live[:, :, None]
    table = jnp.where(jnp.any(named, axis=1), 0.0, FAR).astype(f32)
    table = table.reshape(2, COLS, 3, 2, COLS).transpose(1, 4, 2, 3, 0)
    return jnp.repeat(table.reshape(COLS * 12, 2, 2), TILE, axis=2)


def shards(
    query_input, key_input, value_input, output_grad, query_gain, key_gain, tile_lists, tile_counts
):
    table = bias_table(tile_lists[0], tile_counts[0])
    vmem = pl.BlockSpec(memory_space=pltpu.VMEM)
    anywhere = pl.BlockSpec(memory_space=pl.ANY)
    token = jax.ShapeDtypeStruct((TILE, F), bf16)
    n = HPD * COLS
    attention, query_grad, key_grad, value_grad, gains = pl.pallas_call(
        kernel,
        name="tiles",
        out_shape=(token, token, token, token, jax.ShapeDtypeStruct((8, HS), f32)),
        in_specs=[vmem] * 7,
        out_specs=(anywhere, vmem, vmem, anywhere, vmem),
        scratch_shapes=[
            pltpu.VMEM((HEADS, TILE, HS), bf16),
            pltpu.VMEM((HEADS, TILE, HS), bf16),
            pltpu.VMEM((TILE, HS), f32),
            pltpu.VMEM((TILE, HS), f32),
            pltpu.VMEM((HPD, COLS, CH, HS), bf16),
            pltpu.VMEM((HPD, COLS, CH, HS), bf16),
            pltpu.VMEM((HPD, COLS, 3, CH, HS), bf16),
            pltpu.VMEM((HPD, COLS, 3, CH, HS), bf16),
            pltpu.VMEM((12, HS, CH), bf16),
            pltpu.VMEM((12, HS, CH), bf16),
            pltpu.VMEM((9, CH, CH), f32),
            pltpu.VMEM((9, CH, CH), bf16),
            pltpu.VMEM((12, CH, HS), f32),
            pltpu.VMEM((12, CH, HS), f32),
            pltpu.VMEM((n, 2, CH, HS), f32),
            pltpu.VMEM((n, 2, 2, CH, HS), bf16),
            pltpu.VMEM((n, 2, 2, CH, HS), bf16),
            pltpu.VMEM((n, 2, CH, HS), bf16),
            pltpu.VMEM((HPD, COLS, CH, HS), bf16),
            pltpu.VMEM((HPD, COLS, CH, HS), bf16),
            pltpu.VMEM((HEADS, TILE, HS), bf16),
            pltpu.VMEM((HEADS, TILE, HS), bf16),
            pltpu.VMEM((HPD, 8, HS), f32),
            pltpu.VMEM((2 * NB, HPD, 8, HS), f32),
            pltpu.SemaphoreType.DMA((2,)),
            pltpu.SemaphoreType.DMA((4,)),
            pltpu.SemaphoreType.DMA((4, HPD)),
            pltpu.SemaphoreType.DMA((HPD, 2, 2)),
            pltpu.SemaphoreType.DMA((HPD, 2, 2)),
            pltpu.SemaphoreType.DMA((n, 2)),
            pltpu.SemaphoreType.DMA((n, 2)),
            pltpu.SemaphoreType.DMA((4,)),
            pltpu.SemaphoreType.DMA((4,)),
        ],
        compiler_params=pltpu.CompilerParams(
            collective_id=0, has_side_effects=True, vmem_limit_bytes=62 * 1024 * 1024
        ),
    )(
        query_input[0],
        key_input[0],
        value_input[0],
        output_grad[0],
        query_gain[None],
        key_gain[None],
        table,
    )
    width = F // (2 * NB * NH)
    return (
        attention[None],
        query_grad[None],
        key_grad[None],
        value_grad[None],
        gains[0, :width],
        gains[1, :width],
    )


def solution(mesh):
    tokens = P("dp", ("blk", "head"), None)
    features = P(("dp", "blk", "head"))
    return jax.shard_map(
        shards,
        mesh=mesh,
        in_specs=(tokens, tokens, tokens, tokens, P(), P(), P("dp", None, None), P("dp", None)),
        out_specs=(tokens, tokens, tokens, tokens, features, features),
        check_vma=False,
    )
```

```python
import functools

import jax
import jax.numpy as jnp
from jax import lax
from jax.experimental import pallas as pl
from jax.experimental.pallas import tpu as pltpu
from jax.sharding import PartitionSpec as P

HS = 128
TILE = 192
KMAX = 12
HEADS = 24
HPD = 3
COLS = 4
NB = 8
NH = 8
F = HEADS * HS
CH = 2 * TILE
ROWS = 16
EPSILON = 1e-06
SCALE = HS**-0.5
SCALE2 = SCALE * 1.4426950408889634
FAR = -1e30
f32 = jnp.float32
bf16 = jnp.bfloat16


def nn(a, b):
    return lax.dot_general(a, b, (((1,), (0,)), ((), ())), preferred_element_type=f32)


def nt(a, b):
    return lax.dot_general(a, b, (((1,), (1,)), ((), ())), preferred_element_type=f32)


def group_of(slab, device):
    low = device % 2
    return device - low + (low + slab // 4) % 2


def wait_for(ref, sem):
    pltpu.make_async_copy(ref, ref, sem).wait()


def kernel(
    q_in,
    k_in,
    v_in,
    g_in,
    q_gain,
    k_gain,
    bias,
    att_out,
    qgrad_out,
    kgrad_out,
    vgrad_out,
    gain_out,
    q_stage,
    k_stage,
    q_fac,
    k_fac,
    qbuf,
    gbuf,
    kbuf,
    vbuf,
    kt_buf,
    vt_buf,
    s_buf,
    p_buf,
    ds_buf,
    acc_k,
    acc_v,
    own_acc,
    edge_send,
    edge_recv,
    own_send,
    o_send,
    dq_send,
    dq_recv,
    dk_recv,
    gain_tab,
    gain_recv,
    gain_sem,
    in_send,
    in_recv,
    halo_send,
    halo_recv,
    edge_ssem,
    edge_rsem,
    back_send,
    back_recv,
):
    d = lax.axis_index("dp")
    b = lax.axis_index("blk")
    tile = lax.axis_index("head")
    g = group_of(b, tile)
    has_low = b > 0
    has_high = b < NB - 1
    below = {"blk": b - 1, "head": group_of(b - 1, g)}
    above = {"blk": b + 1, "head": group_of(b + 1, g)}
    my_row = tile // COLS
    my_col = tile % COLS
    gain_group = d * 4 + b // 2
    gain_self = gain_group == g
    my_rows = pl.ds(pl.multiple_of(my_row * TILE, TILE), TILE)

    barrier = pltpu.get_barrier_semaphore()

    def greet(i, carry):
        pl.semaphore_signal(barrier, inc=1, device_id={"head": (tile + i) % NH})
        return carry

    lax.fori_loop(1, NH, greet, 0)

    def gain_target(j):
        return {"dp": g // 4, "blk": 2 * (g % 4) + j // NH, "head": j % NH}

    def gain_target_is_me(j):
        return (g // 4 == d) & (2 * (g % 4) + j // NH == b) & (j % NH == tile)

    def greet_gain(j, carry):
        @pl.when(jnp.logical_not(gain_target_is_me(j)))
        def _():
            pl.semaphore_signal(barrier, inc=1, device_id=gain_target(j))

        @pl.when(jnp.logical_not((j // NB == d) & (j % NB == b) & gain_self))
        def _():
            pl.semaphore_signal(
                barrier,
                inc=1,
                device_id={"dp": j // NB, "blk": j % NB, "head": group_of(j % NB, gain_group)},
            )

        return carry

    lax.fori_loop(0, 2 * NB, greet_gain, 0)

    @pl.when(has_low)
    def _():
        pl.semaphore_signal(barrier, inc=1, device_id=below)

    @pl.when(has_high)
    def _():
        pl.semaphore_signal(barrier, inc=1, device_id=above)

    def clear_side(slab, side):
        zeros = jnp.zeros((CH, HS), bf16)

        def one(e, carry):
            h, c = e // COLS, e % COLS
            kbuf[h, c, slab] = zeros
            vbuf[h, c, slab] = zeros
            edge_recv[e, side, 0] = zeros
            edge_recv[e, side, 1] = zeros
            return carry

        lax.fori_loop(0, HPD * COLS, one, 0)

    @pl.when(jnp.logical_not(has_low))
    def _():
        clear_side(0, 0)

    @pl.when(jnp.logical_not(has_high))
    def _():
        clear_side(2, 1)

    def normalize(x_in, gain, stage, fac):
        def block(i, carry):
            rows = pl.ds(pl.multiple_of(i * ROWS, ROWS), ROWS)
            total = jnp.zeros((ROWS, HS), f32)
            for h in range(HEADS):
                x = x_in[rows, h * HS : (h + 1) * HS].astype(f32)
                total = total + x * x
            mean = jnp.sum(total, axis=1, keepdims=True) * (1.0 / F)
            factor = jnp.broadcast_to(lax.rsqrt(mean + EPSILON), (ROWS, HS))
            fac[rows, :] = factor
            for h in range(HEADS):
                x = x_in[rows, h * HS : (h + 1) * HS].astype(f32)
                stage[h, rows, :] = (x * factor * gain[:, h * HS : (h + 1) * HS]).astype(bf16)
            return carry

        lax.fori_loop(0, TILE // ROWS, block, 0)

    def send_in(h, which, src_of, dst):
        here = pltpu.make_async_copy(src_of(g * HPD + h), dst, in_recv.at[which, h])
        here.start()

        def one(i, carry):
            to = (tile + i) % NH
            pltpu.make_async_remote_copy(
                src_ref=src_of(group_of(b, to) * HPD + h),
                dst_ref=dst,
                send_sem=in_send.at[which],
                recv_sem=in_recv.at[which, h],
                device_id={"head": to},
            ).start()
            return carry

        lax.fori_loop(1, NH, one, 0)

    def columns(h):
        return pl.ds(pl.multiple_of(h * HS, HS), HS)

    def send_k(h):
        send_in(h, 0, lambda n: k_stage.at[n], kbuf.at[h, my_col, 1, my_rows])

    def send_v(h):
        send_in(h, 1, lambda n: v_in.at[:, columns(n)], vbuf.at[h, my_col, 1, my_rows])

    def send_q(h):
        send_in(h, 2, lambda n: q_stage.at[n], qbuf.at[h, my_col, my_rows])

    def send_g(h):
        send_in(h, 3, lambda n: g_in.at[:, columns(n)], gbuf.at[h, my_col, my_rows])

    normalize(k_in, k_gain, k_stage, k_fac)
    pl.semaphore_wait(
        barrier,
        NH
        - 1
        + 4 * NB
        - 2 * gain_self.astype(jnp.int32)
        + has_low.astype(jnp.int32)
        + has_high.astype(jnp.int32),
    )
    send_v(0)
    send_k(0)
    normalize(q_in, q_gain, q_stage, q_fac)
    send_q(0)
    send_g(0)

    def halo_copy(h, which, up):
        buf = (kbuf, vbuf)[which]
        side = 0 if up else 1
        return pltpu.make_async_remote_copy(
            src_ref=buf.at[h, :, 1],
            dst_ref=buf.at[h, :, 0 if up else 2],
            send_sem=halo_send.at[h, which, side],
            recv_sem=halo_recv.at[h, which, side],
            device_id=above if up else below,
        )

    def forward(h):
        wait_for(kbuf.at[h, :, 1], in_recv.at[0, h])
        wait_for(vbuf.at[h, :, 1], in_recv.at[1, h])
        for which in range(2):

            @pl.when(has_high)
            def _():
                halo_copy(h, which, True).start()

            @pl.when(has_low)
            def _():
                halo_copy(h, which, False).start()

    def await_halo(h):
        for which in range(2):

            @pl.when(has_low)
            def _():
                halo_copy(h, which, True).wait_recv()

            @pl.when(has_high)
            def _():
                halo_copy(h, which, False).wait_recv()

    def send_back(which, src, dst, t):
        @pl.when(t == tile)
        def _():
            pltpu.make_async_copy(src, dst, back_recv.at[which]).start()

        @pl.when(t != tile)
        def _():
            pltpu.make_async_remote_copy(
                src_ref=src,
                dst_ref=dst,
                send_sem=back_send.at[which],
                recv_sem=back_recv.at[which],
                device_id={"head": t},
            ).start()

    def attend(h, c):
        low = jnp.maximum(c - 1, 0)
        high = jnp.minimum(c + 2, COLS)
        q = qbuf[h, c]

        def first(k, top):
            for slab in range(3):
                s = nt(kbuf[h, k, slab], q)
                s_buf[k - low, slab] = s
                away = bias[c * 12 + k * 3 + slab]
                top = jnp.maximum(top, jnp.max(s[:TILE], axis=0, keepdims=True) + away[0:1])
                top = jnp.maximum(top, jnp.max(s[TILE:], axis=0, keepdims=True) + away[1:2])
            return top

        top = lax.fori_loop(low, high, first, jnp.full((1, CH), 2 * FAR, f32)) * SCALE2

        def second(k, carry):
            total, out = carry
            for slab in range(3):
                away = bias[c * 12 + k * 3 + slab]
                s = s_buf[k - low, slab]
                e0 = jnp.exp2(s[:TILE] * SCALE2 - (top - away[0:1]))
                e1 = jnp.exp2(s[TILE:] * SCALE2 - (top - away[1:2]))
                total = total + jnp.sum(e0, axis=0, keepdims=True)
                total = total + jnp.sum(e1, axis=0, keepdims=True)
                p_buf[k - low, slab * CH : slab * CH + TILE] = e0.astype(bf16)
                p_buf[k - low, slab * CH + TILE : (slab + 1) * CH] = e1.astype(bf16)
            return total, out + nn(vt_buf[k], p_buf[k - low])

        total, out = lax.fori_loop(
            low, high, second, (jnp.zeros((1, CH), f32), jnp.zeros((HS, CH), f32))
        )
        inverse = 1.0 / total
        out = out * inverse
        o_send[h, c] = out.T.astype(bf16)
        grad = gbuf[h, c].astype(f32).T
        delta = jnp.sum(out * grad, axis=0, keepdims=True) * inverse
        grad = grad * inverse
        grad_t = grad.astype(bf16)
        grad_s = grad.T.astype(bf16)

        def third(k, dq):
            for slab in range(3):
                e = p_buf[k - low, slab * CH : (slab + 1) * CH]
                dp = nn(vbuf[h, k, slab], grad_t)
                ds = (e.astype(f32) * (dp - delta)).astype(bf16)
                ds_buf[slab * CH : (slab + 1) * CH] = ds
                acc_v[k * 3 + slab] += nn(e, grad_s)
                acc_k[k * 3 + slab] += nn(ds, q)
            return dq + nn(kt_buf[k], ds_buf[...])

        dq = lax.fori_loop(low, high, third, jnp.zeros((HS, CH), f32))
        dq = (dq * SCALE).T.astype(bf16)
        dq_send[h, c] = dq
        gain_tab[h, 0:1, :] += jnp.sum(dq.astype(f32) * q.astype(f32), axis=0, keepdims=True)
        for r in range(2):
            rows = pl.ds(r * TILE, TILE)
            t = r * COLS + c
            send_back(0, o_send.at[h, c, rows], att_out.at[:, columns(g * HPD + h)], t)
            send_back(1, dq_send.at[h, c, rows], dq_recv.at[g * HPD + h], t)

    def edge_copy(e, up):
        return pltpu.make_async_remote_copy(
            src_ref=edge_send.at[e, 1 if up else 0],
            dst_ref=edge_recv.at[e, 0 if up else 1],
            send_sem=edge_ssem.at[e, 1 if up else 0],
            recv_sem=edge_rsem.at[e, 0 if up else 1],
            device_id=above if up else below,
        )

    def finish(h, c):
        e = h * COLS + c
        for side, slab in ((0, 0), (1, 2)):
            edge_send[e, side, 0] = (acc_k[c * 3 + slab] * SCALE).astype(bf16)
            edge_send[e, side, 1] = acc_v[c * 3 + slab].astype(bf16)
        own_acc[e, 0] = acc_k[c * 3 + 1] * SCALE
        own_acc[e, 1] = acc_v[c * 3 + 1]

        @pl.when(has_high)
        def _():
            edge_copy(e, True).start()

        @pl.when(has_low)
        def _():
            edge_copy(e, False).start()

    def settle(e):
        h, c = e // COLS, e % COLS

        @pl.when(has_low)
        def _():
            edge_copy(e, True).wait_recv()

        @pl.when(has_high)
        def _():
            edge_copy(e, False).wait_recv()

        for a in range(2):
            own_send[e, a] = (
                own_acc[e, a] + edge_recv[e, 0, a].astype(f32) + edge_recv[e, 1, a].astype(f32)
            ).astype(bf16)
        product = own_send[e, 0].astype(f32) * kbuf[h, c, 1].astype(f32)
        gain_tab[h, 1:2, :] += jnp.sum(product, axis=0, keepdims=True)
        for r in range(2):
            rows = pl.ds(r * TILE, TILE)
            t = r * COLS + c
            send_back(2, own_send.at[e, 0, rows], dk_recv.at[g * HPD + h], t)
            send_back(3, own_send.at[e, 1, rows], vgrad_out.at[:, columns(g * HPD + h)], t)

    def start_head(h):
        await_halo(h)
        wait_for(qbuf.at[h], in_recv.at[2, h])
        wait_for(gbuf.at[h], in_recv.at[3, h])

        def turn(k, carry):
            for slab in range(3):
                keys = slice(slab * CH, (slab + 1) * CH)
                kt_buf[k, :, keys] = kbuf[h, k, slab].T
                vt_buf[k, :, keys] = vbuf[h, k, slab].T
                acc_k[k * 3 + slab] = jnp.zeros((CH, HS), f32)
                acc_v[k * 3 + slab] = jnp.zeros((CH, HS), f32)
            return carry

        lax.fori_loop(0, COLS, turn, 0)

    gain_tab[...] = jnp.zeros_like(gain_tab)
    forward(0)

    def rest(h, carry):
        send_k(h)
        send_v(h)
        send_q(h)
        send_g(h)
        return carry

    lax.fori_loop(1, HPD, rest, 0)

    def step(s, carry):
        h, c = s // COLS, s % COLS

        @pl.when(c == 0)
        def _():
            start_head(h)

        @pl.when((c == 1) & (h < HPD - 1))
        def _():
            forward(h + 1)

        attend(h, c)

        @pl.when(c > 0)
        def _():
            finish(h, c - 1)

        @pl.when(c == COLS - 1)
        def _():
            finish(h, COLS - 1)

        @pl.when(s > 1)
        def _():
            settle(s - 2)

        return carry

    lax.fori_loop(0, HPD * COLS, step, 0)

    def last(e, carry):
        settle(e)
        return carry

    lax.fori_loop(HPD * COLS - 2, HPD * COLS, last, 0)

    for h in range(HPD):
        for row, gain in ((0, q_gain), (1, k_gain)):
            gain_tab[h, row : row + 1, :] = gain_tab[h, row : row + 1, :] / gain[:, columns(g * HPD + h)]

    def give(j, carry):
        dst = gain_recv.at[d * NB + b]
        me = gain_target_is_me(j)

        @pl.when(me)
        def _():
            pltpu.make_async_copy(gain_tab, dst, gain_sem.at[1]).start()

        @pl.when(jnp.logical_not(me))
        def _():
            pltpu.make_async_remote_copy(
                src_ref=gain_tab,
                dst_ref=dst,
                send_sem=gain_sem.at[0],
                recv_sem=gain_sem.at[1],
                device_id=gain_target(j),
            ).start()

        return carry

    lax.fori_loop(0, 2 * NB, give, 0)

    def norm_back(x_in, gain, fac, d_recv, grad_out):
        def block(i, carry):
            rows = pl.ds(pl.multiple_of(i * ROWS, ROWS), ROWS)
            factor = fac[rows, :]
            total = jnp.zeros((ROWS, HS), f32)
            for h in range(HEADS):
                lanes = slice(h * HS, (h + 1) * HS)
                hat = x_in[rows, lanes].astype(f32) * factor
                product = d_recv[h, rows, :].astype(f32) * hat
                total = total + product * gain[:, lanes]
            inner = jnp.sum(total, axis=1, keepdims=True) * (1.0 / F)
            for h in range(HEADS):
                lanes = slice(h * HS, (h + 1) * HS)
                hat = x_in[rows, lanes].astype(f32) * factor
                scaled = d_recv[h, rows, :].astype(f32) * gain[:, lanes]
                grad_out[rows, lanes] = (factor * (scaled - hat * inner)).astype(bf16)
            return carry

        lax.fori_loop(0, TILE // ROWS, block, 0)

    wait_for(dq_recv, back_recv.at[1])
    norm_back(q_in, q_gain, q_fac, dq_recv, qgrad_out)
    wait_for(dk_recv, back_recv.at[2])
    norm_back(k_in, k_gain, k_fac, dk_recv, kgrad_out)
    wait_for(gain_recv, gain_sem.at[1])
    start = 24 * ((b % 2) * NH + tile)
    lane = lax.broadcasted_iota(jnp.int32, (HS, HS), 1)
    source = lax.broadcasted_iota(jnp.int32, (HS, HS), 0)
    sums = jnp.zeros((8, HS), f32)
    for h in range(HPD):
        pick = ((source + h * HS == lane + start) & (lane < 24)).astype(f32)
        part = gain_recv[0, h]
        for i in range(1, 2 * NB):
            part = part + gain_recv[i, h]
        sums = sums + jnp.dot(
            part, pick, precision=lax.Precision.HIGHEST, preferred_element_type=f32
        )
    gain_out[...] = sums
    wait_for(att_out, back_recv.at[0])
    wait_for(vgrad_out, back_recv.at[3])

    wait_for(gain_recv.at[0 : 2 * NB - 1], gain_sem.at[0])

    @pl.when(jnp.logical_not(gain_self))
    def _():
        wait_for(gain_recv.at[0], gain_sem.at[0])

    sent = dq_recv.at[0 : HEADS - HPD]
    for which in range(4):
        wait_for(sent, in_send.at[which])
        wait_for(sent, back_send.at[which])

    def drain(h, carry):
        for which in range(2):

            @pl.when(has_high)
            def _():
                halo_copy(h, which, True).wait_send()

            @pl.when(has_low)
            def _():
                halo_copy(h, which, False).wait_send()

        return carry

    lax.fori_loop(0, HPD, drain, 0)

    def drain_edges(e, carry):
        @pl.when(has_high)
        def _():
            edge_copy(e, True).wait_send()

        @pl.when(has_low)
        def _():
            edge_copy(e, False).wait_send()

        return carry

    lax.fori_loop(0, HPD * COLS, drain_edges, 0)


def bias_table(tile_lists, tile_counts):
    per_slab = 2 * COLS
    slab = lax.axis_index("blk")
    lists = lax.dynamic_slice_in_dim(tile_lists, slab * per_slab, per_slab, 0)
    counts = lax.dynamic_slice_in_dim(tile_counts, slab * per_slab, per_slab, 0)
    relative = lists - (slab - 1) * per_slab
    live = jnp.arange(KMAX)[None, :] < counts[:, None]
    named = (relative[:, :, None] == jnp.arange(3 * per_slab)[None, None, :]) & live[:, :, None]
    table = jnp.where(jnp.any(named, axis=1), 0.0, FAR).astype(f32)
    table = table.reshape(2, COLS, 3, 2, COLS).transpose(1, 4, 2, 3, 0)
    return jnp.repeat(table.reshape(COLS * 12, 2, 2), TILE, axis=2)


def shards(
    query_input, key_input, value_input, output_grad, query_gain, key_gain, tile_lists, tile_counts
):
    table = bias_table(tile_lists[0], tile_counts[0])
    vmem = pl.BlockSpec(memory_space=pltpu.VMEM)
    anywhere = pl.BlockSpec(memory_space=pl.ANY)
    token = jax.ShapeDtypeStruct((TILE, F), bf16)
    n = HPD * COLS
    attention, query_grad, key_grad, value_grad, gains = pl.pallas_call(
        kernel,
        name="tiles",
        out_shape=(token, token, token, token, jax.ShapeDtypeStruct((8, HS), f32)),
        in_specs=[vmem] * 7,
        out_specs=(anywhere, vmem, vmem, anywhere, vmem),
        scratch_shapes=[
            pltpu.VMEM((HEADS, TILE, HS), bf16),
            pltpu.VMEM((HEADS, TILE, HS), bf16),
            pltpu.VMEM((TILE, HS), f32),
            pltpu.VMEM((TILE, HS), f32),
            pltpu.VMEM((HPD, COLS, CH, HS), bf16),
            pltpu.VMEM((HPD, COLS, CH, HS), bf16),
            pltpu.VMEM((HPD, COLS, 3, CH, HS), bf16),
            pltpu.VMEM((HPD, COLS, 3, CH, HS), bf16),
            pltpu.VMEM((COLS, HS, 3 * CH), bf16),
            pltpu.VMEM((COLS, HS, 3 * CH), bf16),
            pltpu.VMEM((3, 3, CH, CH), f32),
            pltpu.VMEM((3, 3 * CH, CH), bf16),
            pltpu.VMEM((3 * CH, CH), bf16),
            pltpu.VMEM((12, CH, HS), f32),
            pltpu.VMEM((12, CH, HS), f32),
            pltpu.VMEM((n, 2, CH, HS), f32),
            pltpu.VMEM((n, 2, 2, CH, HS), bf16),
            pltpu.VMEM((n, 2, 2, CH, HS), bf16),
            pltpu.VMEM((n, 2, CH, HS), bf16),
            pltpu.VMEM((HPD, COLS, CH, HS), bf16),
            pltpu.VMEM((HPD, COLS, CH, HS), bf16),
            pltpu.VMEM((HEADS, TILE, HS), bf16),
            pltpu.VMEM((HEADS, TILE, HS), bf16),
            pltpu.VMEM((HPD, 8, HS), f32),
            pltpu.VMEM((2 * NB, HPD, 8, HS), f32),
            pltpu.SemaphoreType.DMA((2,)),
            pltpu.SemaphoreType.DMA((4,)),
            pltpu.SemaphoreType.DMA((4, HPD)),
            pltpu.SemaphoreType.DMA((HPD, 2, 2)),
            pltpu.SemaphoreType.DMA((HPD, 2, 2)),
            pltpu.SemaphoreType.DMA((n, 2)),
            pltpu.SemaphoreType.DMA((n, 2)),
            pltpu.SemaphoreType.DMA((4,)),
            pltpu.SemaphoreType.DMA((4,)),
        ],
        compiler_params=pltpu.CompilerParams(
            collective_id=0, has_side_effects=True, vmem_limit_bytes=62 * 1024 * 1024
        ),
    )(
        query_input[0],
        key_input[0],
        value_input[0],
        output_grad[0],
        query_gain[None],
        key_gain[None],
        table,
    )
    width = F // (2 * NB * NH)
    return (
        attention[None],
        query_grad[None],
        key_grad[None],
        value_grad[None],
        gains[0, :width],
        gains[1, :width],
    )


def solution(mesh):
    tokens = P("dp", ("blk", "head"), None)
    features = P(("dp", "blk", "head"))
    return jax.shard_map(
        shards,
        mesh=mesh,
        in_specs=(tokens, tokens, tokens, tokens, P(), P(), P("dp", None, None), P("dp", None)),
        out_specs=(tokens, tokens, tokens, tokens, features, features),
        check_vma=False,
    )
```

```python
import functools

import jax
import jax.numpy as jnp
from jax import lax
from jax.experimental import pallas as pl
from jax.experimental.pallas import tpu as pltpu
from jax.sharding import PartitionSpec as P

HS = 128
TILE = 192
KMAX = 12
HEADS = 24
HPD = 3
COLS = 4
NB = 8
NH = 8
F = HEADS * HS
CH = 2 * TILE
ROWS = 16
LAG = 3
EPSILON = 1e-06
SCALE = HS**-0.5
SCALE2 = SCALE * 1.4426950408889634
FAR = -1e30
NOWHERE = -1000
f32 = jnp.float32
bf16 = jnp.bfloat16


def nn(a, b):
    return lax.dot_general(a, b, (((1,), (0,)), ((), ())), preferred_element_type=f32)


def nt(a, b):
    return lax.dot_general(a, b, (((1,), (1,)), ((), ())), preferred_element_type=f32)


def group_of(slab, device):
    low = device % 2
    return device - low + (low + slab // 4) % 2


def owner(seq, slab):
    pair, part = slab % 4 // 2, slab % 2
    x = pair * (2 + seq) + (1 - pair) * (1 - seq)
    return {"dp": (part + pair) % 2, "blk": slab // 4 * 4 + x}


def unit(core, blk):
    x = blk % 4
    pair = x // 2
    seq = pair * (x - 2) + (1 - pair) * (1 - x)
    return seq, blk // 4 * 4 + 2 * pair + (core + pair) % 2


def wait_for(ref, sem):
    pltpu.make_async_copy(ref, ref, sem).wait()


def kernel(
    q_in,
    k_in,
    v_in,
    g_in,
    q_gain,
    k_gain,
    lists,
    counts,
    att_out,
    qgrad_out,
    kgrad_out,
    vgrad_out,
    gain_out,
    q_stage,
    k_stage,
    q_fac,
    k_fac,
    qbuf,
    gbuf,
    kbuf,
    vbuf,
    kt_buf,
    vt_buf,
    s_buf,
    p_buf,
    ds_buf,
    acc_k,
    acc_v,
    own_acc,
    edge_send,
    edge_recv,
    own_send,
    o_send,
    dq_send,
    dq_recv,
    dk_recv,
    named,
    named_here,
    bias,
    list_sem,
    gain_tab,
    gain_recv,
    gain_sem,
    in_send,
    in_recv,
    halo_send,
    halo_recv,
    edge_ssem,
    edge_rsem,
    back_send,
    back_recv,
):
    d = lax.axis_index("dp")
    b = lax.axis_index("blk")
    tile = lax.axis_index("head")
    seq, slab_here = unit(d, b)
    g = group_of(b, tile)
    has_low = slab_here > 0
    has_high = slab_here < NB - 1
    below = {**owner(seq, slab_here - 1), "head": group_of(slab_here - 1, g)}
    above = {**owner(seq, slab_here + 1), "head": group_of(slab_here + 1, g)}
    work = owner(d, b)
    lists_local = seq == d
    other_core = {"dp": 1 - d}
    my_row = tile // COLS
    my_col = tile % COLS
    gain_group = d * 4 + b // 2
    gain_self = gain_group == g
    my_rows = pl.ds(pl.multiple_of(my_row * TILE, TILE), TILE)

    barrier = pltpu.get_barrier_semaphore()

    def greet(i, carry):
        pl.semaphore_signal(barrier, inc=1, device_id={**work, "head": i})
        pl.semaphore_signal(barrier, inc=1, device_id={"dp": seq, "blk": slab_here, "head": i})
        return carry

    lax.fori_loop(0, NH, greet, 0)
    pl.semaphore_signal(barrier, inc=1, device_id=other_core)

    def gain_target(j):
        return {"dp": g // 4, "blk": 2 * (g % 4) + j // NH, "head": j % NH}

    def gain_target_is_me(j):
        return (g // 4 == d) & (2 * (g % 4) + j // NH == b) & (j % NH == tile)

    def greet_gain(j, carry):
        @pl.when(jnp.logical_not(gain_target_is_me(j)))
        def _():
            pl.semaphore_signal(barrier, inc=1, device_id=gain_target(j))

        @pl.when(jnp.logical_not((j // NB == seq) & (j % NB == slab_here) & gain_self))
        def _():
            pl.semaphore_signal(
                barrier,
                inc=1,
                device_id={**owner(j // NB, j % NB), "head": group_of(j % NB, gain_group)},
            )

        return carry

    lax.fori_loop(0, 2 * NB, greet_gain, 0)

    @pl.when(has_low)
    def _():
        pl.semaphore_signal(barrier, inc=1, device_id=below)

    @pl.when(has_high)
    def _():
        pl.semaphore_signal(barrier, inc=1, device_id=above)

    def clear_side(slab, side):
        zeros = jnp.zeros((CH, HS), bf16)

        def one(e, carry):
            h, c = e // COLS, e % COLS
            kbuf[h, c, slab] = zeros
            vbuf[h, c, slab] = zeros
            edge_recv[e, side, 0] = zeros
            edge_recv[e, side, 1] = zeros
            return carry

        lax.fori_loop(0, HPD * COLS, one, 0)

    @pl.when(jnp.logical_not(has_low))
    def _():
        clear_side(0, 0)

    @pl.when(jnp.logical_not(has_high))
    def _():
        clear_side(2, 1)

    def normalize(x_in, gain, stage, fac):
        def block(i, carry):
            rows = pl.ds(pl.multiple_of(i * ROWS, ROWS), ROWS)
            total = jnp.zeros((ROWS, HS), f32)
            for h in range(HEADS):
                x = x_in[rows, h * HS : (h + 1) * HS].astype(f32)
                total = total + x * x
            mean = jnp.sum(total, axis=1, keepdims=True) * (1.0 / F)
            factor = jnp.broadcast_to(lax.rsqrt(mean + EPSILON), (ROWS, HS))
            fac[rows, :] = factor
            for h in range(HEADS):
                x = x_in[rows, h * HS : (h + 1) * HS].astype(f32)
                stage[h, rows, :] = (x * factor * gain[:, h * HS : (h + 1) * HS]).astype(bf16)
            return carry

        lax.fori_loop(0, TILE // ROWS, block, 0)

    def send_in(h, which, src_of, dst):
        def one(i, carry):
            to = (tile + i) % NH
            pltpu.make_async_remote_copy(
                src_ref=src_of(group_of(b, to) * HPD + h),
                dst_ref=dst,
                send_sem=in_send.at[which],
                recv_sem=in_recv.at[which, h],
                device_id={**work, "head": to},
            ).start()
            return carry

        lax.fori_loop(0, NH, one, 0)

    def columns(h):
        return pl.ds(pl.multiple_of(h * HS, HS), HS)

    def send_k(h):
        send_in(h, 0, lambda n: k_stage.at[n], kbuf.at[h, my_col, 1, my_rows])

    def send_v(h):
        send_in(h, 1, lambda n: v_in.at[:, columns(n)], vbuf.at[h, my_col, 1, my_rows])

    def send_q(h):
        send_in(h, 2, lambda n: q_stage.at[n], qbuf.at[h, my_col, my_rows])

    def send_g(h):
        send_in(h, 3, lambda n: g_in.at[:, columns(n)], gbuf.at[h, my_col, my_rows])

    tiles = NB * 8
    sublane = lax.broadcasted_iota(jnp.int32, (tiles, tiles), 0)
    lane = lax.broadcasted_iota(jnp.int32, (tiles, tiles), 1)
    live = jnp.where(sublane == lane, counts[...], 0).astype(f32)
    live = jnp.sum(live, axis=1, keepdims=True)
    slot = lax.broadcasted_iota(jnp.int32, (tiles, KMAX), 1).astype(f32)
    named[...] = jnp.full((tiles, HS), NOWHERE, jnp.int32)
    named[:, 0:KMAX] = jnp.where(slot < live, lists[...], NOWHERE)

    def list_copy():
        slab = unit(1 - d, b)[1]
        return pltpu.make_async_remote_copy(
            src_ref=named.at[pl.ds(pl.multiple_of(slab * 8, 8), 8)],
            dst_ref=named_here,
            send_sem=list_sem.at[0],
            recv_sem=list_sem.at[1],
            device_id=other_core,
        )

    def build_bias():
        @pl.when(lists_local)
        def _():
            named_here[...] = named[pl.ds(pl.multiple_of(slab_here * 8, 8), 8), :]

        @pl.when(jnp.logical_not(lists_local))
        def _():
            list_copy().wait_recv()

        found = (named_here[...] - (slab_here - 1) * 8).astype(f32)
        first_row = lax.broadcasted_iota(jnp.int32, (1, CH), 1) < TILE
        for near in range(24):
            hit = jnp.max(jnp.where(found == near, 1.0, 0.0), axis=1, keepdims=True)
            away = jnp.broadcast_to(jnp.where(hit > 0.5, 0.0, FAR), (8, CH))
            slab, row, col = near // 8, near // COLS % 2, near % COLS
            for c in range(COLS):
                bias[c * 12 + col * 3 + slab, row : row + 1, :] = jnp.where(
                    first_row, away[c : c + 1], away[COLS + c : COLS + c + 1]
                )

    normalize(k_in, k_gain, k_stage, k_fac)
    pl.semaphore_wait(
        barrier,
        2 * NH
        + 1
        + 4 * NB
        - 2 * gain_self.astype(jnp.int32)
        + has_low.astype(jnp.int32)
        + has_high.astype(jnp.int32),
    )
    @pl.when(lists_local)
    def _():
        list_copy().start()

    send_v(0)
    send_k(0)
    send_g(0)
    normalize(q_in, q_gain, q_stage, q_fac)
    send_q(0)
    build_bias()

    def halo_copy(h, c, which, up):
        buf = (kbuf, vbuf)[which]
        side = 0 if up else 1
        return pltpu.make_async_remote_copy(
            src_ref=buf.at[h, c, 1],
            dst_ref=buf.at[h, c, 0 if up else 2],
            send_sem=halo_send.at[h * COLS + c, which, side],
            recv_sem=halo_recv.at[h * COLS + c, which, side],
            device_id=above if up else below,
        )

    def forward(h):
        wait_for(kbuf.at[h, :, 1], in_recv.at[0, h])
        wait_for(vbuf.at[h, :, 1], in_recv.at[1, h])

        def one(c, carry):
            for which in range(2):

                @pl.when(has_high)
                def _():
                    halo_copy(h, c, which, True).start()

                @pl.when(has_low)
                def _():
                    halo_copy(h, c, which, False).start()

            return carry

        lax.fori_loop(0, COLS, one, 0)

    def await_halo(h, c):
        for which in range(2):

            @pl.when(has_low)
            def _():
                halo_copy(h, c, which, True).wait_recv()

            @pl.when(has_high)
            def _():
                halo_copy(h, c, which, False).wait_recv()

    def send_back(which, src, dst, t):
        pltpu.make_async_remote_copy(
            src_ref=src,
            dst_ref=dst,
            send_sem=back_send.at[which],
            recv_sem=back_recv.at[which],
            device_id={"dp": seq, "blk": slab_here, "head": t},
        ).start()

    def attend(h, c):
        low = jnp.maximum(c - 1, 0)
        high = jnp.minimum(c + 2, COLS)
        q = qbuf[h, c]

        def first(k, top):
            for slab in range(3):
                s = nt(kbuf[h, k, slab], q)
                s_buf[k - low, slab] = s
                away = bias[c * 12 + k * 3 + slab]
                top = jnp.maximum(top, jnp.max(s[:TILE], axis=0, keepdims=True) + away[0:1])
                top = jnp.maximum(top, jnp.max(s[TILE:], axis=0, keepdims=True) + away[1:2])
            return top

        top = lax.fori_loop(low, high, first, jnp.full((1, CH), 2 * FAR, f32)) * SCALE2

        def second(k, carry):
            total, out = carry
            for slab in range(3):
                away = bias[c * 12 + k * 3 + slab]
                s = s_buf[k - low, slab]
                e0 = jnp.exp2(s[:TILE] * SCALE2 - (top - away[0:1]))
                e1 = jnp.exp2(s[TILE:] * SCALE2 - (top - away[1:2]))
                total = total + jnp.sum(e0, axis=0, keepdims=True)
                total = total + jnp.sum(e1, axis=0, keepdims=True)
                p_buf[k - low, slab * CH : slab * CH + TILE] = e0.astype(bf16)
                p_buf[k - low, slab * CH + TILE : (slab + 1) * CH] = e1.astype(bf16)
            return total, out + nn(vt_buf[k], p_buf[k - low])

        total, out = lax.fori_loop(
            low, high, second, (jnp.zeros((1, CH), f32), jnp.zeros((HS, CH), f32))
        )
        inverse = 1.0 / total
        out = out * inverse
        o_send[h, c] = out.T.astype(bf16)
        grad = gbuf[h, c].astype(f32).T
        delta = jnp.sum(out * grad, axis=0, keepdims=True) * inverse
        grad = grad * inverse
        grad_t = grad.astype(bf16)
        grad_s = grad.T.astype(bf16)

        def third(k, dq):
            for slab in range(3):
                e = p_buf[k - low, slab * CH : (slab + 1) * CH]
                dp = nn(vbuf[h, k, slab], grad_t)
                ds = (e.astype(f32) * (dp - delta)).astype(bf16)
                ds_buf[slab * CH : (slab + 1) * CH] = ds
                acc_v[k * 3 + slab] += nn(e, grad_s)
                acc_k[k * 3 + slab] += nn(ds, q)
            return dq + nn(kt_buf[k], ds_buf[...])

        dq = lax.fori_loop(low, high, third, jnp.zeros((HS, CH), f32))
        dq = (dq * SCALE).T.astype(bf16)
        dq_send[h, c] = dq
        gain_tab[h, 0:1, :] += jnp.sum(dq.astype(f32) * q.astype(f32), axis=0, keepdims=True)
        for r in range(2):
            rows = pl.ds(r * TILE, TILE)
            t = r * COLS + c
            send_back(0, o_send.at[h, c, rows], att_out.at[:, columns(g * HPD + h)], t)
            send_back(1, dq_send.at[h, c, rows], dq_recv.at[g * HPD + h], t)

    def edge_copy(e, up):
        return pltpu.make_async_remote_copy(
            src_ref=edge_send.at[e, 1 if up else 0],
            dst_ref=edge_recv.at[e, 0 if up else 1],
            send_sem=edge_ssem.at[e, 1 if up else 0],
            recv_sem=edge_rsem.at[e, 0 if up else 1],
            device_id=above if up else below,
        )

    def finish(h, c):
        e = h * COLS + c
        for side, slab in ((0, 0), (1, 2)):
            edge_send[e, side, 0] = (acc_k[c * 3 + slab] * SCALE).astype(bf16)
            edge_send[e, side, 1] = acc_v[c * 3 + slab].astype(bf16)
        own_acc[e, 0] = acc_k[c * 3 + 1] * SCALE
        own_acc[e, 1] = acc_v[c * 3 + 1]

        @pl.when(has_high)
        def _():
            edge_copy(e, True).start()

        @pl.when(has_low)
        def _():
            edge_copy(e, False).start()

    def settle(e):
        h, c = e // COLS, e % COLS

        @pl.when(has_low)
        def _():
            edge_copy(e, True).wait_recv()

        @pl.when(has_high)
        def _():
            edge_copy(e, False).wait_recv()

        for a in range(2):
            own_send[e, a] = (
                own_acc[e, a] + edge_recv[e, 0, a].astype(f32) + edge_recv[e, 1, a].astype(f32)
            ).astype(bf16)
        product = own_send[e, 0].astype(f32) * kbuf[h, c, 1].astype(f32)
        gain_tab[h, 1:2, :] += jnp.sum(product, axis=0, keepdims=True)
        for r in range(2):
            rows = pl.ds(r * TILE, TILE)
            t = r * COLS + c
            send_back(2, own_send.at[e, 0, rows], dk_recv.at[g * HPD + h], t)
            send_back(3, own_send.at[e, 1, rows], vgrad_out.at[:, columns(g * HPD + h)], t)

    def start_column(h, k):
        await_halo(h, k)
        for slab in range(3):
            keys = slice(slab * CH, (slab + 1) * CH)
            kt_buf[k, :, keys] = kbuf[h, k, slab].T
            vt_buf[k, :, keys] = vbuf[h, k, slab].T
            acc_k[k * 3 + slab] = jnp.zeros((CH, HS), f32)
            acc_v[k * 3 + slab] = jnp.zeros((CH, HS), f32)

    gain_tab[...] = jnp.zeros_like(gain_tab)
    forward(0)

    def rest(h, carry):
        send_k(h)
        send_v(h)
        send_q(h)
        send_g(h)
        return carry

    lax.fori_loop(1, HPD, rest, 0)

    def step(s, carry):
        h, c = s // COLS, s % COLS

        @pl.when(c == 0)
        def _():
            start_column(h, 0)

            @pl.when(h < HPD - 1)
            def _():
                forward(h + 1)

            wait_for(qbuf.at[h], in_recv.at[2, h])
            wait_for(gbuf.at[h], in_recv.at[3, h])

        @pl.when(c < COLS - 1)
        def _():
            start_column(h, c + 1)

        attend(h, c)

        @pl.when(c > 0)
        def _():
            finish(h, c - 1)

        @pl.when(c == COLS - 1)
        def _():
            finish(h, COLS - 1)

        @pl.when(s >= LAG)
        def _():
            settle(s - LAG)

        return carry

    lax.fori_loop(0, HPD * COLS, step, 0)

    def last(e, carry):
        settle(e)
        return carry

    lax.fori_loop(HPD * COLS - LAG, HPD * COLS, last, 0)

    for h in range(HPD):
        for row, gain in ((0, q_gain), (1, k_gain)):
            gain_tab[h, row : row + 1, :] = gain_tab[h, row : row + 1, :] / gain[:, columns(g * HPD + h)]

    def give(j, carry):
        dst = gain_recv.at[seq * NB + slab_here]
        me = gain_target_is_me(j)

        @pl.when(me)
        def _():
            pltpu.make_async_copy(gain_tab, dst, gain_sem.at[1]).start()

        @pl.when(jnp.logical_not(me))
        def _():
            pltpu.make_async_remote_copy(
                src_ref=gain_tab,
                dst_ref=dst,
                send_sem=gain_sem.at[0],
                recv_sem=gain_sem.at[1],
                device_id=gain_target(j),
            ).start()

        return carry

    lax.fori_loop(0, 2 * NB, give, 0)

    def norm_back(x_in, gain, fac, d_recv, grad_out):
        def block(i, carry):
            rows = pl.ds(pl.multiple_of(i * ROWS, ROWS), ROWS)
            factor = fac[rows, :]
            total = jnp.zeros((ROWS, HS), f32)
            for h in range(HEADS):
                lanes = slice(h * HS, (h + 1) * HS)
                hat = x_in[rows, lanes].astype(f32) * factor
                product = d_recv[h, rows, :].astype(f32) * hat
                total = total + product * gain[:, lanes]
            inner = jnp.sum(total, axis=1, keepdims=True) * (1.0 / F)
            for h in range(HEADS):
                lanes = slice(h * HS, (h + 1) * HS)
                hat = x_in[rows, lanes].astype(f32) * factor
                scaled = d_recv[h, rows, :].astype(f32) * gain[:, lanes]
                grad_out[rows, lanes] = (factor * (scaled - hat * inner)).astype(bf16)
            return carry

        lax.fori_loop(0, TILE // ROWS, block, 0)

    wait_for(dq_recv, back_recv.at[1])
    norm_back(q_in, q_gain, q_fac, dq_recv, qgrad_out)
    wait_for(dk_recv, back_recv.at[2])
    norm_back(k_in, k_gain, k_fac, dk_recv, kgrad_out)
    wait_for(gain_recv, gain_sem.at[1])
    start = 24 * ((b % 2) * NH + tile)
    lane = lax.broadcasted_iota(jnp.int32, (HS, HS), 1)
    source = lax.broadcasted_iota(jnp.int32, (HS, HS), 0)
    sums = jnp.zeros((8, HS), f32)
    for h in range(HPD):
        pick = ((source + h * HS == lane + start) & (lane < 24)).astype(f32)
        part = gain_recv[0, h]
        for i in range(1, 2 * NB):
            part = part + gain_recv[i, h]
        sums = sums + jnp.dot(
            part, pick, precision=lax.Precision.HIGHEST, preferred_element_type=f32
        )
    gain_out[...] = sums
    wait_for(att_out, back_recv.at[0])
    wait_for(vgrad_out, back_recv.at[3])

    wait_for(gain_recv.at[0 : 2 * NB - 1], gain_sem.at[0])

    @pl.when(jnp.logical_not(gain_self))
    def _():
        wait_for(gain_recv.at[0], gain_sem.at[0])

    for which in range(4):
        wait_for(dq_recv, in_send.at[which])
        wait_for(dq_recv, back_send.at[which])

    @pl.when(lists_local)
    def _():
        list_copy().wait_send()

    def drain_edges(e, carry):
        for which in range(2):

            @pl.when(has_high)
            def _():
                halo_copy(e // COLS, e % COLS, which, True).wait_send()

            @pl.when(has_low)
            def _():
                halo_copy(e // COLS, e % COLS, which, False).wait_send()

        @pl.when(has_high)
        def _():
            edge_copy(e, True).wait_send()

        @pl.when(has_low)
        def _():
            edge_copy(e, False).wait_send()

        return carry

    lax.fori_loop(0, HPD * COLS, drain_edges, 0)


def shards(
    query_input, key_input, value_input, output_grad, query_gain, key_gain, tile_lists, tile_counts
):
    vmem = pl.BlockSpec(memory_space=pltpu.VMEM)
    anywhere = pl.BlockSpec(memory_space=pl.ANY)
    token = jax.ShapeDtypeStruct((TILE, F), bf16)
    n = HPD * COLS
    attention, query_grad, key_grad, value_grad, gains = pl.pallas_call(
        kernel,
        name="tiles",
        out_shape=(token, token, token, token, jax.ShapeDtypeStruct((8, HS), f32)),
        in_specs=[vmem] * 8,
        out_specs=(anywhere, vmem, vmem, anywhere, vmem),
        scratch_shapes=[
            pltpu.VMEM((HEADS, TILE, HS), bf16),
            pltpu.VMEM((HEADS, TILE, HS), bf16),
            pltpu.VMEM((TILE, HS), f32),
            pltpu.VMEM((TILE, HS), f32),
            pltpu.VMEM((HPD, COLS, CH, HS), bf16),
            pltpu.VMEM((HPD, COLS, CH, HS), bf16),
            pltpu.VMEM((HPD, COLS, 3, CH, HS), bf16),
            pltpu.VMEM((HPD, COLS, 3, CH, HS), bf16),
            pltpu.VMEM((COLS, HS, 3 * CH), bf16),
            pltpu.VMEM((COLS, HS, 3 * CH), bf16),
            pltpu.VMEM((3, 3, CH, CH), f32),
            pltpu.VMEM((3, 3 * CH, CH), bf16),
            pltpu.VMEM((3 * CH, CH), bf16),
            pltpu.VMEM((12, CH, HS), f32),
            pltpu.VMEM((12, CH, HS), f32),
            pltpu.VMEM((n, 2, CH, HS), f32),
            pltpu.VMEM((n, 2, 2, CH, HS), bf16),
            pltpu.VMEM((n, 2, 2, CH, HS), bf16),
            pltpu.VMEM((n, 2, CH, HS), bf16),
            pltpu.VMEM((HPD, COLS, CH, HS), bf16),
            pltpu.VMEM((HPD, COLS, CH, HS), bf16),
            pltpu.VMEM((HEADS, TILE, HS), bf16),
            pltpu.VMEM((HEADS, TILE, HS), bf16),
            pltpu.VMEM((NB * 8, HS), jnp.int32),
            pltpu.VMEM((8, HS), jnp.int32),
            pltpu.VMEM((12 * COLS, 2, CH), f32),
            pltpu.SemaphoreType.DMA((2,)),
            pltpu.VMEM((HPD, 8, HS), f32),
            pltpu.VMEM((2 * NB, HPD, 8, HS), f32),
            pltpu.SemaphoreType.DMA((2,)),
            pltpu.SemaphoreType.DMA((4,)),
            pltpu.SemaphoreType.DMA((4, HPD)),
            pltpu.SemaphoreType.DMA((n, 2, 2)),
            pltpu.SemaphoreType.DMA((n, 2, 2)),
            pltpu.SemaphoreType.DMA((n, 2)),
            pltpu.SemaphoreType.DMA((n, 2)),
            pltpu.SemaphoreType.DMA((4,)),
            pltpu.SemaphoreType.DMA((4,)),
        ],
        compiler_params=pltpu.CompilerParams(
            collective_id=0, has_side_effects=True, vmem_limit_bytes=62 * 1024 * 1024
        ),
    )(
        query_input[0],
        key_input[0],
        value_input[0],
        output_grad[0],
        query_gain[None],
        key_gain[None],
        tile_lists[0],
        tile_counts,
    )
    width = F // (2 * NB * NH)
    return (
        attention[None],
        query_grad[None],
        key_grad[None],
        value_grad[None],
        gains[0, :width],
        gains[1, :width],
    )


def solution(mesh):
    tokens = P("dp", ("blk", "head"), None)
    features = P(("dp", "blk", "head"))
    return jax.shard_map(
        shards,
        mesh=mesh,
        in_specs=(tokens, tokens, tokens, tokens, P(), P(), P("dp", None, None), P("dp", None)),
        out_specs=(tokens, tokens, tokens, tokens, features, features),
        check_vma=False,
    )
```

```python
import functools

import jax
import jax.numpy as jnp
from jax import lax
from jax.experimental import pallas as pl
from jax.experimental.pallas import tpu as pltpu
from jax.sharding import PartitionSpec as P

HS = 128
TILE = 192
KMAX = 12
HEADS = 24
HPD = 3
COLS = 4
NB = 8
NH = 8
F = HEADS * HS
CH = 2 * TILE
ROWS = 16
BLOCK = 64
WIDTH = 24
LAG = 3
EPSILON = 1e-06
SCALE = HS**-0.5
SCALE2 = SCALE * 1.4426950408889634
FAR = -1e30
NOWHERE = -1000.0
f32 = jnp.float32
bf16 = jnp.bfloat16


def nn(a, b):
    return lax.dot_general(a, b, (((1,), (0,)), ((), ())), preferred_element_type=f32)


def nt(a, b):
    return lax.dot_general(a, b, (((1,), (1,)), ((), ())), preferred_element_type=f32)


def group_of(slab, device):
    low = device % 2
    return device - low + (low + slab // 4) % 2


def owner(seq, slab):
    pair, part = slab % 4 // 2, slab % 2
    x = pair * (2 + seq) + (1 - pair) * (1 - seq)
    return {"dp": (part + pair) % 2, "blk": slab // 4 * 4 + x}


def unit(core, blk):
    x = blk % 4
    pair = x // 2
    seq = pair * (x - 2) + (1 - pair) * (1 - x)
    return seq, blk // 4 * 4 + 2 * pair + (core + pair) % 2


def wait_for(ref, sem):
    pltpu.make_async_copy(ref, ref, sem).wait()


def kernel(
    q_in,
    k_in,
    v_in,
    g_in,
    q_gain,
    k_gain,
    lists,
    counts,
    att_out,
    dq_recv,
    dk_recv,
    vgrad_out,
    gain_out,
    q_tokens,
    k_tokens,
    token_sem,
    q_stage,
    k_stage,
    qbuf,
    gbuf,
    kbuf,
    vbuf,
    kt_buf,
    vt_buf,
    s_buf,
    p_buf,
    ds_buf,
    acc_k,
    acc_v,
    own_acc,
    edge_send,
    edge_recv,
    own_send,
    o_send,
    dq_send,
    slots,
    named,
    named_here,
    bias,
    list_sem,
    gain_tab,
    gain_recv,
    gain_sem,
    in_send,
    in_recv,
    halo_send,
    halo_recv,
    edge_ssem,
    edge_rsem,
    back_send,
    back_recv,
):
    d = lax.axis_index("dp")
    b = lax.axis_index("blk")
    tile = lax.axis_index("head")
    seq, slab_here = unit(d, b)
    g = group_of(b, tile)
    has_low = slab_here > 0
    has_high = slab_here < NB - 1
    below = {**owner(seq, slab_here - 1), "head": group_of(slab_here - 1, g)}
    above = {**owner(seq, slab_here + 1), "head": group_of(slab_here + 1, g)}
    work = owner(d, b)
    lists_local = seq == d
    other_core = {"dp": 1 - d}
    my_row = tile // COLS
    my_col = tile % COLS
    gain_group = d * 4 + b // 2
    gain_self = gain_group == g
    my_rows = pl.ds(pl.multiple_of(my_row * TILE, TILE), TILE)

    barrier = pltpu.get_barrier_semaphore()

    def greet(i, carry):
        pl.semaphore_signal(barrier, inc=1, device_id={**work, "head": i})
        pl.semaphore_signal(barrier, inc=1, device_id={"dp": seq, "blk": slab_here, "head": i})
        return carry

    lax.fori_loop(0, NH, greet, 0)
    pl.semaphore_signal(barrier, inc=1, device_id=other_core)

    def gain_target(j):
        return {"dp": g // 4, "blk": 2 * (g % 4) + j // NH, "head": j % NH}

    def gain_target_is_me(j):
        return (g // 4 == d) & (2 * (g % 4) + j // NH == b) & (j % NH == tile)

    def greet_gain(j, carry):
        @pl.when(jnp.logical_not(gain_target_is_me(j)))
        def _():
            pl.semaphore_signal(barrier, inc=1, device_id=gain_target(j))

        @pl.when(jnp.logical_not((j // NB == seq) & (j % NB == slab_here) & gain_self))
        def _():
            pl.semaphore_signal(
                barrier,
                inc=1,
                device_id={**owner(j // NB, j % NB), "head": group_of(j % NB, gain_group)},
            )

        return carry

    lax.fori_loop(0, 2 * NB, greet_gain, 0)

    @pl.when(has_low)
    def _():
        pl.semaphore_signal(barrier, inc=1, device_id=below)

    @pl.when(has_high)
    def _():
        pl.semaphore_signal(barrier, inc=1, device_id=above)

    def clear_side(slab, side):
        zeros = jnp.zeros((CH, HS), bf16)

        def one(e, carry):
            h, c = e // COLS, e % COLS
            kbuf[h, c, slab] = zeros
            vbuf[h, c, slab] = zeros
            edge_recv[e, side, 0] = zeros
            edge_recv[e, side, 1] = zeros
            return carry

        lax.fori_loop(0, HPD * COLS, one, 0)

    @pl.when(jnp.logical_not(has_low))
    def _():
        clear_side(0, 0)

    @pl.when(jnp.logical_not(has_high))
    def _():
        clear_side(2, 1)

    for which, (src, dst) in enumerate(((k_in, k_tokens), (q_in, q_tokens))):
        pltpu.make_async_copy(src, dst, token_sem.at[which]).start()

    def normalize(x_in, gain, stage):
        def block(i, carry):
            rows = pl.ds(pl.multiple_of(i * ROWS, ROWS), ROWS)
            total = jnp.zeros((ROWS, HS), f32)
            for h in range(HEADS):
                x = x_in[rows, h * HS : (h + 1) * HS].astype(f32)
                total = total + x * x
            mean = jnp.sum(total, axis=1, keepdims=True) * (1.0 / F)
            factor = jnp.broadcast_to(lax.rsqrt(mean + EPSILON), (ROWS, HS))
            for h in range(HEADS):
                x = x_in[rows, h * HS : (h + 1) * HS].astype(f32)
                stage[h, rows, :] = (x * factor * gain[:, h * HS : (h + 1) * HS]).astype(bf16)
            return carry

        lax.fori_loop(0, TILE // ROWS, block, 0)

    def send_in(h, which, src_of, dst):
        def one(i, carry):
            to = (tile + i) % NH
            pltpu.make_async_remote_copy(
                src_ref=src_of(group_of(b, to) * HPD + h),
                dst_ref=dst,
                send_sem=in_send.at[which],
                recv_sem=in_recv.at[which, h],
                device_id={**work, "head": to},
            ).start()
            return carry

        lax.fori_loop(0, NH, one, 0)

    def columns(h):
        return pl.ds(pl.multiple_of(h * HS, HS), HS)

    def send_k(h):
        send_in(h, 0, lambda n: k_stage.at[n], kbuf.at[h, my_col, 1, my_rows])

    def send_v(h):
        send_in(h, 1, lambda n: v_in.at[:, columns(n)], vbuf.at[h, my_col, 1, my_rows])

    def send_q(h):
        send_in(h, 2, lambda n: q_stage.at[n], qbuf.at[h, my_col, my_rows])

    def send_g(h):
        send_in(h, 3, lambda n: g_in.at[:, columns(n)], gbuf.at[h, my_col, my_rows])

    tiles = NB * 8
    slot = lax.broadcasted_iota(jnp.int32, (KMAX, tiles), 0)
    slots[...] = jnp.full((HS, HS), NOWHERE, f32)
    slots[0:KMAX, 0:tiles] = jnp.where(slot < counts[...], lists[:, 0, :], NOWHERE).astype(f32)
    named[...] = slots[...].T

    def list_copy():
        slab = unit(1 - d, b)[1]
        return pltpu.make_async_remote_copy(
            src_ref=named.at[pl.ds(pl.multiple_of(slab * 8, 8), 8)],
            dst_ref=named_here,
            send_sem=list_sem.at[0],
            recv_sem=list_sem.at[1],
            device_id=other_core,
        )

    def build_bias():
        @pl.when(lists_local)
        def _():
            named_here[...] = named[pl.ds(pl.multiple_of(slab_here * 8, 8), 8), :]

        @pl.when(jnp.logical_not(lists_local))
        def _():
            list_copy().wait_recv()

        found = named_here[...] - ((slab_here - 1) * 8).astype(f32)
        first_row = lax.broadcasted_iota(jnp.int32, (1, CH), 1) < TILE
        for near in range(24):
            hit = jnp.max(jnp.where(found == near, 1.0, 0.0), axis=1, keepdims=True)
            away = jnp.broadcast_to(jnp.where(hit > 0.5, 0.0, FAR), (8, CH))
            slab, row, col = near // 8, near // COLS % 2, near % COLS
            for c in range(COLS):
                bias[c * 12 + col * 3 + slab, row : row + 1, :] = jnp.where(
                    first_row, away[c : c + 1], away[COLS + c : COLS + c + 1]
                )

    wait_for(k_tokens, token_sem.at[0])
    normalize(k_tokens, k_gain, k_stage)
    pl.semaphore_wait(
        barrier,
        2 * NH
        + 1
        + 4 * NB
        - 2 * gain_self.astype(jnp.int32)
        + has_low.astype(jnp.int32)
        + has_high.astype(jnp.int32),
    )
    @pl.when(lists_local)
    def _():
        list_copy().start()

    send_v(0)
    send_k(0)
    send_g(0)
    wait_for(q_tokens, token_sem.at[1])
    normalize(q_tokens, q_gain, q_stage)
    send_q(0)
    build_bias()

    def halo_copy(h, c, which, up):
        buf = (kbuf, vbuf)[which]
        side = 0 if up else 1
        return pltpu.make_async_remote_copy(
            src_ref=buf.at[h, c, 1],
            dst_ref=buf.at[h, c, 0 if up else 2],
            send_sem=halo_send.at[h * COLS + c, which, side],
            recv_sem=halo_recv.at[h * COLS + c, which, side],
            device_id=above if up else below,
        )

    def forward(h):
        wait_for(kbuf.at[h, :, 1], in_recv.at[0, h])
        wait_for(vbuf.at[h, :, 1], in_recv.at[1, h])

        def one(c, carry):
            for which in range(2):

                @pl.when(has_high)
                def _():
                    halo_copy(h, c, which, True).start()

                @pl.when(has_low)
                def _():
                    halo_copy(h, c, which, False).start()

            return carry

        lax.fori_loop(0, COLS, one, 0)

    def await_halo(h, c):
        for which in range(2):

            @pl.when(has_low)
            def _():
                halo_copy(h, c, which, True).wait_recv()

            @pl.when(has_high)
            def _():
                halo_copy(h, c, which, False).wait_recv()

    def send_back(which, src, dst, t):
        pltpu.make_async_remote_copy(
            src_ref=src,
            dst_ref=dst,
            send_sem=back_send.at[which],
            recv_sem=back_recv.at[which],
            device_id={"dp": seq, "blk": slab_here, "head": t},
        ).start()

    def attend(h, c):
        low = jnp.maximum(c - 1, 0)
        high = jnp.minimum(c + 2, COLS)
        q = qbuf[h, c]

        def first(k, top):
            for slab in range(3):
                s = nt(kbuf[h, k, slab], q)
                s_buf[k - low, slab] = s
                away = bias[c * 12 + k * 3 + slab]
                top = jnp.maximum(top, jnp.max(s[:TILE], axis=0, keepdims=True) + away[0:1])
                top = jnp.maximum(top, jnp.max(s[TILE:], axis=0, keepdims=True) + away[1:2])
            return top

        top = lax.fori_loop(low, high, first, jnp.full((1, CH), 2 * FAR, f32)) * SCALE2

        def second(k, carry):
            total, out = carry
            for slab in range(3):
                away = bias[c * 12 + k * 3 + slab]
                s = s_buf[k - low, slab]
                e0 = jnp.exp2(s[:TILE] * SCALE2 - (top - away[0:1]))
                e1 = jnp.exp2(s[TILE:] * SCALE2 - (top - away[1:2]))
                total = total + jnp.sum(e0, axis=0, keepdims=True)
                total = total + jnp.sum(e1, axis=0, keepdims=True)
                p_buf[k - low, slab * CH : slab * CH + TILE] = e0.astype(bf16)
                p_buf[k - low, slab * CH + TILE : (slab + 1) * CH] = e1.astype(bf16)
            return total, out + nn(vt_buf[k], p_buf[k - low])

        total, out = lax.fori_loop(
            low, high, second, (jnp.zeros((1, CH), f32), jnp.zeros((HS, CH), f32))
        )
        inverse = 1.0 / total
        out = out * inverse
        o_send[h, c] = out.T.astype(bf16)
        grad = gbuf[h, c].astype(f32).T
        delta = jnp.sum(out * grad, axis=0, keepdims=True) * inverse
        grad = grad * inverse
        grad_t = grad.astype(bf16)
        grad_s = grad.T.astype(bf16)

        def third(k, dq):
            for slab in range(3):
                e = p_buf[k - low, slab * CH : (slab + 1) * CH]
                dp = nn(vbuf[h, k, slab], grad_t)
                ds = (e.astype(f32) * (dp - delta)).astype(bf16)
                ds_buf[slab * CH : (slab + 1) * CH] = ds
                acc_v[k * 3 + slab] += nn(e, grad_s)
                acc_k[k * 3 + slab] += nn(ds, q)
            return dq + nn(kt_buf[k], ds_buf[...])

        dq = lax.fori_loop(low, high, third, jnp.zeros((HS, CH), f32))
        dq = (dq * SCALE).T.astype(bf16)
        dq_send[h, c] = dq
        gain_tab[h, 0:1, :] += jnp.sum(dq.astype(f32) * q.astype(f32), axis=0, keepdims=True)
        for r in range(2):
            rows = pl.ds(r * TILE, TILE)
            t = r * COLS + c
            send_back(0, o_send.at[h, c, rows], att_out.at[:, columns(g * HPD + h)], t)
            send_back(1, dq_send.at[h, c, rows], dq_recv.at[g * HPD + h], t)

    def edge_copy(e, up):
        return pltpu.make_async_remote_copy(
            src_ref=edge_send.at[e, 1 if up else 0],
            dst_ref=edge_recv.at[e, 0 if up else 1],
            send_sem=edge_ssem.at[e, 1 if up else 0],
            recv_sem=edge_rsem.at[e, 0 if up else 1],
            device_id=above if up else below,
        )

    def finish(h, c):
        e = h * COLS + c
        for side, slab in ((0, 0), (1, 2)):
            edge_send[e, side, 0] = (acc_k[c * 3 + slab] * SCALE).astype(bf16)
            edge_send[e, side, 1] = acc_v[c * 3 + slab].astype(bf16)
        own_acc[e, 0] = acc_k[c * 3 + 1] * SCALE
        own_acc[e, 1] = acc_v[c * 3 + 1]

        @pl.when(has_high)
        def _():
            edge_copy(e, True).start()

        @pl.when(has_low)
        def _():
            edge_copy(e, False).start()

    def settle(e):
        h, c = e // COLS, e % COLS

        @pl.when(has_low)
        def _():
            edge_copy(e, True).wait_recv()

        @pl.when(has_high)
        def _():
            edge_copy(e, False).wait_recv()

        for a in range(2):
            own_send[e, a] = (
                own_acc[e, a] + edge_recv[e, 0, a].astype(f32) + edge_recv[e, 1, a].astype(f32)
            ).astype(bf16)
        product = own_send[e, 0].astype(f32) * kbuf[h, c, 1].astype(f32)
        gain_tab[h, 1:2, :] += jnp.sum(product, axis=0, keepdims=True)
        for r in range(2):
            rows = pl.ds(r * TILE, TILE)
            t = r * COLS + c
            send_back(2, own_send.at[e, 0, rows], dk_recv.at[g * HPD + h], t)
            send_back(3, own_send.at[e, 1, rows], vgrad_out.at[:, columns(g * HPD + h)], t)

    def start_column(h, k):
        await_halo(h, k)
        for slab in range(3):
            keys = slice(slab * CH, (slab + 1) * CH)
            kt_buf[k, :, keys] = kbuf[h, k, slab].T
            vt_buf[k, :, keys] = vbuf[h, k, slab].T
            acc_k[k * 3 + slab] = jnp.zeros((CH, HS), f32)
            acc_v[k * 3 + slab] = jnp.zeros((CH, HS), f32)

    gain_tab[...] = jnp.zeros_like(gain_tab)
    forward(0)

    def rest(h, carry):
        send_k(h)
        send_v(h)
        send_q(h)
        send_g(h)
        return carry

    lax.fori_loop(1, HPD, rest, 0)

    def step(s, carry):
        h, c = s // COLS, s % COLS

        @pl.when(c == 0)
        def _():
            start_column(h, 0)

            @pl.when(h < HPD - 1)
            def _():
                forward(h + 1)

            wait_for(qbuf.at[h], in_recv.at[2, h])
            wait_for(gbuf.at[h], in_recv.at[3, h])

        @pl.when(c < COLS - 1)
        def _():
            start_column(h, c + 1)

        attend(h, c)

        @pl.when(c > 0)
        def _():
            finish(h, c - 1)

        @pl.when(c == COLS - 1)
        def _():
            finish(h, COLS - 1)

        @pl.when(s >= LAG)
        def _():
            settle(s - LAG)

        return carry

    lax.fori_loop(0, HPD * COLS, step, 0)

    def last(e, carry):
        settle(e)
        return carry

    lax.fori_loop(HPD * COLS - LAG, HPD * COLS, last, 0)

    for h in range(HPD):
        for row, gain in ((0, q_gain), (1, k_gain)):
            gain_tab[h, row : row + 1, :] = gain_tab[h, row : row + 1, :] / gain[:, columns(g * HPD + h)]

    def give(j, carry):
        dst = gain_recv.at[seq * NB + slab_here]
        me = gain_target_is_me(j)

        @pl.when(me)
        def _():
            pltpu.make_async_copy(gain_tab, dst, gain_sem.at[1]).start()

        @pl.when(jnp.logical_not(me))
        def _():
            pltpu.make_async_remote_copy(
                src_ref=gain_tab,
                dst_ref=dst,
                send_sem=gain_sem.at[0],
                recv_sem=gain_sem.at[1],
                device_id=gain_target(j),
            ).start()

        return carry

    lax.fori_loop(0, 2 * NB, give, 0)

    wait_for(gain_recv, gain_sem.at[1])
    start = 24 * ((b % 2) * NH + tile)
    lane = lax.broadcasted_iota(jnp.int32, (HS, HS), 1)
    source = lax.broadcasted_iota(jnp.int32, (HS, HS), 0)
    sums = jnp.zeros((8, HS), f32)
    for h in range(HPD):
        pick = ((source + h * HS == lane + start) & (lane < 24)).astype(f32)
        part = gain_recv[0, h]
        for i in range(1, 2 * NB):
            part = part + gain_recv[i, h]
        sums = sums + jnp.dot(
            part, pick, precision=lax.Precision.HIGHEST, preferred_element_type=f32
        )
    gain_out[...] = sums
    wait_for(att_out, back_recv.at[0])
    wait_for(dq_recv, back_recv.at[1])
    wait_for(dk_recv, back_recv.at[2])
    wait_for(vgrad_out, back_recv.at[3])

    wait_for(gain_recv.at[0 : 2 * NB - 1], gain_sem.at[0])

    @pl.when(jnp.logical_not(gain_self))
    def _():
        wait_for(gain_recv.at[0], gain_sem.at[0])

    for which in range(4):
        wait_for(dq_recv, in_send.at[which])
        wait_for(dq_recv, back_send.at[which])

    @pl.when(lists_local)
    def _():
        list_copy().wait_send()

    def drain_edges(e, carry):
        for which in range(2):

            @pl.when(has_high)
            def _():
                halo_copy(e // COLS, e % COLS, which, True).wait_send()

            @pl.when(has_low)
            def _():
                halo_copy(e // COLS, e % COLS, which, False).wait_send()

        @pl.when(has_high)
        def _():
            edge_copy(e, True).wait_send()

        @pl.when(has_low)
        def _():
            edge_copy(e, False).wait_send()

        return carry

    lax.fori_loop(0, HPD * COLS, drain_edges, 0)


def norm_back(x_in, gain, d_in, grad_out):
    def block(i, carry):
        rows = pl.ds(pl.multiple_of(i * ROWS, ROWS), ROWS)
        squares = jnp.zeros((ROWS, HS), f32)
        total = jnp.zeros((ROWS, HS), f32)
        for h in range(HEADS):
            lanes = slice(h * HS, (h + 1) * HS)
            x = x_in[rows, lanes].astype(f32)
            squares = squares + x * x
            total = total + d_in[h, rows, :].astype(f32) * gain[:, lanes] * x
        mean = jnp.sum(squares, axis=1, keepdims=True) * (1.0 / F)
        factor = lax.rsqrt(mean + EPSILON)
        inner = jnp.sum(total, axis=1, keepdims=True) * factor * (1.0 / F)
        factor = jnp.broadcast_to(factor, (ROWS, HS))
        inner = jnp.broadcast_to(inner, (ROWS, HS)) * factor
        for h in range(HEADS):
            lanes = slice(h * HS, (h + 1) * HS)
            x = x_in[rows, lanes].astype(f32)
            scaled = d_in[h, rows, :].astype(f32) * gain[:, lanes]
            grad_out[rows, lanes] = (factor * (scaled - x * inner)).astype(bf16)
        return carry

    lax.fori_loop(0, BLOCK // ROWS, block, 0)


def closing(
    att_in, dv_in, q_in, k_in, dq_in, dk_in, q_gain, k_gain, gain_in,
    att_out, dv_out, q_out, k_out, q_gain_out, k_gain_out,
):
    att_out[...] = att_in[...]
    dv_out[...] = dv_in[...]

    @pl.when(pl.program_id(0) == 0)
    def _():
        q_gain_out[...] = gain_in[0:1, 0:WIDTH]
        k_gain_out[...] = gain_in[1:2, 0:WIDTH]

    norm_back(q_in, q_gain, dq_in, q_out)
    norm_back(k_in, k_gain, dk_in, k_out)


def shards(
    query_input, key_input, value_input, output_grad, query_gain, key_gain, tile_lists, tile_counts
):
    vmem = pl.BlockSpec(memory_space=pltpu.VMEM)
    anywhere = pl.BlockSpec(memory_space=pl.ANY)
    token = jax.ShapeDtypeStruct((TILE, F), bf16)
    heads = jax.ShapeDtypeStruct((HEADS, TILE, HS), bf16)
    n = HPD * COLS
    attention, dq, dk, value_grad, gains = pl.pallas_call(
        kernel,
        name="tiles",
        out_shape=(token, heads, heads, token, jax.ShapeDtypeStruct((8, HS), f32)),
        in_specs=[anywhere] * 4 + [vmem] * 4,
        out_specs=(anywhere,) * 4 + (vmem,),
        scratch_shapes=[
            pltpu.VMEM((TILE, F), bf16),
            pltpu.VMEM((TILE, F), bf16),
            pltpu.SemaphoreType.DMA((2,)),
            pltpu.VMEM((HEADS, TILE, HS), bf16),
            pltpu.VMEM((HEADS, TILE, HS), bf16),
            pltpu.VMEM((HPD, COLS, CH, HS), bf16),
            pltpu.VMEM((HPD, COLS, CH, HS), bf16),
            pltpu.VMEM((HPD, COLS, 3, CH, HS), bf16),
            pltpu.VMEM((HPD, COLS, 3, CH, HS), bf16),
            pltpu.VMEM((COLS, HS, 3 * CH), bf16),
            pltpu.VMEM((COLS, HS, 3 * CH), bf16),
            pltpu.VMEM((3, 3, CH, CH), f32),
            pltpu.VMEM((3, 3 * CH, CH), bf16),
            pltpu.VMEM((3 * CH, CH), bf16),
            pltpu.VMEM((12, CH, HS), f32),
            pltpu.VMEM((12, CH, HS), f32),
            pltpu.VMEM((n, 2, CH, HS), f32),
            pltpu.VMEM((n, 2, 2, CH, HS), bf16),
            pltpu.VMEM((n, 2, 2, CH, HS), bf16),
            pltpu.VMEM((n, 2, CH, HS), bf16),
            pltpu.VMEM((HPD, COLS, CH, HS), bf16),
            pltpu.VMEM((HPD, COLS, CH, HS), bf16),
            pltpu.VMEM((HS, HS), f32),
            pltpu.VMEM((HS, HS), f32),
            pltpu.VMEM((8, HS), f32),
            pltpu.VMEM((12 * COLS, 2, CH), f32),
            pltpu.SemaphoreType.DMA((2,)),
            pltpu.VMEM((HPD, 8, HS), f32),
            pltpu.VMEM((2 * NB, HPD, 8, HS), f32),
            pltpu.SemaphoreType.DMA((2,)),
            pltpu.SemaphoreType.DMA((4,)),
            pltpu.SemaphoreType.DMA((4, HPD)),
            pltpu.SemaphoreType.DMA((n, 2, 2)),
            pltpu.SemaphoreType.DMA((n, 2, 2)),
            pltpu.SemaphoreType.DMA((n, 2)),
            pltpu.SemaphoreType.DMA((n, 2)),
            pltpu.SemaphoreType.DMA((4,)),
            pltpu.SemaphoreType.DMA((4,)),
        ],
        compiler_params=pltpu.CompilerParams(
            collective_id=0, has_side_effects=True, vmem_limit_bytes=62 * 1024 * 1024
        ),
    )(
        query_input[0],
        key_input[0],
        value_input[0],
        output_grad[0],
        query_gain[None],
        key_gain[None],
        tile_lists.transpose(2, 0, 1),
        tile_counts,
    )
    rows = pl.BlockSpec((BLOCK, F), lambda i: (i, 0))
    by_head = pl.BlockSpec((HEADS, BLOCK, HS), lambda i: (0, i, 0))
    whole = pl.BlockSpec((1, F), lambda i: (0, 0))
    few = pl.BlockSpec((1, WIDTH), lambda i: (0, 0))
    narrow = jax.ShapeDtypeStruct((1, WIDTH), f32)
    attention, value_grad, query_grad, key_grad, query_gains, key_gains = pl.pallas_call(
        closing,
        name="closing",
        grid=(TILE // BLOCK,),
        out_shape=(token, token, token, token, narrow, narrow),
        in_specs=[rows, rows, rows, rows, by_head, by_head, whole, whole]
        + [pl.BlockSpec((8, HS), lambda i: (0, 0))],
        out_specs=(rows, rows, rows, rows, few, few),
        compiler_params=pltpu.CompilerParams(vmem_limit_bytes=62 * 1024 * 1024),
    )(
        attention,
        value_grad,
        query_input[0],
        key_input[0],
        dq,
        dk,
        query_gain[None],
        key_gain[None],
        gains,
    )
    return (
        attention[None],
        query_grad[None],
        key_grad[None],
        value_grad[None],
        query_gains[0],
        key_gains[0],
    )


def solution(mesh):
    tokens = P("dp", ("blk", "head"), None)
    features = P(("dp", "blk", "head"))
    return jax.shard_map(
        shards,
        mesh=mesh,
        in_specs=(tokens, tokens, tokens, tokens, P(), P(), P("dp", None, None), P("dp", None)),
        out_specs=(tokens, tokens, tokens, tokens, features, features),
        check_vma=False,
    )
```

```python
import functools

import jax
import jax.numpy as jnp
from jax import lax
from jax.experimental import pallas as pl
from jax.experimental.pallas import tpu as pltpu
from jax.sharding import PartitionSpec as P

HS = 128
TILE = 192
KMAX = 12
HEADS = 24
HPD = 3
COLS = 4
NB = 8
NH = 8
F = HEADS * HS
CH = 2 * TILE
ROWS = 16
BLOCK = 64
WIDTH = 24
LAG = 5
EPSILON = 1e-06
SCALE = HS**-0.5
SCALE2 = SCALE * 1.4426950408889634
FAR = -1e30
NOWHERE = -1000.0
f32 = jnp.float32
bf16 = jnp.bfloat16


def nn(a, b):
    return lax.dot_general(a, b, (((1,), (0,)), ((), ())), preferred_element_type=f32)


def nt(a, b):
    return lax.dot_general(a, b, (((1,), (1,)), ((), ())), preferred_element_type=f32)


def group_of(slab, device):
    low = device % 2
    return device - low + (low + slab // 4) % 2


def owner(seq, slab):
    pair, part = slab % 4 // 2, slab % 2
    x = pair * (2 + seq) + (1 - pair) * (1 - seq)
    return {"dp": (part + pair) % 2, "blk": slab // 4 * 4 + x}


def unit(core, blk):
    x = blk % 4
    pair = x // 2
    seq = pair * (x - 2) + (1 - pair) * (1 - x)
    return seq, blk // 4 * 4 + 2 * pair + (core + pair) % 2


def wait_for(ref, sem):
    pltpu.make_async_copy(ref, ref, sem).wait()


def kernel(
    q_in,
    k_in,
    v_in,
    g_in,
    q_gain,
    k_gain,
    lists,
    counts,
    att_out,
    dq_recv,
    dk_recv,
    vgrad_out,
    gain_out,
    q_tokens,
    k_tokens,
    token_sem,
    q_stage,
    k_stage,
    qbuf,
    gbuf,
    kbuf,
    vbuf,
    kt_buf,
    vt_buf,
    s_buf,
    p_buf,
    ds_buf,
    acc_k,
    acc_v,
    own_acc,
    edge_send,
    edge_recv,
    own_send,
    o_send,
    dq_send,
    slots,
    named,
    named_here,
    bias,
    list_sem,
    gain_tab,
    gain_recv,
    gain_sem,
    in_send,
    in_recv,
    halo_send,
    halo_recv,
    edge_ssem,
    edge_rsem,
    back_send,
    back_recv,
):
    d = lax.axis_index("dp")
    b = lax.axis_index("blk")
    tile = lax.axis_index("head")
    seq, slab_here = unit(d, b)
    g = group_of(b, tile)
    has_low = slab_here > 0
    has_high = slab_here < NB - 1
    below = {**owner(seq, slab_here - 1), "head": group_of(slab_here - 1, g)}
    above = {**owner(seq, slab_here + 1), "head": group_of(slab_here + 1, g)}
    work = owner(d, b)
    lists_local = seq == d
    other_core = {"dp": 1 - d}
    turned = g // 2 % 2

    def column_at(k):
        return k + turned * (COLS - 1 - 2 * k)

    my_row = tile // COLS
    my_col = tile % COLS
    gain_group = d * 4 + b // 2
    gain_self = gain_group == g
    my_rows = pl.ds(pl.multiple_of(my_row * TILE, TILE), TILE)

    barrier = pltpu.get_barrier_semaphore()

    def greet(i, carry):
        pl.semaphore_signal(barrier, inc=1, device_id={**work, "head": i})
        pl.semaphore_signal(barrier, inc=1, device_id={"dp": seq, "blk": slab_here, "head": i})
        return carry

    lax.fori_loop(0, NH, greet, 0)
    pl.semaphore_signal(barrier, inc=1, device_id=other_core)

    def gain_target(j):
        return {"dp": g // 4, "blk": 2 * (g % 4) + j // NH, "head": j % NH}

    def gain_target_is_me(j):
        return (g // 4 == d) & (2 * (g % 4) + j // NH == b) & (j % NH == tile)

    def greet_gain(j, carry):
        @pl.when(jnp.logical_not(gain_target_is_me(j)))
        def _():
            pl.semaphore_signal(barrier, inc=1, device_id=gain_target(j))

        @pl.when(jnp.logical_not((j // NB == seq) & (j % NB == slab_here) & gain_self))
        def _():
            pl.semaphore_signal(
                barrier,
                inc=1,
                device_id={**owner(j // NB, j % NB), "head": group_of(j % NB, gain_group)},
            )

        return carry

    lax.fori_loop(0, 2 * NB, greet_gain, 0)

    @pl.when(has_low)
    def _():
        pl.semaphore_signal(barrier, inc=1, device_id=below)

    @pl.when(has_high)
    def _():
        pl.semaphore_signal(barrier, inc=1, device_id=above)

    def clear_side(slab, side):
        zeros = jnp.zeros((CH, HS), bf16)

        def one(e, carry):
            h, c = e // COLS, e % COLS
            kbuf[h, c, slab] = zeros
            vbuf[h, c, slab] = zeros
            edge_recv[e, side, 0] = zeros
            edge_recv[e, side, 1] = zeros
            return carry

        lax.fori_loop(0, HPD * COLS, one, 0)

    @pl.when(jnp.logical_not(has_low))
    def _():
        clear_side(0, 0)

    @pl.when(jnp.logical_not(has_high))
    def _():
        clear_side(2, 1)

    for which, (src, dst) in enumerate(((k_in, k_tokens), (q_in, q_tokens))):
        pltpu.make_async_copy(src, dst, token_sem.at[which]).start()

    def normalize(x_in, gain, stage):
        def block(i, carry):
            rows = pl.ds(pl.multiple_of(i * ROWS, ROWS), ROWS)
            total = jnp.zeros((ROWS, HS), f32)
            for h in range(HEADS):
                x = x_in[rows, h * HS : (h + 1) * HS].astype(f32)
                total = total + x * x
            mean = jnp.sum(total, axis=1, keepdims=True) * (1.0 / F)
            factor = jnp.broadcast_to(lax.rsqrt(mean + EPSILON), (ROWS, HS))
            for h in range(HEADS):
                x = x_in[rows, h * HS : (h + 1) * HS].astype(f32)
                stage[h, rows, :] = (x * factor * gain[:, h * HS : (h + 1) * HS]).astype(bf16)
            return carry

        lax.fori_loop(0, TILE // ROWS, block, 0)

    def send_in(h, which, src_of, dst):
        def one(i, carry):
            to = (tile + i) % NH
            pltpu.make_async_remote_copy(
                src_ref=src_of(group_of(b, to) * HPD + h),
                dst_ref=dst,
                send_sem=in_send.at[which],
                recv_sem=in_recv.at[which, h],
                device_id={**work, "head": to},
            ).start()
            return carry

        lax.fori_loop(0, NH, one, 0)

    def columns(h):
        return pl.ds(pl.multiple_of(h * HS, HS), HS)

    def send_k(h):
        send_in(h, 0, lambda n: k_stage.at[n], kbuf.at[h, my_col, 1, my_rows])

    def send_v(h):
        send_in(h, 1, lambda n: v_in.at[:, columns(n)], vbuf.at[h, my_col, 1, my_rows])

    def send_q(h):
        send_in(h, 2, lambda n: q_stage.at[n], qbuf.at[h, my_col, my_rows])

    def send_g(h):
        send_in(h, 3, lambda n: g_in.at[:, columns(n)], gbuf.at[h, my_col, my_rows])

    tiles = NB * 8
    slot = lax.broadcasted_iota(jnp.int32, (KMAX, tiles), 0)
    slots[...] = jnp.full((HS, HS), NOWHERE, f32)
    slots[0:KMAX, 0:tiles] = jnp.where(slot < counts[...], lists[:, 0, :], NOWHERE).astype(f32)
    named[...] = slots[...].T

    def list_copy():
        slab = unit(1 - d, b)[1]
        return pltpu.make_async_remote_copy(
            src_ref=named.at[pl.ds(pl.multiple_of(slab * 8, 8), 8)],
            dst_ref=named_here,
            send_sem=list_sem.at[0],
            recv_sem=list_sem.at[1],
            device_id=other_core,
        )

    def build_bias():
        @pl.when(lists_local)
        def _():
            named_here[...] = named[pl.ds(pl.multiple_of(slab_here * 8, 8), 8), :]

        @pl.when(jnp.logical_not(lists_local))
        def _():
            list_copy().wait_recv()

        found = named_here[...] - ((slab_here - 1) * 8).astype(f32)
        first_row = lax.broadcasted_iota(jnp.int32, (1, CH), 1) < TILE
        for near in range(24):
            hit = jnp.max(jnp.where(found == near, 1.0, 0.0), axis=1, keepdims=True)
            away = jnp.broadcast_to(jnp.where(hit > 0.5, 0.0, FAR), (8, CH))
            slab, row, col = near // 8, near // COLS % 2, near % COLS
            for c in range(COLS):
                bias[c * 12 + col * 3 + slab, row : row + 1, :] = jnp.where(
                    first_row, away[c : c + 1], away[COLS + c : COLS + c + 1]
                )

    wait_for(k_tokens, token_sem.at[0])
    normalize(k_tokens, k_gain, k_stage)
    pl.semaphore_wait(
        barrier,
        2 * NH
        + 1
        + 4 * NB
        - 2 * gain_self.astype(jnp.int32)
        + has_low.astype(jnp.int32)
        + has_high.astype(jnp.int32),
    )
    @pl.when(lists_local)
    def _():
        list_copy().start()

    send_v(0)
    send_k(0)
    send_g(0)
    wait_for(q_tokens, token_sem.at[1])
    normalize(q_tokens, q_gain, q_stage)
    send_q(0)
    build_bias()

    def halo_copy(h, c, which, up):
        buf = (kbuf, vbuf)[which]
        side = 0 if up else 1
        return pltpu.make_async_remote_copy(
            src_ref=buf.at[h, c, 1],
            dst_ref=buf.at[h, c, 0 if up else 2],
            send_sem=halo_send.at[h * COLS + c, which, side],
            recv_sem=halo_recv.at[h * COLS + c, which, side],
            device_id=above if up else below,
        )

    def forward(h):
        wait_for(kbuf.at[h, :, 1], in_recv.at[0, h])
        wait_for(vbuf.at[h, :, 1], in_recv.at[1, h])

        def one(k, carry):
            c = column_at(k)
            for which in range(2):

                @pl.when(has_high)
                def _():
                    halo_copy(h, c, which, True).start()

                @pl.when(has_low)
                def _():
                    halo_copy(h, c, which, False).start()

            return carry

        lax.fori_loop(0, COLS, one, 0)

    def await_halo(h, c):
        for which in range(2):

            @pl.when(has_low)
            def _():
                halo_copy(h, c, which, True).wait_recv()

            @pl.when(has_high)
            def _():
                halo_copy(h, c, which, False).wait_recv()

    def send_back(which, src, dst, t):
        pltpu.make_async_remote_copy(
            src_ref=src,
            dst_ref=dst,
            send_sem=back_send.at[which],
            recv_sem=back_recv.at[which],
            device_id={"dp": seq, "blk": slab_here, "head": t},
        ).start()

    def attend(h, c):
        low = jnp.maximum(c - 1, 0)
        high = jnp.minimum(c + 2, COLS)
        q = qbuf[h, c]

        def first(k, top):
            for slab in range(3):
                s = nt(kbuf[h, k, slab], q)
                s_buf[k - low, slab] = s
                away = bias[c * 12 + k * 3 + slab]
                top = jnp.maximum(top, jnp.max(s[:TILE], axis=0, keepdims=True) + away[0:1])
                top = jnp.maximum(top, jnp.max(s[TILE:], axis=0, keepdims=True) + away[1:2])
            return top

        top = lax.fori_loop(low, high, first, jnp.full((1, CH), 2 * FAR, f32)) * SCALE2

        def second(k, carry):
            total, out = carry
            for slab in range(3):
                away = bias[c * 12 + k * 3 + slab]
                s = s_buf[k - low, slab]
                e0 = jnp.exp2(s[:TILE] * SCALE2 - (top - away[0:1]))
                e1 = jnp.exp2(s[TILE:] * SCALE2 - (top - away[1:2]))
                total = total + jnp.sum(e0, axis=0, keepdims=True)
                total = total + jnp.sum(e1, axis=0, keepdims=True)
                p_buf[k - low, slab * CH : slab * CH + TILE] = e0.astype(bf16)
                p_buf[k - low, slab * CH + TILE : (slab + 1) * CH] = e1.astype(bf16)
            return total, out + nn(vt_buf[k], p_buf[k - low])

        total, out = lax.fori_loop(
            low, high, second, (jnp.zeros((1, CH), f32), jnp.zeros((HS, CH), f32))
        )
        inverse = 1.0 / total
        out = out * inverse
        o_send[h, c] = out.T.astype(bf16)
        grad = gbuf[h, c].astype(f32).T
        delta = jnp.sum(out * grad, axis=0, keepdims=True) * inverse
        grad = grad * inverse
        grad_t = grad.astype(bf16)
        grad_s = grad.T.astype(bf16)

        def third(k, dq):
            for slab in range(3):
                e = p_buf[k - low, slab * CH : (slab + 1) * CH]
                dp = nn(vbuf[h, k, slab], grad_t)
                ds = (e.astype(f32) * (dp - delta)).astype(bf16)
                ds_buf[slab * CH : (slab + 1) * CH] = ds
                acc_v[k * 3 + slab] += nn(e, grad_s)
                acc_k[k * 3 + slab] += nn(ds, q)
            return dq + nn(kt_buf[k], ds_buf[...])

        dq = lax.fori_loop(low, high, third, jnp.zeros((HS, CH), f32))
        dq = (dq * SCALE).T.astype(bf16)
        dq_send[h, c] = dq
        gain_tab[h, 0:1, :] += jnp.sum(dq.astype(f32) * q.astype(f32), axis=0, keepdims=True)
        for r in range(2):
            rows = pl.ds(r * TILE, TILE)
            t = r * COLS + c
            send_back(0, o_send.at[h, c, rows], att_out.at[:, columns(g * HPD + h)], t)
            send_back(1, dq_send.at[h, c, rows], dq_recv.at[g * HPD + h], t)

    def edge_copy(e, up):
        return pltpu.make_async_remote_copy(
            src_ref=edge_send.at[e, 1 if up else 0],
            dst_ref=edge_recv.at[e, 0 if up else 1],
            send_sem=edge_ssem.at[e, 1 if up else 0],
            recv_sem=edge_rsem.at[e, 0 if up else 1],
            device_id=above if up else below,
        )

    def finish(h, c):
        e = h * COLS + c
        for side, slab in ((0, 0), (1, 2)):
            edge_send[e, side, 0] = (acc_k[c * 3 + slab] * SCALE).astype(bf16)
            edge_send[e, side, 1] = acc_v[c * 3 + slab].astype(bf16)
        own_acc[e, 0] = acc_k[c * 3 + 1] * SCALE
        own_acc[e, 1] = acc_v[c * 3 + 1]

        @pl.when(has_high)
        def _():
            edge_copy(e, True).start()

        @pl.when(has_low)
        def _():
            edge_copy(e, False).start()

    def settle(n):
        h, c = n // COLS, column_at(n % COLS)
        e = h * COLS + c

        @pl.when(has_low)
        def _():
            edge_copy(e, True).wait_recv()

        @pl.when(has_high)
        def _():
            edge_copy(e, False).wait_recv()

        for a in range(2):
            own_send[e, a] = (
                own_acc[e, a] + edge_recv[e, 0, a].astype(f32) + edge_recv[e, 1, a].astype(f32)
            ).astype(bf16)
        product = own_send[e, 0].astype(f32) * kbuf[h, c, 1].astype(f32)
        gain_tab[h, 1:2, :] += jnp.sum(product, axis=0, keepdims=True)
        for r in range(2):
            rows = pl.ds(r * TILE, TILE)
            t = r * COLS + c
            send_back(2, own_send.at[e, 0, rows], dk_recv.at[g * HPD + h], t)
            send_back(3, own_send.at[e, 1, rows], vgrad_out.at[:, columns(g * HPD + h)], t)

    def start_column(h, k):
        await_halo(h, k)
        for slab in range(3):
            keys = slice(slab * CH, (slab + 1) * CH)
            kt_buf[k, :, keys] = kbuf[h, k, slab].T
            vt_buf[k, :, keys] = vbuf[h, k, slab].T
            acc_k[k * 3 + slab] = jnp.zeros((CH, HS), f32)
            acc_v[k * 3 + slab] = jnp.zeros((CH, HS), f32)

    gain_tab[...] = jnp.zeros_like(gain_tab)
    forward(0)

    def rest(h, carry):
        send_k(h)
        send_v(h)
        send_q(h)
        send_g(h)
        return carry

    lax.fori_loop(1, HPD, rest, 0)

    def step(s, carry):
        h, k = s // COLS, s % COLS
        c = column_at(k)

        @pl.when(k == 0)
        def _():
            start_column(h, c)

            @pl.when(h < HPD - 1)
            def _():
                forward(h + 1)

            wait_for(qbuf.at[h], in_recv.at[2, h])
            wait_for(gbuf.at[h], in_recv.at[3, h])

        @pl.when(k < COLS - 1)
        def _():
            start_column(h, column_at(k + 1))

        attend(h, c)

        @pl.when(k > 0)
        def _():
            finish(h, column_at(k - 1))

        @pl.when(k == COLS - 1)
        def _():
            finish(h, c)

        @pl.when(s >= LAG)
        def _():
            settle(s - LAG)

        return carry

    lax.fori_loop(0, HPD * COLS, step, 0)

    def last(e, carry):
        settle(e)
        return carry

    lax.fori_loop(HPD * COLS - LAG, HPD * COLS, last, 0)

    for h in range(HPD):
        for row, gain in ((0, q_gain), (1, k_gain)):
            gain_tab[h, row : row + 1, :] = gain_tab[h, row : row + 1, :] / gain[:, columns(g * HPD + h)]

    def give(j, carry):
        dst = gain_recv.at[seq * NB + slab_here]
        me = gain_target_is_me(j)

        @pl.when(me)
        def _():
            pltpu.make_async_copy(gain_tab, dst, gain_sem.at[1]).start()

        @pl.when(jnp.logical_not(me))
        def _():
            pltpu.make_async_remote_copy(
                src_ref=gain_tab,
                dst_ref=dst,
                send_sem=gain_sem.at[0],
                recv_sem=gain_sem.at[1],
                device_id=gain_target(j),
            ).start()

        return carry

    lax.fori_loop(0, 2 * NB, give, 0)

    wait_for(gain_recv, gain_sem.at[1])
    start = 24 * ((b % 2) * NH + tile)
    lane = lax.broadcasted_iota(jnp.int32, (HS, HS), 1)
    source = lax.broadcasted_iota(jnp.int32, (HS, HS), 0)
    sums = jnp.zeros((8, HS), f32)
    for h in range(HPD):
        pick = ((source + h * HS == lane + start) & (lane < 24)).astype(f32)
        part = gain_recv[0, h]
        for i in range(1, 2 * NB):
            part = part + gain_recv[i, h]
        sums = sums + jnp.dot(
            part, pick, precision=lax.Precision.HIGHEST, preferred_element_type=f32
        )
    gain_out[...] = sums
    wait_for(att_out, back_recv.at[0])
    wait_for(dq_recv, back_recv.at[1])
    wait_for(dk_recv, back_recv.at[2])
    wait_for(vgrad_out, back_recv.at[3])

    wait_for(gain_recv.at[0 : 2 * NB - 1], gain_sem.at[0])

    @pl.when(jnp.logical_not(gain_self))
    def _():
        wait_for(gain_recv.at[0], gain_sem.at[0])

    for which in range(4):
        wait_for(dq_recv, in_send.at[which])
        wait_for(dq_recv, back_send.at[which])

    @pl.when(lists_local)
    def _():
        list_copy().wait_send()

    def drain_edges(e, carry):
        for which in range(2):

            @pl.when(has_high)
            def _():
                halo_copy(e // COLS, e % COLS, which, True).wait_send()

            @pl.when(has_low)
            def _():
                halo_copy(e // COLS, e % COLS, which, False).wait_send()

        @pl.when(has_high)
        def _():
            edge_copy(e, True).wait_send()

        @pl.when(has_low)
        def _():
            edge_copy(e, False).wait_send()

        return carry

    lax.fori_loop(0, HPD * COLS, drain_edges, 0)


def norm_back(x_in, gain, d_in, grad_out):
    def block(i, carry):
        rows = pl.ds(pl.multiple_of(i * ROWS, ROWS), ROWS)
        squares = jnp.zeros((ROWS, HS), f32)
        total = jnp.zeros((ROWS, HS), f32)
        for h in range(HEADS):
            lanes = slice(h * HS, (h + 1) * HS)
            x = x_in[rows, lanes].astype(f32)
            squares = squares + x * x
            total = total + d_in[h, rows, :].astype(f32) * gain[:, lanes] * x
        mean = jnp.sum(squares, axis=1, keepdims=True) * (1.0 / F)
        factor = lax.rsqrt(mean + EPSILON)
        inner = jnp.sum(total, axis=1, keepdims=True) * factor * (1.0 / F)
        factor = jnp.broadcast_to(factor, (ROWS, HS))
        inner = jnp.broadcast_to(inner, (ROWS, HS)) * factor
        for h in range(HEADS):
            lanes = slice(h * HS, (h + 1) * HS)
            x = x_in[rows, lanes].astype(f32)
            scaled = d_in[h, rows, :].astype(f32) * gain[:, lanes]
            grad_out[rows, lanes] = (factor * (scaled - x * inner)).astype(bf16)
        return carry

    lax.fori_loop(0, BLOCK // ROWS, block, 0)


def closing(
    att_in, dv_in, q_in, k_in, dq_in, dk_in, q_gain, k_gain, gain_in,
    att_out, dv_out, q_out, k_out, q_gain_out, k_gain_out,
):
    att_out[...] = att_in[...]
    dv_out[...] = dv_in[...]

    @pl.when(pl.program_id(0) == 0)
    def _():
        q_gain_out[...] = gain_in[0:1, 0:WIDTH]
        k_gain_out[...] = gain_in[1:2, 0:WIDTH]

    norm_back(q_in, q_gain, dq_in, q_out)
    norm_back(k_in, k_gain, dk_in, k_out)


def shards(
    query_input, key_input, value_input, output_grad, query_gain, key_gain, tile_lists, tile_counts
):
    vmem = pl.BlockSpec(memory_space=pltpu.VMEM)
    anywhere = pl.BlockSpec(memory_space=pl.ANY)
    token = jax.ShapeDtypeStruct((TILE, F), bf16)
    heads = jax.ShapeDtypeStruct((HEADS, TILE, HS), bf16)
    n = HPD * COLS
    attention, dq, dk, value_grad, gains = pl.pallas_call(
        kernel,
        name="tiles",
        out_shape=(token, heads, heads, token, jax.ShapeDtypeStruct((8, HS), f32)),
        in_specs=[anywhere] * 4 + [vmem] * 4,
        out_specs=(anywhere,) * 4 + (vmem,),
        scratch_shapes=[
            pltpu.VMEM((TILE, F), bf16),
            pltpu.VMEM((TILE, F), bf16),
            pltpu.SemaphoreType.DMA((2,)),
            pltpu.VMEM((HEADS, TILE, HS), bf16),
            pltpu.VMEM((HEADS, TILE, HS), bf16),
            pltpu.VMEM((HPD, COLS, CH, HS), bf16),
            pltpu.VMEM((HPD, COLS, CH, HS), bf16),
            pltpu.VMEM((HPD, COLS, 3, CH, HS), bf16),
            pltpu.VMEM((HPD, COLS, 3, CH, HS), bf16),
            pltpu.VMEM((COLS, HS, 3 * CH), bf16),
            pltpu.VMEM((COLS, HS, 3 * CH), bf16),
            pltpu.VMEM((3, 3, CH, CH), f32),
            pltpu.VMEM((3, 3 * CH, CH), bf16),
            pltpu.VMEM((3 * CH, CH), bf16),
            pltpu.VMEM((12, CH, HS), f32),
            pltpu.VMEM((12, CH, HS), f32),
            pltpu.VMEM((n, 2, CH, HS), f32),
            pltpu.VMEM((n, 2, 2, CH, HS), bf16),
            pltpu.VMEM((n, 2, 2, CH, HS), bf16),
            pltpu.VMEM((n, 2, CH, HS), bf16),
            pltpu.VMEM((HPD, COLS, CH, HS), bf16),
            pltpu.VMEM((HPD, COLS, CH, HS), bf16),
            pltpu.VMEM((HS, HS), f32),
            pltpu.VMEM((HS, HS), f32),
            pltpu.VMEM((8, HS), f32),
            pltpu.VMEM((12 * COLS, 2, CH), f32),
            pltpu.SemaphoreType.DMA((2,)),
            pltpu.VMEM((HPD, 8, HS), f32),
            pltpu.VMEM((2 * NB, HPD, 8, HS), f32),
            pltpu.SemaphoreType.DMA((2,)),
            pltpu.SemaphoreType.DMA((4,)),
            pltpu.SemaphoreType.DMA((4, HPD)),
            pltpu.SemaphoreType.DMA((n, 2, 2)),
            pltpu.SemaphoreType.DMA((n, 2, 2)),
            pltpu.SemaphoreType.DMA((n, 2)),
            pltpu.SemaphoreType.DMA((n, 2)),
            pltpu.SemaphoreType.DMA((4,)),
            pltpu.SemaphoreType.DMA((4,)),
        ],
        compiler_params=pltpu.CompilerParams(
            collective_id=0, has_side_effects=True, vmem_limit_bytes=62 * 1024 * 1024
        ),
    )(
        query_input[0],
        key_input[0],
        value_input[0],
        output_grad[0],
        query_gain[None],
        key_gain[None],
        tile_lists.transpose(2, 0, 1),
        tile_counts,
    )
    rows = pl.BlockSpec((BLOCK, F), lambda i: (i, 0))
    by_head = pl.BlockSpec((HEADS, BLOCK, HS), lambda i: (0, i, 0))
    whole = pl.BlockSpec((1, F), lambda i: (0, 0))
    few = pl.BlockSpec((1, WIDTH), lambda i: (0, 0))
    narrow = jax.ShapeDtypeStruct((1, WIDTH), f32)
    attention, value_grad, query_grad, key_grad, query_gains, key_gains = pl.pallas_call(
        closing,
        name="closing",
        grid=(TILE // BLOCK,),
        out_shape=(token, token, token, token, narrow, narrow),
        in_specs=[rows, rows, rows, rows, by_head, by_head, whole, whole]
        + [pl.BlockSpec((8, HS), lambda i: (0, 0))],
        out_specs=(rows, rows, rows, rows, few, few),
        compiler_params=pltpu.CompilerParams(vmem_limit_bytes=62 * 1024 * 1024),
    )(
        attention,
        value_grad,
        query_input[0],
        key_input[0],
        dq,
        dk,
        query_gain[None],
        key_gain[None],
        gains,
    )
    return (
        attention[None],
        query_grad[None],
        key_grad[None],
        value_grad[None],
        query_gains[0],
        key_gains[0],
    )


def solution(mesh):
    tokens = P("dp", ("blk", "head"), None)
    features = P(("dp", "blk", "head"))
    return jax.shard_map(
        shards,
        mesh=mesh,
        in_specs=(tokens, tokens, tokens, tokens, P(), P(), P("dp", None, None), P("dp", None)),
        out_specs=(tokens, tokens, tokens, tokens, features, features),
        check_vma=False,
    )
```

```python
import functools

import jax
import jax.numpy as jnp
from jax import lax
from jax.experimental import pallas as pl
from jax.experimental.pallas import tpu as pltpu
from jax.sharding import PartitionSpec as P

HS = 128
TILE = 192
KMAX = 12
HEADS = 24
HPD = 3
COLS = 4
NB = 8
NH = 8
F = HEADS * HS
CH = 2 * TILE
ROWS = 16
BLOCK = 64
WIDTH = 24
LAG = 5
EPSILON = 1e-06
SCALE = HS**-0.5
SCALE2 = SCALE * 1.4426950408889634
FAR = -1e30
NOWHERE = -1000.0
f32 = jnp.float32
bf16 = jnp.bfloat16


def nn(a, b):
    return lax.dot_general(a, b, (((1,), (0,)), ((), ())), preferred_element_type=f32)


def nt(a, b):
    return lax.dot_general(a, b, (((1,), (1,)), ((), ())), preferred_element_type=f32)


def group_of(slab, device):
    low = device % 2
    return device - low + (low + slab // 4) % 2


def owner(seq, slab):
    pair, part = slab % 4 // 2, slab % 2
    x = pair * (2 + seq) + (1 - pair) * (1 - seq)
    return {"dp": (part + pair) % 2, "blk": slab // 4 * 4 + x}


def unit(core, blk):
    x = blk % 4
    pair = x // 2
    seq = pair * (x - 2) + (1 - pair) * (1 - x)
    return seq, blk // 4 * 4 + 2 * pair + (core + pair) % 2


def wait_for(ref, sem):
    pltpu.make_async_copy(ref, ref, sem).wait()


def norm_back(x_in, gain, d_in, grad_out, count):
    def block(i, carry):
        rows = pl.ds(pl.multiple_of(i * ROWS, ROWS), ROWS)
        squares = jnp.zeros((ROWS, HS), f32)
        total = jnp.zeros((ROWS, HS), f32)
        for h in range(HEADS):
            lanes = slice(h * HS, (h + 1) * HS)
            x = x_in[rows, lanes].astype(f32)
            squares = squares + x * x
            total = total + d_in[h, rows, :].astype(f32) * gain[:, lanes] * x
        mean = jnp.sum(squares, axis=1, keepdims=True) * (1.0 / F)
        factor = lax.rsqrt(mean + EPSILON)
        inner = jnp.sum(total, axis=1, keepdims=True) * factor * (1.0 / F)
        factor = jnp.broadcast_to(factor, (ROWS, HS))
        inner = jnp.broadcast_to(inner, (ROWS, HS)) * factor
        for h in range(HEADS):
            lanes = slice(h * HS, (h + 1) * HS)
            x = x_in[rows, lanes].astype(f32)
            scaled = d_in[h, rows, :].astype(f32) * gain[:, lanes]
            grad_out[rows, lanes] = (factor * (scaled - x * inner)).astype(bf16)
        return carry

    lax.fori_loop(0, count // ROWS, block, 0)


def kernel(
    q_in,
    k_in,
    v_in,
    g_in,
    q_gain,
    k_gain,
    lists,
    counts,
    att_out,
    qgrad_out,
    dk_recv,
    vgrad_out,
    gain_out,
    q_tokens,
    k_tokens,
    token_sem,
    q_stage,
    k_stage,
    qbuf,
    gbuf,
    kbuf,
    vbuf,
    kt_buf,
    vt_buf,
    s_buf,
    p_buf,
    ds_buf,
    acc_k,
    acc_v,
    own_acc,
    edge_send,
    edge_recv,
    own_send,
    o_send,
    dq_send,
    dq_recv,
    slots,
    named,
    named_here,
    bias,
    list_sem,
    gain_tab,
    gain_recv,
    gain_sem,
    in_send,
    in_recv,
    halo_send,
    halo_recv,
    edge_ssem,
    edge_rsem,
    back_send,
    back_recv,
):
    d = lax.axis_index("dp")
    b = lax.axis_index("blk")
    tile = lax.axis_index("head")
    seq, slab_here = unit(d, b)
    g = group_of(b, tile)
    has_low = slab_here > 0
    has_high = slab_here < NB - 1
    below = {**owner(seq, slab_here - 1), "head": group_of(slab_here - 1, g)}
    above = {**owner(seq, slab_here + 1), "head": group_of(slab_here + 1, g)}
    work = owner(d, b)
    lists_local = seq == d
    other_core = {"dp": 1 - d}
    turned = g // 2 % 2

    def column_at(k):
        return k + turned * (COLS - 1 - 2 * k)

    my_row = tile // COLS
    my_col = tile % COLS
    gain_group = d * 4 + b // 2
    gain_self = gain_group == g
    my_rows = pl.ds(pl.multiple_of(my_row * TILE, TILE), TILE)

    barrier = pltpu.get_barrier_semaphore()

    def greet(i, carry):
        pl.semaphore_signal(barrier, inc=1, device_id={**work, "head": i})
        pl.semaphore_signal(barrier, inc=1, device_id={"dp": seq, "blk": slab_here, "head": i})
        return carry

    lax.fori_loop(0, NH, greet, 0)
    pl.semaphore_signal(barrier, inc=1, device_id=other_core)

    def gain_target(j):
        return {"dp": g // 4, "blk": 2 * (g % 4) + j // NH, "head": j % NH}

    def gain_target_is_me(j):
        return (g // 4 == d) & (2 * (g % 4) + j // NH == b) & (j % NH == tile)

    def greet_gain(j, carry):
        @pl.when(jnp.logical_not(gain_target_is_me(j)))
        def _():
            pl.semaphore_signal(barrier, inc=1, device_id=gain_target(j))

        @pl.when(jnp.logical_not((j // NB == seq) & (j % NB == slab_here) & gain_self))
        def _():
            pl.semaphore_signal(
                barrier,
                inc=1,
                device_id={**owner(j // NB, j % NB), "head": group_of(j % NB, gain_group)},
            )

        return carry

    lax.fori_loop(0, 2 * NB, greet_gain, 0)

    @pl.when(has_low)
    def _():
        pl.semaphore_signal(barrier, inc=1, device_id=below)

    @pl.when(has_high)
    def _():
        pl.semaphore_signal(barrier, inc=1, device_id=above)

    def clear_side(slab, side):
        zeros = jnp.zeros((CH, HS), bf16)

        def one(e, carry):
            h, c = e // COLS, e % COLS
            kbuf[h, c, slab] = zeros
            vbuf[h, c, slab] = zeros
            edge_recv[e, side, 0] = zeros
            edge_recv[e, side, 1] = zeros
            return carry

        lax.fori_loop(0, HPD * COLS, one, 0)

    @pl.when(jnp.logical_not(has_low))
    def _():
        clear_side(0, 0)

    @pl.when(jnp.logical_not(has_high))
    def _():
        clear_side(2, 1)

    for which, (src, dst) in enumerate(((k_in, k_tokens), (q_in, q_tokens))):
        pltpu.make_async_copy(src, dst, token_sem.at[which]).start()

    def normalize(x_in, gain, stage):
        def block(i, carry):
            rows = pl.ds(pl.multiple_of(i * ROWS, ROWS), ROWS)
            total = jnp.zeros((ROWS, HS), f32)
            for h in range(HEADS):
                x = x_in[rows, h * HS : (h + 1) * HS].astype(f32)
                total = total + x * x
            mean = jnp.sum(total, axis=1, keepdims=True) * (1.0 / F)
            factor = jnp.broadcast_to(lax.rsqrt(mean + EPSILON), (ROWS, HS))
            for h in range(HEADS):
                x = x_in[rows, h * HS : (h + 1) * HS].astype(f32)
                stage[h, rows, :] = (x * factor * gain[:, h * HS : (h + 1) * HS]).astype(bf16)
            return carry

        lax.fori_loop(0, TILE // ROWS, block, 0)

    def send_in(h, which, src_of, dst):
        def one(i, carry):
            to = (tile + i) % NH
            pltpu.make_async_remote_copy(
                src_ref=src_of(group_of(b, to) * HPD + h),
                dst_ref=dst,
                send_sem=in_send.at[which],
                recv_sem=in_recv.at[which, h],
                device_id={**work, "head": to},
            ).start()
            return carry

        lax.fori_loop(0, NH, one, 0)

    def columns(h):
        return pl.ds(pl.multiple_of(h * HS, HS), HS)

    def send_k(h):
        send_in(h, 0, lambda n: k_stage.at[n], kbuf.at[h, my_col, 1, my_rows])

    def send_v(h):
        send_in(h, 1, lambda n: v_in.at[:, columns(n)], vbuf.at[h, my_col, 1, my_rows])

    def send_q(h):
        send_in(h, 2, lambda n: q_stage.at[n], qbuf.at[h, my_col, my_rows])

    def send_g(h):
        send_in(h, 3, lambda n: g_in.at[:, columns(n)], gbuf.at[h, my_col, my_rows])

    tiles = NB * 8
    slot = lax.broadcasted_iota(jnp.int32, (KMAX, tiles), 0)
    slots[...] = jnp.full((HS, HS), NOWHERE, f32)
    slots[0:KMAX, 0:tiles] = jnp.where(slot < counts[...], lists[:, 0, :], NOWHERE).astype(f32)
    named[...] = slots[...].T

    def list_copy():
        slab = unit(1 - d, b)[1]
        return pltpu.make_async_remote_copy(
            src_ref=named.at[pl.ds(pl.multiple_of(slab * 8, 8), 8)],
            dst_ref=named_here,
            send_sem=list_sem.at[0],
            recv_sem=list_sem.at[1],
            device_id=other_core,
        )

    def build_bias():
        @pl.when(lists_local)
        def _():
            named_here[...] = named[pl.ds(pl.multiple_of(slab_here * 8, 8), 8), :]

        @pl.when(jnp.logical_not(lists_local))
        def _():
            list_copy().wait_recv()

        found = named_here[...] - ((slab_here - 1) * 8).astype(f32)
        first_row = lax.broadcasted_iota(jnp.int32, (1, CH), 1) < TILE
        for near in range(24):
            hit = jnp.max(jnp.where(found == near, 1.0, 0.0), axis=1, keepdims=True)
            away = jnp.broadcast_to(jnp.where(hit > 0.5, 0.0, FAR), (8, CH))
            slab, row, col = near // 8, near // COLS % 2, near % COLS
            for c in range(COLS):
                bias[c * 12 + col * 3 + slab, row : row + 1, :] = jnp.where(
                    first_row, away[c : c + 1], away[COLS + c : COLS + c + 1]
                )

    wait_for(k_tokens, token_sem.at[0])
    normalize(k_tokens, k_gain, k_stage)
    pl.semaphore_wait(
        barrier,
        2 * NH
        + 1
        + 4 * NB
        - 2 * gain_self.astype(jnp.int32)
        + has_low.astype(jnp.int32)
        + has_high.astype(jnp.int32),
    )
    @pl.when(lists_local)
    def _():
        list_copy().start()

    send_v(0)
    send_k(0)
    send_g(0)
    wait_for(q_tokens, token_sem.at[1])
    normalize(q_tokens, q_gain, q_stage)
    send_q(0)
    build_bias()

    def halo_copy(h, c, which, up):
        buf = (kbuf, vbuf)[which]
        side = 0 if up else 1
        return pltpu.make_async_remote_copy(
            src_ref=buf.at[h, c, 1],
            dst_ref=buf.at[h, c, 0 if up else 2],
            send_sem=halo_send.at[h * COLS + c, which, side],
            recv_sem=halo_recv.at[h * COLS + c, which, side],
            device_id=above if up else below,
        )

    def forward(h):
        wait_for(kbuf.at[h, :, 1], in_recv.at[0, h])
        wait_for(vbuf.at[h, :, 1], in_recv.at[1, h])

        def one(k, carry):
            c = column_at(k)
            for which in range(2):

                @pl.when(has_high)
                def _():
                    halo_copy(h, c, which, True).start()

                @pl.when(has_low)
                def _():
                    halo_copy(h, c, which, False).start()

            return carry

        lax.fori_loop(0, COLS, one, 0)

    def await_halo(h, c):
        for which in range(2):

            @pl.when(has_low)
            def _():
                halo_copy(h, c, which, True).wait_recv()

            @pl.when(has_high)
            def _():
                halo_copy(h, c, which, False).wait_recv()

    def send_back(which, src, dst, t):
        pltpu.make_async_remote_copy(
            src_ref=src,
            dst_ref=dst,
            send_sem=back_send.at[which],
            recv_sem=back_recv.at[which],
            device_id={"dp": seq, "blk": slab_here, "head": t},
        ).start()

    def attend(h, c):
        low = jnp.maximum(c - 1, 0)
        high = jnp.minimum(c + 2, COLS)
        q = qbuf[h, c]

        def first(k, top):
            for slab in range(3):
                s = nt(kbuf[h, k, slab], q)
                s_buf[k - low, slab] = s
                away = bias[c * 12 + k * 3 + slab]
                top = jnp.maximum(top, jnp.max(s[:TILE], axis=0, keepdims=True) + away[0:1])
                top = jnp.maximum(top, jnp.max(s[TILE:], axis=0, keepdims=True) + away[1:2])
            return top

        top = lax.fori_loop(low, high, first, jnp.full((1, CH), 2 * FAR, f32)) * SCALE2

        def second(k, carry):
            total, out = carry
            for slab in range(3):
                away = bias[c * 12 + k * 3 + slab]
                s = s_buf[k - low, slab]
                e0 = jnp.exp2(s[:TILE] * SCALE2 - (top - away[0:1]))
                e1 = jnp.exp2(s[TILE:] * SCALE2 - (top - away[1:2]))
                total = total + jnp.sum(e0, axis=0, keepdims=True)
                total = total + jnp.sum(e1, axis=0, keepdims=True)
                p_buf[k - low, slab * CH : slab * CH + TILE] = e0.astype(bf16)
                p_buf[k - low, slab * CH + TILE : (slab + 1) * CH] = e1.astype(bf16)
            return total, out + nn(vt_buf[k], p_buf[k - low])

        total, out = lax.fori_loop(
            low, high, second, (jnp.zeros((1, CH), f32), jnp.zeros((HS, CH), f32))
        )
        inverse = 1.0 / total
        out = out * inverse
        o_send[h, c] = out.T.astype(bf16)
        grad = gbuf[h, c].astype(f32).T
        delta = jnp.sum(out * grad, axis=0, keepdims=True) * inverse
        grad = grad * inverse
        grad_t = grad.astype(bf16)
        grad_s = grad.T.astype(bf16)

        def third(k, dq):
            for slab in range(3):
                e = p_buf[k - low, slab * CH : (slab + 1) * CH]
                dp = nn(vbuf[h, k, slab], grad_t)
                ds = (e.astype(f32) * (dp - delta)).astype(bf16)
                ds_buf[slab * CH : (slab + 1) * CH] = ds
                acc_v[k * 3 + slab] += nn(e, grad_s)
                acc_k[k * 3 + slab] += nn(ds, q)
            return dq + nn(kt_buf[k], ds_buf[...])

        dq = lax.fori_loop(low, high, third, jnp.zeros((HS, CH), f32))
        dq = (dq * SCALE).T.astype(bf16)
        dq_send[h, c] = dq
        gain_tab[h, 0:1, :] += jnp.sum(dq.astype(f32) * q.astype(f32), axis=0, keepdims=True)
        for r in range(2):
            rows = pl.ds(r * TILE, TILE)
            t = r * COLS + c
            send_back(0, o_send.at[h, c, rows], att_out.at[:, columns(g * HPD + h)], t)
            send_back(1, dq_send.at[h, c, rows], dq_recv.at[g * HPD + h], t)

    def edge_copy(e, up):
        return pltpu.make_async_remote_copy(
            src_ref=edge_send.at[e, 1 if up else 0],
            dst_ref=edge_recv.at[e, 0 if up else 1],
            send_sem=edge_ssem.at[e, 1 if up else 0],
            recv_sem=edge_rsem.at[e, 0 if up else 1],
            device_id=above if up else below,
        )

    def finish(h, c):
        e = h * COLS + c
        for side, slab in ((0, 0), (1, 2)):
            edge_send[e, side, 0] = (acc_k[c * 3 + slab] * SCALE).astype(bf16)
            edge_send[e, side, 1] = acc_v[c * 3 + slab].astype(bf16)
        own_acc[e, 0] = acc_k[c * 3 + 1] * SCALE
        own_acc[e, 1] = acc_v[c * 3 + 1]

        @pl.when(has_high)
        def _():
            edge_copy(e, True).start()

        @pl.when(has_low)
        def _():
            edge_copy(e, False).start()

    def settle(n):
        h, c = n // COLS, column_at(n % COLS)
        e = h * COLS + c

        @pl.when(has_low)
        def _():
            edge_copy(e, True).wait_recv()

        @pl.when(has_high)
        def _():
            edge_copy(e, False).wait_recv()

        for a in range(2):
            own_send[e, a] = (
                own_acc[e, a] + edge_recv[e, 0, a].astype(f32) + edge_recv[e, 1, a].astype(f32)
            ).astype(bf16)
        product = own_send[e, 0].astype(f32) * kbuf[h, c, 1].astype(f32)
        gain_tab[h, 1:2, :] += jnp.sum(product, axis=0, keepdims=True)
        for r in range(2):
            rows = pl.ds(r * TILE, TILE)
            t = r * COLS + c
            send_back(2, own_send.at[e, 0, rows], dk_recv.at[g * HPD + h], t)
            send_back(3, own_send.at[e, 1, rows], vgrad_out.at[:, columns(g * HPD + h)], t)

    def start_column(h, k):
        await_halo(h, k)
        for slab in range(3):
            keys = slice(slab * CH, (slab + 1) * CH)
            kt_buf[k, :, keys] = kbuf[h, k, slab].T
            vt_buf[k, :, keys] = vbuf[h, k, slab].T
            acc_k[k * 3 + slab] = jnp.zeros((CH, HS), f32)
            acc_v[k * 3 + slab] = jnp.zeros((CH, HS), f32)

    gain_tab[...] = jnp.zeros_like(gain_tab)
    forward(0)

    def rest(h, carry):
        send_k(h)
        send_v(h)
        send_q(h)
        send_g(h)
        return carry

    lax.fori_loop(1, HPD, rest, 0)

    def step(s, carry):
        h, k = s // COLS, s % COLS
        c = column_at(k)

        @pl.when(k == 0)
        def _():
            start_column(h, c)

            @pl.when(h < HPD - 1)
            def _():
                forward(h + 1)

            wait_for(qbuf.at[h], in_recv.at[2, h])
            wait_for(gbuf.at[h], in_recv.at[3, h])

        @pl.when(k < COLS - 1)
        def _():
            start_column(h, column_at(k + 1))

        attend(h, c)

        @pl.when(k > 0)
        def _():
            finish(h, column_at(k - 1))

        @pl.when(k == COLS - 1)
        def _():
            finish(h, c)

        @pl.when(s >= LAG)
        def _():
            settle(s - LAG)

        return carry

    lax.fori_loop(0, HPD * COLS, step, 0)

    def last(e, carry):
        settle(e)
        return carry

    lax.fori_loop(HPD * COLS - LAG, HPD * COLS, last, 0)

    for h in range(HPD):
        for row, gain in ((0, q_gain), (1, k_gain)):
            gain_tab[h, row : row + 1, :] = gain_tab[h, row : row + 1, :] / gain[:, columns(g * HPD + h)]

    def give(j, carry):
        dst = gain_recv.at[seq * NB + slab_here]
        me = gain_target_is_me(j)

        @pl.when(me)
        def _():
            pltpu.make_async_copy(gain_tab, dst, gain_sem.at[1]).start()

        @pl.when(jnp.logical_not(me))
        def _():
            pltpu.make_async_remote_copy(
                src_ref=gain_tab,
                dst_ref=dst,
                send_sem=gain_sem.at[0],
                recv_sem=gain_sem.at[1],
                device_id=gain_target(j),
            ).start()

        return carry

    lax.fori_loop(0, 2 * NB, give, 0)

    wait_for(dq_recv, back_recv.at[1])
    norm_back(q_tokens, q_gain, dq_recv, k_tokens, TILE)
    written = pltpu.make_async_copy(k_tokens, qgrad_out, token_sem.at[0])
    written.start()

    wait_for(gain_recv, gain_sem.at[1])
    start = 24 * ((b % 2) * NH + tile)
    lane = lax.broadcasted_iota(jnp.int32, (HS, HS), 1)
    source = lax.broadcasted_iota(jnp.int32, (HS, HS), 0)
    sums = jnp.zeros((8, HS), f32)
    for h in range(HPD):
        pick = ((source + h * HS == lane + start) & (lane < 24)).astype(f32)
        part = gain_recv[0, h]
        for i in range(1, 2 * NB):
            part = part + gain_recv[i, h]
        sums = sums + jnp.dot(
            part, pick, precision=lax.Precision.HIGHEST, preferred_element_type=f32
        )
    gain_out[...] = sums
    wait_for(att_out, back_recv.at[0])
    wait_for(dk_recv, back_recv.at[2])
    wait_for(vgrad_out, back_recv.at[3])
    written.wait()

    wait_for(gain_recv.at[0 : 2 * NB - 1], gain_sem.at[0])

    @pl.when(jnp.logical_not(gain_self))
    def _():
        wait_for(gain_recv.at[0], gain_sem.at[0])

    for which in range(4):
        wait_for(dq_recv, in_send.at[which])
        wait_for(dq_recv, back_send.at[which])

    @pl.when(lists_local)
    def _():
        list_copy().wait_send()

    def drain_edges(e, carry):
        for which in range(2):

            @pl.when(has_high)
            def _():
                halo_copy(e // COLS, e % COLS, which, True).wait_send()

            @pl.when(has_low)
            def _():
                halo_copy(e // COLS, e % COLS, which, False).wait_send()

        @pl.when(has_high)
        def _():
            edge_copy(e, True).wait_send()

        @pl.when(has_low)
        def _():
            edge_copy(e, False).wait_send()

        return carry

    lax.fori_loop(0, HPD * COLS, drain_edges, 0)


def closing(
    att_in, dv_in, q_in, k_in, dk_in, k_gain, gain_in,
    att_out, dv_out, q_out, k_out, q_gain_out, k_gain_out,
):
    att_out[...] = att_in[...]
    dv_out[...] = dv_in[...]
    q_out[...] = q_in[...]

    @pl.when(pl.program_id(0) == 0)
    def _():
        q_gain_out[...] = gain_in[0:1, 0:WIDTH]
        k_gain_out[...] = gain_in[1:2, 0:WIDTH]

    norm_back(k_in, k_gain, dk_in, k_out, BLOCK)


def shards(
    query_input, key_input, value_input, output_grad, query_gain, key_gain, tile_lists, tile_counts
):
    vmem = pl.BlockSpec(memory_space=pltpu.VMEM)
    anywhere = pl.BlockSpec(memory_space=pl.ANY)
    token = jax.ShapeDtypeStruct((TILE, F), bf16)
    heads = jax.ShapeDtypeStruct((HEADS, TILE, HS), bf16)
    n = HPD * COLS
    attention, query_grad, dk, value_grad, gains = pl.pallas_call(
        kernel,
        name="tiles",
        out_shape=(token, token, heads, token, jax.ShapeDtypeStruct((8, HS), f32)),
        in_specs=[anywhere] * 4 + [vmem] * 4,
        out_specs=(anywhere,) * 4 + (vmem,),
        scratch_shapes=[
            pltpu.VMEM((TILE, F), bf16),
            pltpu.VMEM((TILE, F), bf16),
            pltpu.SemaphoreType.DMA((2,)),
            pltpu.VMEM((HEADS, TILE, HS), bf16),
            pltpu.VMEM((HEADS, TILE, HS), bf16),
            pltpu.VMEM((HPD, COLS, CH, HS), bf16),
            pltpu.VMEM((HPD, COLS, CH, HS), bf16),
            pltpu.VMEM((HPD, COLS, 3, CH, HS), bf16),
            pltpu.VMEM((HPD, COLS, 3, CH, HS), bf16),
            pltpu.VMEM((COLS, HS, 3 * CH), bf16),
            pltpu.VMEM((COLS, HS, 3 * CH), bf16),
            pltpu.VMEM((3, 3, CH, CH), f32),
            pltpu.VMEM((3, 3 * CH, CH), bf16),
            pltpu.VMEM((3 * CH, CH), bf16),
            pltpu.VMEM((12, CH, HS), f32),
            pltpu.VMEM((12, CH, HS), f32),
            pltpu.VMEM((n, 2, CH, HS), f32),
            pltpu.VMEM((n, 2, 2, CH, HS), bf16),
            pltpu.VMEM((n, 2, 2, CH, HS), bf16),
            pltpu.VMEM((n, 2, CH, HS), bf16),
            pltpu.VMEM((HPD, COLS, CH, HS), bf16),
            pltpu.VMEM((HPD, COLS, CH, HS), bf16),
            pltpu.VMEM((HEADS, TILE, HS), bf16),
            pltpu.VMEM((HS, HS), f32),
            pltpu.VMEM((HS, HS), f32),
            pltpu.VMEM((8, HS), f32),
            pltpu.VMEM((12 * COLS, 2, CH), f32),
            pltpu.SemaphoreType.DMA((2,)),
            pltpu.VMEM((HPD, 8, HS), f32),
            pltpu.VMEM((2 * NB, HPD, 8, HS), f32),
            pltpu.SemaphoreType.DMA((2,)),
            pltpu.SemaphoreType.DMA((4,)),
            pltpu.SemaphoreType.DMA((4, HPD)),
            pltpu.SemaphoreType.DMA((n, 2, 2)),
            pltpu.SemaphoreType.DMA((n, 2, 2)),
            pltpu.SemaphoreType.DMA((n, 2)),
            pltpu.SemaphoreType.DMA((n, 2)),
            pltpu.SemaphoreType.DMA((4,)),
            pltpu.SemaphoreType.DMA((4,)),
        ],
        compiler_params=pltpu.CompilerParams(
            collective_id=0, has_side_effects=True, vmem_limit_bytes=62 * 1024 * 1024
        ),
    )(
        query_input[0],
        key_input[0],
        value_input[0],
        output_grad[0],
        query_gain[None],
        key_gain[None],
        tile_lists.transpose(2, 0, 1),
        tile_counts,
    )
    rows = pl.BlockSpec((BLOCK, F), lambda i: (i, 0))
    by_head = pl.BlockSpec((HEADS, BLOCK, HS), lambda i: (0, i, 0))
    whole = pl.BlockSpec((1, F), lambda i: (0, 0))
    few = pl.BlockSpec((1, WIDTH), lambda i: (0, 0))
    narrow = jax.ShapeDtypeStruct((1, WIDTH), f32)
    attention, value_grad, query_grad, key_grad, query_gains, key_gains = pl.pallas_call(
        closing,
        name="closing",
        grid=(TILE // BLOCK,),
        out_shape=(token, token, token, token, narrow, narrow),
        in_specs=[rows, rows, rows, rows, by_head, whole]
        + [pl.BlockSpec((8, HS), lambda i: (0, 0))],
        out_specs=(rows, rows, rows, rows, few, few),
        compiler_params=pltpu.CompilerParams(vmem_limit_bytes=62 * 1024 * 1024),
    )(
        attention,
        value_grad,
        query_grad,
        key_input[0],
        dk,
        key_gain[None],
        gains,
    )
    return (
        attention[None],
        query_grad[None],
        key_grad[None],
        value_grad[None],
        query_gains[0],
        key_gains[0],
    )


def solution(mesh):
    tokens = P("dp", ("blk", "head"), None)
    features = P(("dp", "blk", "head"))
    return jax.shard_map(
        shards,
        mesh=mesh,
        in_specs=(tokens, tokens, tokens, tokens, P(), P(), P("dp", None, None), P("dp", None)),
        out_specs=(tokens, tokens, tokens, tokens, features, features),
        check_vma=False,
    )
```

```python
import functools

import jax
import jax.numpy as jnp
from jax import lax
from jax.experimental import pallas as pl
from jax.experimental.pallas import tpu as pltpu
from jax.sharding import PartitionSpec as P

HS = 128
TILE = 192
KMAX = 12
HEADS = 24
HPD = 3
COLS = 4
NB = 8
NH = 8
F = HEADS * HS
CH = 2 * TILE
ROWS = 16
BLOCK = 64
WIDTH = 24
LAG = 5
EPSILON = 1e-06
SCALE = HS**-0.5
SCALE2 = SCALE * 1.4426950408889634
FAR = -1e30
NOWHERE = -1000.0
f32 = jnp.float32
bf16 = jnp.bfloat16


def nn(a, b):
    return lax.dot_general(a, b, (((1,), (0,)), ((), ())), preferred_element_type=f32)


def nt(a, b):
    return lax.dot_general(a, b, (((1,), (1,)), ((), ())), preferred_element_type=f32)


def group_of(slab, device):
    low = device % 2
    return device - low + (low + slab // 4) % 2


def owner(seq, slab):
    pair, part = slab % 4 // 2, slab % 2
    x = pair * (2 + seq) + (1 - pair) * (1 - seq)
    return {"dp": (part + pair) % 2, "blk": slab // 4 * 4 + x}


def unit(core, blk):
    x = blk % 4
    pair = x // 2
    seq = pair * (x - 2) + (1 - pair) * (1 - x)
    return seq, blk // 4 * 4 + 2 * pair + (core + pair) % 2


def wait_for(ref, sem):
    pltpu.make_async_copy(ref, ref, sem).wait()


def norm_back(x_in, gain, d_in, grad_out, count):
    def block(i, carry):
        rows = pl.ds(pl.multiple_of(i * ROWS, ROWS), ROWS)
        squares = jnp.zeros((ROWS, HS), f32)
        total = jnp.zeros((ROWS, HS), f32)
        for h in range(HEADS):
            lanes = slice(h * HS, (h + 1) * HS)
            x = x_in[rows, lanes].astype(f32)
            squares = squares + x * x
            total = total + d_in[h, rows, :].astype(f32) * gain[:, lanes] * x
        mean = jnp.sum(squares, axis=1, keepdims=True) * (1.0 / F)
        factor = lax.rsqrt(mean + EPSILON)
        inner = jnp.sum(total, axis=1, keepdims=True) * factor * (1.0 / F)
        factor = jnp.broadcast_to(factor, (ROWS, HS))
        inner = jnp.broadcast_to(inner, (ROWS, HS)) * factor
        for h in range(HEADS):
            lanes = slice(h * HS, (h + 1) * HS)
            x = x_in[rows, lanes].astype(f32)
            scaled = d_in[h, rows, :].astype(f32) * gain[:, lanes]
            grad_out[rows, lanes] = (factor * (scaled - x * inner)).astype(bf16)
        return carry

    lax.fori_loop(0, count // ROWS, block, 0)


def kernel(
    q_in,
    k_in,
    v_in,
    g_in,
    q_gain,
    k_gain,
    lists,
    counts,
    att_out,
    qgrad_out,
    dk_recv,
    vgrad_out,
    gain_out,
    q_tokens,
    k_tokens,
    token_sem,
    q_stage,
    k_stage,
    qbuf,
    gbuf,
    kbuf,
    vbuf,
    kt_buf,
    vt_buf,
    s_buf,
    p_buf,
    ds_buf,
    acc_k,
    acc_v,
    own_acc,
    edge_send,
    edge_recv,
    own_send,
    o_send,
    dq_send,
    dq_recv,
    slots,
    named,
    named_here,
    bias,
    list_sem,
    gain_tab,
    gain_recv,
    gain_sem,
    in_send,
    in_recv,
    halo_send,
    halo_recv,
    edge_ssem,
    edge_rsem,
    back_send,
    back_recv,
):
    d = lax.axis_index("dp")
    b = lax.axis_index("blk")
    tile = lax.axis_index("head")
    seq, slab_here = unit(d, b)
    g = group_of(b, tile)
    has_low = slab_here > 0
    has_high = slab_here < NB - 1
    below = {**owner(seq, slab_here - 1), "head": group_of(slab_here - 1, g)}
    above = {**owner(seq, slab_here + 1), "head": group_of(slab_here + 1, g)}
    work = owner(d, b)
    lists_local = seq == d
    other_core = {"dp": 1 - d}
    turned = g // 2 % 2

    def column_at(k):
        return k + turned * (COLS - 1 - 2 * k)

    my_row = tile // COLS
    my_col = tile % COLS
    gain_group = d * 4 + b // 2
    gain_self = gain_group == g
    my_rows = pl.ds(pl.multiple_of(my_row * TILE, TILE), TILE)

    barrier = pltpu.get_barrier_semaphore()

    def greet(i, carry):
        pl.semaphore_signal(barrier, inc=1, device_id={**work, "head": i})
        pl.semaphore_signal(barrier, inc=1, device_id={"dp": seq, "blk": slab_here, "head": i})
        return carry

    lax.fori_loop(0, NH, greet, 0)
    pl.semaphore_signal(barrier, inc=1, device_id=other_core)

    def gain_target(j):
        return {"dp": g // 4, "blk": 2 * (g % 4) + j // NH, "head": j % NH}

    def gain_target_is_me(j):
        return (g // 4 == d) & (2 * (g % 4) + j // NH == b) & (j % NH == tile)

    def greet_gain(j, carry):
        @pl.when(jnp.logical_not(gain_target_is_me(j)))
        def _():
            pl.semaphore_signal(barrier, inc=1, device_id=gain_target(j))

        @pl.when(jnp.logical_not((j // NB == seq) & (j % NB == slab_here) & gain_self))
        def _():
            pl.semaphore_signal(
                barrier,
                inc=1,
                device_id={**owner(j // NB, j % NB), "head": group_of(j % NB, gain_group)},
            )

        return carry

    lax.fori_loop(0, 2 * NB, greet_gain, 0)

    @pl.when(has_low)
    def _():
        pl.semaphore_signal(barrier, inc=1, device_id=below)

    @pl.when(has_high)
    def _():
        pl.semaphore_signal(barrier, inc=1, device_id=above)

    def clear_side(slab, side):
        zeros = jnp.zeros((CH, HS), bf16)

        def one(e, carry):
            h, c = e // COLS, e % COLS
            kbuf[h, c, slab] = zeros
            vbuf[h, c, slab] = zeros
            edge_recv[e, side, 0] = zeros
            edge_recv[e, side, 1] = zeros
            return carry

        lax.fori_loop(0, HPD * COLS, one, 0)

    @pl.when(jnp.logical_not(has_low))
    def _():
        clear_side(0, 0)

    @pl.when(jnp.logical_not(has_high))
    def _():
        clear_side(2, 1)

    for which, (src, dst) in enumerate(((k_in, k_tokens), (q_in, q_tokens))):
        pltpu.make_async_copy(src, dst, token_sem.at[which]).start()

    def normalize(x_in, gain, stage):
        def block(i, carry):
            rows = pl.ds(pl.multiple_of(i * ROWS, ROWS), ROWS)
            total = jnp.zeros((ROWS, HS), f32)
            for h in range(HEADS):
                x = x_in[rows, h * HS : (h + 1) * HS].astype(f32)
                total = total + x * x
            mean = jnp.sum(total, axis=1, keepdims=True) * (1.0 / F)
            factor = jnp.broadcast_to(lax.rsqrt(mean + EPSILON), (ROWS, HS))
            for h in range(HEADS):
                x = x_in[rows, h * HS : (h + 1) * HS].astype(f32)
                stage[h, rows, :] = (x * factor * gain[:, h * HS : (h + 1) * HS]).astype(bf16)
            return carry

        lax.fori_loop(0, TILE // ROWS, block, 0)

    def send_in(h, which, src_of, dst):
        def one(i, carry):
            to = (tile + i) % NH
            pltpu.make_async_remote_copy(
                src_ref=src_of(group_of(b, to) * HPD + h),
                dst_ref=dst,
                send_sem=in_send.at[which],
                recv_sem=in_recv.at[which, h],
                device_id={**work, "head": to},
            ).start()
            return carry

        lax.fori_loop(0, NH, one, 0)

    def columns(h):
        return pl.ds(pl.multiple_of(h * HS, HS), HS)

    def send_k(h):
        send_in(h, 0, lambda n: k_stage.at[n], kbuf.at[h, my_col, 1, my_rows])

    def send_v(h):
        send_in(h, 1, lambda n: v_in.at[:, columns(n)], vbuf.at[h, my_col, 1, my_rows])

    def send_q(h):
        send_in(h, 2, lambda n: q_stage.at[n], qbuf.at[h, my_col, my_rows])

    def send_g(h):
        send_in(h, 3, lambda n: g_in.at[:, columns(n)], gbuf.at[h, my_col, my_rows])

    tiles = NB * 8
    slot = lax.broadcasted_iota(jnp.int32, (KMAX, tiles), 0)
    slots[...] = jnp.full((HS, HS), NOWHERE, f32)
    slots[0:KMAX, 0:tiles] = jnp.where(slot < counts[...], lists[:, 0, :], NOWHERE).astype(f32)
    named[...] = slots[...].T

    def list_copy():
        slab = unit(1 - d, b)[1]
        return pltpu.make_async_remote_copy(
            src_ref=named.at[pl.ds(pl.multiple_of(slab * 8, 8), 8)],
            dst_ref=named_here,
            send_sem=list_sem.at[0],
            recv_sem=list_sem.at[1],
            device_id=other_core,
        )

    def build_bias():
        @pl.when(lists_local)
        def _():
            named_here[...] = named[pl.ds(pl.multiple_of(slab_here * 8, 8), 8), :]

        @pl.when(jnp.logical_not(lists_local))
        def _():
            list_copy().wait_recv()

        found = named_here[...] - ((slab_here - 1) * 8).astype(f32)
        first_row = lax.broadcasted_iota(jnp.int32, (1, CH), 1) < TILE
        for near in range(24):
            hit = jnp.max(jnp.where(found == near, 1.0, 0.0), axis=1, keepdims=True)
            away = jnp.broadcast_to(jnp.where(hit > 0.5, 0.0, FAR), (8, CH))
            slab, row, col = near // 8, near // COLS % 2, near % COLS
            for c in range(COLS):
                bias[c * 12 + col * 3 + slab, row : row + 1, :] = jnp.where(
                    first_row, away[c : c + 1], away[COLS + c : COLS + c + 1]
                )

    wait_for(k_tokens, token_sem.at[0])
    normalize(k_tokens, k_gain, k_stage)
    pl.semaphore_wait(
        barrier,
        2 * NH
        + 1
        + 4 * NB
        - 2 * gain_self.astype(jnp.int32)
        + has_low.astype(jnp.int32)
        + has_high.astype(jnp.int32),
    )
    @pl.when(lists_local)
    def _():
        list_copy().start()

    send_v(0)
    send_k(0)
    send_g(0)
    wait_for(q_tokens, token_sem.at[1])
    normalize(q_tokens, q_gain, q_stage)
    send_q(0)
    build_bias()

    def halo_copy(h, c, which, up):
        buf = (kbuf, vbuf)[which]
        side = 0 if up else 1
        return pltpu.make_async_remote_copy(
            src_ref=buf.at[h, c, 1],
            dst_ref=buf.at[h, c, 0 if up else 2],
            send_sem=halo_send.at[h * COLS + c, which, side],
            recv_sem=halo_recv.at[h * COLS + c, which, side],
            device_id=above if up else below,
        )

    def forward(h):
        wait_for(kbuf.at[h, :, 1], in_recv.at[0, h])
        wait_for(vbuf.at[h, :, 1], in_recv.at[1, h])

        def one(k, carry):
            c = column_at(k)
            for which in range(2):

                @pl.when(has_high)
                def _():
                    halo_copy(h, c, which, True).start()

                @pl.when(has_low)
                def _():
                    halo_copy(h, c, which, False).start()

            return carry

        lax.fori_loop(0, COLS, one, 0)

    def await_halo(h, c):
        for which in range(2):

            @pl.when(has_low)
            def _():
                halo_copy(h, c, which, True).wait_recv()

            @pl.when(has_high)
            def _():
                halo_copy(h, c, which, False).wait_recv()

    def send_back(which, src, dst, t):
        pltpu.make_async_remote_copy(
            src_ref=src,
            dst_ref=dst,
            send_sem=back_send.at[which],
            recv_sem=back_recv.at[which],
            device_id={"dp": seq, "blk": slab_here, "head": t},
        ).start()

    def attend(h, c):
        low = jnp.maximum(c - 1, 0)
        high = jnp.minimum(c + 2, COLS)
        q = qbuf[h, c]

        def first(k, top):
            for slab in range(3):
                s = nt(kbuf[h, k, slab], q)
                s_buf[k - low, slab] = s
                away = bias[c * 12 + k * 3 + slab]
                top = jnp.maximum(top, jnp.max(s[:TILE], axis=0, keepdims=True) + away[0:1])
                top = jnp.maximum(top, jnp.max(s[TILE:], axis=0, keepdims=True) + away[1:2])
            return top

        top = lax.fori_loop(low, high, first, jnp.full((1, CH), 2 * FAR, f32)) * SCALE2

        def second(k, carry):
            total, out = carry
            for slab in range(3):
                away = bias[c * 12 + k * 3 + slab]
                s = s_buf[k - low, slab]
                e0 = jnp.exp2(s[:TILE] * SCALE2 - (top - away[0:1]))
                e1 = jnp.exp2(s[TILE:] * SCALE2 - (top - away[1:2]))
                total = total + jnp.sum(e0, axis=0, keepdims=True)
                total = total + jnp.sum(e1, axis=0, keepdims=True)
                p_buf[k - low, slab * CH : slab * CH + TILE] = e0.astype(bf16)
                p_buf[k - low, slab * CH + TILE : (slab + 1) * CH] = e1.astype(bf16)
            return total, out + nn(vt_buf[k], p_buf[k - low])

        total, out = lax.fori_loop(
            low, high, second, (jnp.zeros((1, CH), f32), jnp.zeros((HS, CH), f32))
        )
        inverse = 1.0 / total
        out = out * inverse
        o_send[h, c] = out.T.astype(bf16)
        grad = gbuf[h, c].astype(f32).T
        delta = jnp.sum(out * grad, axis=0, keepdims=True) * inverse
        grad = grad * inverse
        grad_t = grad.astype(bf16)
        grad_s = grad.T.astype(bf16)

        def third(k, dq):
            for slab in range(3):
                e = p_buf[k - low, slab * CH : (slab + 1) * CH]
                dp = nn(vbuf[h, k, slab], grad_t)
                ds = (e.astype(f32) * (dp - delta)).astype(bf16)
                ds_buf[slab * CH : (slab + 1) * CH] = ds
                acc_v[k * 3 + slab] += nn(e, grad_s)
                acc_k[k * 3 + slab] += nn(ds, q)
            return dq + nn(kt_buf[k], ds_buf[...])

        dq = lax.fori_loop(low, high, third, jnp.zeros((HS, CH), f32))
        dq = (dq * SCALE).T.astype(bf16)
        dq_send[h, c] = dq
        gain_tab[h, 0:1, :] += jnp.sum(dq.astype(f32) * q.astype(f32), axis=0, keepdims=True)
        for r in range(2):
            rows = pl.ds(r * TILE, TILE)
            t = r * COLS + c
            send_back(0, o_send.at[h, c, rows], att_out.at[:, columns(g * HPD + h)], t)
            send_back(1, dq_send.at[h, c, rows], dq_recv.at[g * HPD + h], t)

    def edge_copy(e, up):
        return pltpu.make_async_remote_copy(
            src_ref=edge_send.at[e, 1 if up else 0],
            dst_ref=edge_recv.at[e, 0 if up else 1],
            send_sem=edge_ssem.at[e, 1 if up else 0],
            recv_sem=edge_rsem.at[e, 0 if up else 1],
            device_id=above if up else below,
        )

    def finish(h, c):
        e = h * COLS + c
        for side, slab in ((0, 0), (1, 2)):
            edge_send[e, side, 0] = (acc_k[c * 3 + slab] * SCALE).astype(bf16)
            edge_send[e, side, 1] = acc_v[c * 3 + slab].astype(bf16)
        own_acc[e, 0] = acc_k[c * 3 + 1] * SCALE
        own_acc[e, 1] = acc_v[c * 3 + 1]

        @pl.when(has_high)
        def _():
            edge_copy(e, True).start()

        @pl.when(has_low)
        def _():
            edge_copy(e, False).start()

    def settle(n):
        h, c = n // COLS, column_at(n % COLS)
        e = h * COLS + c

        @pl.when(has_low)
        def _():
            edge_copy(e, True).wait_recv()

        @pl.when(has_high)
        def _():
            edge_copy(e, False).wait_recv()

        for a in range(2):
            own_send[e, a] = (
                own_acc[e, a] + edge_recv[e, 0, a].astype(f32) + edge_recv[e, 1, a].astype(f32)
            ).astype(bf16)
        product = own_send[e, 0].astype(f32) * kbuf[h, c, 1].astype(f32)
        gain_tab[h, 1:2, :] += jnp.sum(product, axis=0, keepdims=True)
        for r in range(2):
            rows = pl.ds(r * TILE, TILE)
            t = r * COLS + c
            send_back(2, own_send.at[e, 0, rows], dk_recv.at[g * HPD + h], t)
            send_back(3, own_send.at[e, 1, rows], vgrad_out.at[:, columns(g * HPD + h)], t)

    def start_column(h, k):
        await_halo(h, k)
        for slab in range(3):
            keys = slice(slab * CH, (slab + 1) * CH)
            kt_buf[k, :, keys] = kbuf[h, k, slab].T
            vt_buf[k, :, keys] = vbuf[h, k, slab].T
            acc_k[k * 3 + slab] = jnp.zeros((CH, HS), f32)
            acc_v[k * 3 + slab] = jnp.zeros((CH, HS), f32)

    gain_tab[...] = jnp.zeros_like(gain_tab)
    forward(0)

    def rest(h, carry):
        send_k(h)
        send_v(h)
        send_q(h)
        send_g(h)
        return carry

    lax.fori_loop(1, HPD, rest, 0)

    def step(s, carry):
        h, k = s // COLS, s % COLS
        c = column_at(k)

        @pl.when(k == 0)
        def _():
            start_column(h, c)
            wait_for(qbuf.at[h], in_recv.at[2, h])
            wait_for(gbuf.at[h], in_recv.at[3, h])

        @pl.when(k < COLS - 1)
        def _():
            start_column(h, column_at(k + 1))

        @pl.when((k == 1) & (h < HPD - 1))
        def _():
            forward(h + 1)

        attend(h, c)

        @pl.when(k > 0)
        def _():
            finish(h, column_at(k - 1))

        @pl.when(k == COLS - 1)
        def _():
            finish(h, c)

        @pl.when((s >= LAG) & (s < HPD * COLS - 1))
        def _():
            settle(s - LAG)

        @pl.when(s >= HPD * COLS - 2)
        def _():
            settle(s - LAG + 1)

        return carry

    lax.fori_loop(0, HPD * COLS, step, 0)

    def last(e, carry):
        settle(e)
        return carry

    lax.fori_loop(HPD * COLS - LAG + 1, HPD * COLS, last, 0)

    for h in range(HPD):
        for row, gain in ((0, q_gain), (1, k_gain)):
            gain_tab[h, row : row + 1, :] = gain_tab[h, row : row + 1, :] / gain[:, columns(g * HPD + h)]

    def give(j, carry):
        dst = gain_recv.at[seq * NB + slab_here]
        me = gain_target_is_me(j)

        @pl.when(me)
        def _():
            pltpu.make_async_copy(gain_tab, dst, gain_sem.at[1]).start()

        @pl.when(jnp.logical_not(me))
        def _():
            pltpu.make_async_remote_copy(
                src_ref=gain_tab,
                dst_ref=dst,
                send_sem=gain_sem.at[0],
                recv_sem=gain_sem.at[1],
                device_id=gain_target(j),
            ).start()

        return carry

    lax.fori_loop(0, 2 * NB, give, 0)

    wait_for(dq_recv, back_recv.at[1])
    norm_back(q_tokens, q_gain, dq_recv, k_tokens, TILE)
    written = pltpu.make_async_copy(k_tokens, qgrad_out, token_sem.at[0])
    written.start()

    wait_for(gain_recv, gain_sem.at[1])
    start = 24 * ((b % 2) * NH + tile)
    lane = lax.broadcasted_iota(jnp.int32, (HS, HS), 1)
    source = lax.broadcasted_iota(jnp.int32, (HS, HS), 0)
    sums = jnp.zeros((8, HS), f32)
    for h in range(HPD):
        pick = ((source + h * HS == lane + start) & (lane < 24)).astype(f32)
        part = gain_recv[0, h]
        for i in range(1, 2 * NB):
            part = part + gain_recv[i, h]
        sums = sums + jnp.dot(
            part, pick, precision=lax.Precision.HIGHEST, preferred_element_type=f32
        )
    gain_out[...] = sums
    wait_for(att_out, back_recv.at[0])
    wait_for(dk_recv, back_recv.at[2])
    wait_for(vgrad_out, back_recv.at[3])
    written.wait()

    wait_for(gain_recv.at[0 : 2 * NB - 1], gain_sem.at[0])

    @pl.when(jnp.logical_not(gain_self))
    def _():
        wait_for(gain_recv.at[0], gain_sem.at[0])

    for which in range(4):
        wait_for(dq_recv, in_send.at[which])
        wait_for(dq_recv, back_send.at[which])

    @pl.when(lists_local)
    def _():
        list_copy().wait_send()

    def drain_edges(e, carry):
        for which in range(2):

            @pl.when(has_high)
            def _():
                halo_copy(e // COLS, e % COLS, which, True).wait_send()

            @pl.when(has_low)
            def _():
                halo_copy(e // COLS, e % COLS, which, False).wait_send()

        @pl.when(has_high)
        def _():
            edge_copy(e, True).wait_send()

        @pl.when(has_low)
        def _():
            edge_copy(e, False).wait_send()

        return carry

    lax.fori_loop(0, HPD * COLS, drain_edges, 0)


def closing(
    att_in, dv_in, q_in, k_in, dk_in, k_gain, gain_in,
    att_out, dv_out, q_out, k_out, q_gain_out, k_gain_out,
):
    att_out[...] = att_in[...]
    dv_out[...] = dv_in[...]
    q_out[...] = q_in[...]

    @pl.when(pl.program_id(0) == 0)
    def _():
        q_gain_out[...] = gain_in[0:1, 0:WIDTH]
        k_gain_out[...] = gain_in[1:2, 0:WIDTH]

    norm_back(k_in, k_gain, dk_in, k_out, BLOCK)


def shards(
    query_input, key_input, value_input, output_grad, query_gain, key_gain, tile_lists, tile_counts
):
    vmem = pl.BlockSpec(memory_space=pltpu.VMEM)
    anywhere = pl.BlockSpec(memory_space=pl.ANY)
    token = jax.ShapeDtypeStruct((TILE, F), bf16)
    heads = jax.ShapeDtypeStruct((HEADS, TILE, HS), bf16)
    n = HPD * COLS
    attention, query_grad, dk, value_grad, gains = pl.pallas_call(
        kernel,
        name="tiles",
        out_shape=(token, token, heads, token, jax.ShapeDtypeStruct((8, HS), f32)),
        in_specs=[anywhere] * 4 + [vmem] * 4,
        out_specs=(anywhere,) * 4 + (vmem,),
        scratch_shapes=[
            pltpu.VMEM((TILE, F), bf16),
            pltpu.VMEM((TILE, F), bf16),
            pltpu.SemaphoreType.DMA((2,)),
            pltpu.VMEM((HEADS, TILE, HS), bf16),
            pltpu.VMEM((HEADS, TILE, HS), bf16),
            pltpu.VMEM((HPD, COLS, CH, HS), bf16),
            pltpu.VMEM((HPD, COLS, CH, HS), bf16),
            pltpu.VMEM((HPD, COLS, 3, CH, HS), bf16),
            pltpu.VMEM((HPD, COLS, 3, CH, HS), bf16),
            pltpu.VMEM((COLS, HS, 3 * CH), bf16),
            pltpu.VMEM((COLS, HS, 3 * CH), bf16),
            pltpu.VMEM((3, 3, CH, CH), f32),
            pltpu.VMEM((3, 3 * CH, CH), bf16),
            pltpu.VMEM((3 * CH, CH), bf16),
            pltpu.VMEM((12, CH, HS), f32),
            pltpu.VMEM((12, CH, HS), f32),
            pltpu.VMEM((n, 2, CH, HS), f32),
            pltpu.VMEM((n, 2, 2, CH, HS), bf16),
            pltpu.VMEM((n, 2, 2, CH, HS), bf16),
            pltpu.VMEM((n, 2, CH, HS), bf16),
            pltpu.VMEM((HPD, COLS, CH, HS), bf16),
            pltpu.VMEM((HPD, COLS, CH, HS), bf16),
            pltpu.VMEM((HEADS, TILE, HS), bf16),
            pltpu.VMEM((HS, HS), f32),
            pltpu.VMEM((HS, HS), f32),
            pltpu.VMEM((8, HS), f32),
            pltpu.VMEM((12 * COLS, 2, CH), f32),
            pltpu.SemaphoreType.DMA((2,)),
            pltpu.VMEM((HPD, 8, HS), f32),
            pltpu.VMEM((2 * NB, HPD, 8, HS), f32),
            pltpu.SemaphoreType.DMA((2,)),
            pltpu.SemaphoreType.DMA((4,)),
            pltpu.SemaphoreType.DMA((4, HPD)),
            pltpu.SemaphoreType.DMA((n, 2, 2)),
            pltpu.SemaphoreType.DMA((n, 2, 2)),
            pltpu.SemaphoreType.DMA((n, 2)),
            pltpu.SemaphoreType.DMA((n, 2)),
            pltpu.SemaphoreType.DMA((4,)),
            pltpu.SemaphoreType.DMA((4,)),
        ],
        compiler_params=pltpu.CompilerParams(
            collective_id=0, has_side_effects=True, vmem_limit_bytes=62 * 1024 * 1024
        ),
    )(
        query_input[0],
        key_input[0],
        value_input[0],
        output_grad[0],
        query_gain[None],
        key_gain[None],
        tile_lists.transpose(2, 0, 1),
        tile_counts,
    )
    rows = pl.BlockSpec((BLOCK, F), lambda i: (i, 0))
    by_head = pl.BlockSpec((HEADS, BLOCK, HS), lambda i: (0, i, 0))
    whole = pl.BlockSpec((1, F), lambda i: (0, 0))
    few = pl.BlockSpec((1, WIDTH), lambda i: (0, 0))
    narrow = jax.ShapeDtypeStruct((1, WIDTH), f32)
    attention, value_grad, query_grad, key_grad, query_gains, key_gains = pl.pallas_call(
        closing,
        name="closing",
        grid=(TILE // BLOCK,),
        out_shape=(token, token, token, token, narrow, narrow),
        in_specs=[rows, rows, rows, rows, by_head, whole]
        + [pl.BlockSpec((8, HS), lambda i: (0, 0))],
        out_specs=(rows, rows, rows, rows, few, few),
        compiler_params=pltpu.CompilerParams(vmem_limit_bytes=62 * 1024 * 1024),
    )(
        attention,
        value_grad,
        query_grad,
        key_input[0],
        dk,
        key_gain[None],
        gains,
    )
    return (
        attention[None],
        query_grad[None],
        key_grad[None],
        value_grad[None],
        query_gains[0],
        key_gains[0],
    )


def solution(mesh):
    tokens = P("dp", ("blk", "head"), None)
    features = P(("dp", "blk", "head"))
    return jax.shard_map(
        shards,
        mesh=mesh,
        in_specs=(tokens, tokens, tokens, tokens, P(), P(), P("dp", None, None), P("dp", None)),
        out_specs=(tokens, tokens, tokens, tokens, features, features),
        check_vma=False,
    )
```
